32 devices in a mesh: dp: 8 (over z, y), section: 4 (over x, core).
Axes of the slice: x: 2, y: 2, z: 4, core: 2. Of those that a mesh axis runs over, the one named last changes fastest.
Arguments:
- encoder_in: bfloat16 [16, 512, 768], P('dp'), may hold values from -6 to 6
- decoder_in: bfloat16 [16, 96, 768], P('dp'), may hold values from -6 to 6
- lengths: int32 [16, 3], P('dp'), may hold values from 64 to 384, as said below
- query_map: int32 [16, 3], P('dp'), may hold values from 0 to 2, as said below
- attn_query: bfloat16 [3, 768, 768], P(None, 'section'), may hold values from -0.02734375 to 0.02734375
- attn_keyval: bfloat16 [6, 768, 768], P(None, 'section'), may hold values from -0.21875 to 0.21875
- attn_output: bfloat16 [3, 768, 768], P(None, 'section'), may hold values from -0.875 to 0.875
- feed_in: bfloat16 [2, 3072, 768], P(None, 'section'), may hold values from -0.21875 to 0.21875
- feed_out: bfloat16 [2, 3072, 768], P(None, 'section'), may hold values from -0.109375 to 0.109375
- norm_gains: float32 [5, 768], replicated, may hold values from 0.5 to 1.5
- position_bias: float32 [2, 32, 12], replicated, may hold values from -4 to 4
- cotangent: bfloat16 [16, 96, 768], P('dp'), may hold values from -6 to 6
Outputs:
- decoder_out: bfloat16 [16, 96, 768], P('dp', 'section')
- encoder_in_grad: bfloat16 [16, 512, 768], P('dp', 'section')
- decoder_in_grad: bfloat16 [16, 96, 768], P('dp', 'section')
- attn_query_grad: float32 [3, 768, 768], P(None, 'section')
- attn_keyval_grad: float32 [6, 768, 768], P(None, 'section')
- attn_output_grad: float32 [3, 768, 768], P(None, 'section')
- feed_in_grad: float32 [2, 3072, 768], P(None, 'section')
- feed_out_grad: float32 [2, 3072, 768], P(None, 'section')
- norm_gains_grad: float32 [5, 768], replicated
- position_bias_grad: float32 [2, 32, 12], replicated
The draws below stay inside these ranges and needn't reach their ends.
Inputs may be any that keep to these rules, and one draw needn't show every extreme that they name: In every buffer the 3 lengths sum to 512, and the longest is exactly 384. `query_map`: in every buffer each of the 3 queries owns at least one passage.
All inputs are finite; a program needn't handle non-finite values.
Results may differ from the reference program's by a relative error of at most 0.028.
Values may be sent and summed in bfloat16 or wider, within the bound.
No kernel may reach another device: no remote copies, remote signals or barrier semaphores. Data moves between devices by JAX's collectives and lax.ppermute only.
A program may use at most 640 MiB of HBM per device.

```python
import jax
import jax.numpy as jnp
from jax import lax

D = 768
HEADS = 12
HD = 64
FF = 3072
NB = 32
BUF = 512
PASS = 3
MINLEN = 64
MAXLEN = 384
QPB = 3
TGT = 32
DEC = 96
BUFFERS = 16


def draw_lengths(key, part):
    key = jax.random.fold_in(key, 11)
    share_key, order_key = jax.random.split(key)
    shares = jax.random.randint(share_key, (BUFFERS, PASS - 1), 1, 64)
    spare = BUF - MAXLEN - (PASS - 1) * MINLEN
    portion = shares * spare // jnp.sum(shares, axis=1, keepdims=True)
    remainder = spare - jnp.sum(portion, axis=1, keepdims=True)
    portion = portion.at[:, 0:1].add(remainder)
    ordered = jnp.concatenate([jnp.full((BUFFERS, 1), MAXLEN, jnp.int32), MINLEN + portion.astype(jnp.int32)], axis=1)
    scores = jax.random.randint(order_key, (BUFFERS, PASS), 0, 1 << 20) * PASS + jnp.arange(PASS)[None, :]
    order = jnp.argsort(scores, axis=1)
    return jnp.take_along_axis(ordered, order, axis=1).astype(jnp.int32)


def draw_query_map(key, part):
    key = jax.random.fold_in(key, 23)
    pick_key, order_key = jax.random.split(key)
    extra = jax.random.randint(pick_key, (BUFFERS, PASS), 0, QPB)
    places = jnp.arange(PASS)[None, :]
    base = jnp.where(places < QPB, places, extra)
    scores = jax.random.randint(order_key, (BUFFERS, PASS), 0, 1 << 20) * PASS + places
    order = jnp.argsort(scores, axis=1)
    return jnp.take_along_axis(base, order, axis=1).astype(jnp.int32)


def steps_of(key, dims, cuts, least, high):
    loudness = 1.0
    for position, shards_of in cuts:
        steps = jax.random.uniform(jax.random.fold_in(jax.random.fold_in(key, 6), position), (shards_of,), jnp.float32, least / len(cuts), high / len(cuts))
        loudness = loudness * jnp.repeat(jnp.exp(steps), dims[position] // shards_of).reshape((-1,) + (1,) * (len(dims) - 1 - position))
    return loudness


def bell_draw(own_key, extent, deviation, bound, pieces=(), kind=jnp.bfloat16):
    level = steps_of(own_key, extent, pieces, -0.22, 0.18) if pieces else 1.0
    drawn = jax.random.normal(own_key, extent, jnp.float32) * deviation * level
    return jnp.minimum(jnp.maximum(drawn, -bound), bound).astype(kind)


def setup_inputs(seed: int = 0) -> dict:
    arg_keys = jax.random.split(jax.random.key(seed), 13)
    return {
        "encoder_in": bell_draw(arg_keys[0], (BUFFERS, BUF, D), 1.0, 6.0, ((0, 8),)),
        "decoder_in": bell_draw(arg_keys[1], (BUFFERS, DEC, D), 1.0, 6.0, ((0, 8),)),
        "lengths": draw_lengths(jax.random.fold_in(arg_keys[12], 71), 0),
        "query_map": draw_query_map(jax.random.fold_in(arg_keys[12], 71), 0),
        "attn_query": bell_draw(arg_keys[4], (3, D, D), (D * HD) ** -0.5, 0.02734375, ((1, 4),)),
        "attn_keyval": bell_draw(arg_keys[5], (6, D, D), D ** -0.5, 0.21875, ((1, 4),)),
        "attn_output": bell_draw(arg_keys[6], (3, D, D), (D // 16) ** -0.5, 0.875, ((1, 4),)),
        "feed_in": bell_draw(arg_keys[7], (2, FF, D), D ** -0.5, 0.21875, ((1, 4),)),
        "feed_out": bell_draw(arg_keys[8], (2, FF, D), FF ** -0.5, 0.109375, ((1, 4),)),
        "norm_gains": jnp.clip(1.0 + 0.1 * jax.random.normal(arg_keys[9], (5, D), jnp.float32), 0.5, 1.5),
        "position_bias": bell_draw(arg_keys[10], (2, NB, HEADS), 1.0, 4.0, (), jnp.float32),
        "cotangent": bell_draw(arg_keys[11], (BUFFERS, DEC, D), 1.0, 6.0, ((0, 8),)),
    }


epsilon = 1e-06
masked_score = -1e+30
highest = lax.Precision.HIGHEST
enc_edges = (12, 16, 23, 32, 46, 64, 91)
dec_edges = (19, 21, 24, 27, 31)

@jax.custom_vjp
def low(v):
    return lax.optimization_barrier(v.astype(jnp.bfloat16)).astype(jnp.float32)

@jax.custom_vjp
def low_back(v):
    return v

def low_keep(v):
    return (low(v), None)

def low_pass(kept, grad):
    return (grad,)

def back_keep(v):
    return (v, None)

def back_low(kept, grad):
    return (low(grad),)
low.defvjp(low_keep, low_pass)
low_back.defvjp(back_keep, back_low)

def product(left, right):
    return jnp.dot(left, right, precision=highest)

def rms_norm(rows, gain):
    return rows * lax.rsqrt(lax.optimization_barrier(jnp.mean(rows * rows, axis=-1, keepdims=True)) + epsilon) * gain

def encoder_bucket(offset):
    distance = jnp.abs(offset)
    bucket = jnp.minimum(distance, 8)
    for boundary in enc_edges:
        bucket = bucket + (distance >= boundary).astype(jnp.int32)
    return bucket + 16 * (offset > 0).astype(jnp.int32)

def decoder_bucket(offset):
    distance = jnp.maximum(-offset, 0)
    bucket = jnp.minimum(distance, 16)
    for boundary in dec_edges:
        bucket = bucket + (distance >= boundary).astype(jnp.int32)
    return bucket

def attention(queries, keys_rows, values_rows, allowed, bias):
    rows = queries.shape[0]
    columns = keys_rows.shape[0]
    heads_q = queries.reshape(rows, HEADS, HD)
    heads_k = keys_rows.reshape(columns, HEADS, HD)
    heads_v = values_rows.reshape(columns, HEADS, HD)
    scores = jnp.einsum('rhd,chd->hrc', heads_q, heads_k, precision=highest) + bias
    scores = low_back(jnp.where(allowed[None], scores, masked_score))
    weights = low(jax.nn.softmax(scores, axis=-1))
    context = jnp.einsum('hrc,chd->rhd', weights, heads_v, precision=highest)
    return context.reshape(rows, D)

def feed(rows, gain, weight_in, weight_out):
    normed = low(rms_norm(rows, gain))
    hidden = low_back(product(normed, weight_in.T))
    active = low(jax.nn.gelu(hidden, approximate=True))
    return product(active, weight_out)

def one_buffer(params, encoder_rows, decoder_rows, lengths_row, owners_row):
    query_w, keyval_w, output_w, feed_w_in, feed_w_out, gains, tables = params
    positions = jnp.arange(BUF, dtype=jnp.int32)
    ends = jnp.cumsum(lengths_row)
    segment = lax.optimization_barrier(jnp.sum((positions[:, None] >= ends[None, :]).astype(jnp.int32), axis=1))
    owner = owners_row[segment]
    offset = positions[None, :] - positions[:, None]
    enc_bias = jnp.transpose(tables[0][encoder_bucket(offset)], (2, 0, 1))
    normed = low(rms_norm(encoder_rows, gains[0]))
    queries = low(low_back(product(normed, query_w[0])))
    keys_rows = low(low_back(product(normed, keyval_w[0])))
    values_rows = low(low_back(product(normed, keyval_w[1])))
    context = low(low_back(attention(queries, keys_rows, values_rows, segment[:, None] == segment[None, :], enc_bias)))
    first_out = low(low_back(encoder_rows + product(context, output_w[0])))
    encoded = low(low_back(first_out + feed(first_out, gains[1], feed_w_in[0], feed_w_out[0])))
    dec_pos = jnp.arange(QPB * TGT, dtype=jnp.int32)
    asked = dec_pos // TGT
    dec_offset = dec_pos[None, :] - dec_pos[:, None]
    dec_bias = jnp.transpose(tables[1][decoder_bucket(dec_offset)], (2, 0, 1))
    causal = (asked[:, None] == asked[None, :]) & (dec_offset <= 0)
    normed = low(rms_norm(decoder_rows, gains[2]))
    queries = low(low_back(product(normed, query_w[1])))
    keys_rows = low(low_back(product(normed, keyval_w[2])))
    values_rows = low(low_back(product(normed, keyval_w[3])))
    context = low(low_back(attention(queries, keys_rows, values_rows, causal, dec_bias)))
    middle = decoder_rows + low_back(product(context, output_w[1]))
    normed = low(rms_norm(middle, gains[3]))
    queries = low(low_back(product(normed, query_w[2])))
    keys_rows = low(low_back(product(encoded, keyval_w[4])))
    values_rows = low(low_back(product(encoded, keyval_w[5])))
    context = low(low_back(attention(queries, keys_rows, values_rows, asked[:, None] == owner[None, :], 0.0)))
    second_out = low(low_back(middle + product(context, output_w[2])))
    return second_out + feed(second_out, gains[4], feed_w_in[1], feed_w_out[1])

def reference(encoder_in, decoder_in, lengths, query_map, attn_query, attn_keyval, attn_output, feed_in, feed_out, norm_gains, position_bias, cotangent):
    params = (attn_query.astype(jnp.float32), attn_keyval.astype(jnp.float32), attn_output.astype(jnp.float32), feed_in.astype(jnp.float32), feed_out.astype(jnp.float32), norm_gains.astype(jnp.float32), position_bias.astype(jnp.float32))

    def whole(weights, encoder_rows, decoder_rows):

        def step(carry, items):
            return (carry, one_buffer(weights, *items))
        unused, outputs = lax.scan(jax.checkpoint(step), jnp.zeros((), jnp.float32), (encoder_rows, decoder_rows, lengths, query_map))
        return outputs
    outputs, backward = jax.vjp(whole, params, encoder_in.astype(jnp.float32), decoder_in.astype(jnp.float32))
    grads, encoder_grad, decoder_grad = backward(cotangent.astype(jnp.float32))
    return (outputs.astype(jnp.bfloat16), encoder_grad.astype(jnp.bfloat16), decoder_grad.astype(jnp.bfloat16), grads[0], grads[1], grads[2], grads[3], grads[4], grads[5], grads[6])
```

```python
import functools

import jax
import jax.numpy as jnp
import numpy as np
from jax import lax
from jax.experimental import pallas as pl
from jax.experimental.pallas import tpu as pltpu
from jax.sharding import PartitionSpec as P

D = 768
HEADS = 12
HD = 64
PAIRS = HEADS // 2
NB = 32
BUF = 512
BIG = 384
SMALL = 64
REST = BUF - BIG
QPB = 3
TGT = 32
DEC = QPB * TGT
WIDE = 512
epsilon = 1e-06
masked_score = -1e30
enc_edges = (12, 16, 23, 32, 46, 64, 91)
dec_edges = (19, 21, 24, 27, 31)
bf16 = jnp.bfloat16
f32 = jnp.float32


def dot_nn(a, b):
    return lax.dot_general(a, b, (((1,), (0,)), ((), ())), preferred_element_type=f32)


def dot_nt(a, b):
    return lax.dot_general(a, b, (((1,), (1,)), ((), ())), preferred_element_type=f32)


def dot_tn(a, b):
    return lax.dot_general(a, b, (((0,), (0,)), ((), ())), preferred_element_type=f32)


def encoder_bucket(offset):
    distance = np.abs(offset)
    bucket = np.minimum(distance, 8)
    for boundary in enc_edges:
        bucket = bucket + (distance >= boundary)
    return bucket + 16 * (offset > 0)


def decoder_bucket(offset):
    distance = np.maximum(-offset, 0)
    bucket = np.minimum(distance, 16)
    for boundary in dec_edges:
        bucket = bucket + (distance >= boundary)
    return bucket


def enc_offsets():
    lane = np.arange(WIDE)
    shifted = np.where(lane < BIG, lane, lane - WIDE)
    return 128 * np.arange(3)[:, None] - shifted[None, :]


def diagonal_offsets(rows, width):
    return rows - 1 - np.arange(width)


def dec_offsets():
    lane = np.arange(256)
    return -np.where(lane < 128, lane, lane - 256)


def one_hot(bucket):
    return (bucket[..., None] == np.arange(NB)).astype(np.float32)


def spread_table(table, bucket):
    hot = jnp.asarray(one_hot(bucket))
    return jnp.sum(hot[None] * jnp.transpose(table).reshape((HEADS,) + (1,) * bucket.ndim + (NB,)), axis=-1)


def lane_half(value, which):
    lane = lax.broadcasted_iota(jnp.int32, value.shape, 1)
    keep = (lane < HD) if which == 0 else (lane >= HD)
    return jnp.where(keep, value, jnp.zeros_like(value))


def softmax_t(scores):
    peak = jnp.max(scores, axis=0, keepdims=True)
    raised = jnp.exp(scores - peak)
    total = jnp.sum(raised, axis=0, keepdims=True)
    return (raised * (1.0 / total)).astype(bf16)


def toeplitz(row, rows):
    spread = jnp.broadcast_to(row, (rows, row.shape[-1]))
    return pltpu.roll(spread, 0, 1, stride=1, stride_axis=0)


def diagonals(value, width):
    rows = value.shape[0]
    row = lax.broadcasted_iota(jnp.int32, (rows, rows), 0)
    col = lax.broadcasted_iota(jnp.int32, (rows, rows), 1)
    flipped = dot_nn((row + col == rows - 1).astype(bf16), value)
    padded = jnp.concatenate([flipped, jnp.zeros((rows, width - value.shape[1]), f32)], axis=1)
    return jnp.sum(pltpu.roll(padded, 0, 1, stride=1, stride_axis=0), axis=0, keepdims=True)


def rest_mask():
    row = lax.broadcasted_iota(jnp.int32, (REST, REST), 0) // SMALL
    col = lax.broadcasted_iota(jnp.int32, (REST, REST), 1) // SMALL
    return row == col


def enc_forward_kernel(q_ref, k_ref, v_ref, bias_ref, c_ref, big_ref, rest_ref):
    values_t = v_ref[...].T
    keys = k_ref[...]
    allowed = rest_mask()
    heads = []
    for hh in range(2):
        queries = lane_half(q_ref[...], hh)
        bias = [toeplitz(bias_ref[hh, b : b + 1, :], 128)[:, :BIG] for b in range(3)]
        scores = dot_nt(keys[:BIG], queries[:BIG]) + jnp.concatenate(bias, axis=0)
        weights = softmax_t(scores)
        big_ref[hh] = weights
        head_v = values_t[hh * HD : (hh + 1) * HD]
        context = dot_nn(head_v[:, :BIG], weights)
        rest = dot_nt(keys[BIG:], queries[BIG:]) + bias[0][:, :REST]
        rest = softmax_t(jnp.where(allowed, rest, masked_score))
        rest_ref[hh] = rest
        heads.append(jnp.concatenate([context, dot_nn(head_v[:, BIG:], rest)], axis=1))
    c_ref[...] = jnp.concatenate(heads, axis=0).T.astype(bf16)


def score_grad(weights, grad_weights, row_sum):
    return (weights.astype(f32) * (grad_weights - row_sum)).astype(bf16)


def enc_backward_kernel(
    q_ref, k_ref, v_ref, c_ref, g_ref, big_ref, rest_ref,
    dq_ref, dk_ref, dv_ref, diag_ref, rdiag_ref,
):
    grads = g_ref[...]
    keys_t = k_ref[...].T
    product_t = (grads.astype(f32) * c_ref[...].astype(f32)).T
    dq_t = []
    dk_big = dv_big = dk_rest = dv_rest = 0.0
    for hh in range(2):
        row_sum = jnp.sum(product_t[hh * HD : (hh + 1) * HD], axis=0, keepdims=True)
        queries = lane_half(q_ref[...], hh)
        values = lane_half(v_ref[...], hh)
        grads_h = lane_half(grads, hh)
        head_k = keys_t[hh * HD : (hh + 1) * HD]
        weights = big_ref[hh]
        ds = score_grad(weights, dot_nt(values[:BIG], grads[:BIG]), row_sum[:, :BIG])
        dv_big = dv_big + dot_nn(weights, grads_h[:BIG])
        dk_big = dk_big + dot_nn(ds, queries[:BIG])
        diag_ref[hh] = jnp.concatenate(
            [diagonals(ds[128 * b : 128 * (b + 1)], WIDE) for b in range(3)], axis=0
        )
        dq_head = dot_nn(head_k[:, :BIG], ds)
        weights = rest_ref[hh]
        ds = score_grad(weights, dot_nt(values[BIG:], grads[BIG:]), row_sum[:, BIG:])
        dv_rest = dv_rest + dot_nn(weights, grads_h[BIG:])
        dk_rest = dk_rest + dot_nn(ds, queries[BIG:])
        rdiag_ref[hh] = diagonals(ds, 2 * REST)
        dq_t.append(jnp.concatenate([dq_head, dot_nn(head_k[:, BIG:], ds)], axis=1))
    dq_ref[...] = jnp.concatenate(dq_t, axis=0).T.astype(bf16)
    dk_ref[...] = jnp.concatenate([dk_big, dk_rest], axis=0).astype(bf16)
    dv_ref[...] = jnp.concatenate([dv_big, dv_rest], axis=0).astype(bf16)


def pair_spec(rows):
    return pl.BlockSpec((rows, 2 * HD), lambda p: (0, p))


def head_spec(*dims):
    return pl.BlockSpec((2,) + dims, lambda p: (p,) + (0,) * len(dims))


def call(kernel, outs, in_specs, out_specs, flops, *args):
    return pl.pallas_call(
        kernel,
        grid=(PAIRS,),
        out_shape=outs,
        in_specs=in_specs,
        out_specs=out_specs,
        compiler_params=pltpu.CompilerParams(vmem_limit_bytes=40 << 20),
        cost_estimate=pl.CostEstimate(flops=flops, bytes_accessed=8 << 20, transcendentals=0),
    )(*args)


def shape(dims, dtype=bf16):
    return jax.ShapeDtypeStruct(dims, dtype)


def enc_attend(q, k, v, bias):
    return call(
        enc_forward_kernel,
        (shape((BUF, D)), shape((HEADS, BIG, BIG)), shape((HEADS, REST, REST))),
        [pair_spec(BUF)] * 3 + [head_spec(3, WIDE)],
        (pair_spec(BUF), head_spec(BIG, BIG), head_spec(REST, REST)),
        4_000_000_000,
        q, k, v, bias,
    )


def enc_attend_back(q, k, v, c, g, big, rest):
    return call(
        enc_backward_kernel,
        (
            shape((BUF, D)), shape((BUF, D)), shape((BUF, D)),
            shape((HEADS, 3, WIDE), f32), shape((HEADS, 1, 2 * REST), f32),
        ),
        [pair_spec(BUF)] * 5 + [head_spec(BIG, BIG), head_spec(REST, REST)],
        (pair_spec(BUF),) * 3 + (head_spec(3, WIDE), head_spec(1, 2 * REST)),
        9_000_000_000,
        q, k, v, c, g, big, rest,
    )


def small_forward_kernel(kind, *refs):
    if kind == "self":
        q_ref, k_ref, v_ref, bias_ref, c_ref, p_ref = refs
    else:
        q_ref, k_ref, v_ref, c_ref, p_ref = refs
    keys = k_ref[...]
    values_t = v_ref[...].T
    count = keys.shape[0]
    row = lax.broadcasted_iota(jnp.int32, (count, DEC), 0)
    col = lax.broadcasted_iota(jnp.int32, (count, DEC), 1)
    if kind == "self":
        allowed = (row // TGT == col // TGT) & (row <= col)
    else:
        allowed = jnp.where(row < BIG, 0, row // SMALL - (BIG // SMALL - 1)) == col // TGT
    heads = []
    for hh in range(2):
        scores = dot_nt(keys, lane_half(q_ref[...], hh))
        if kind == "self":
            scores = scores + toeplitz(bias_ref[hh], DEC)[:, :DEC]
        weights = softmax_t(jnp.where(allowed, scores, masked_score))
        p_ref[hh] = weights
        heads.append(dot_nn(values_t[hh * HD : (hh + 1) * HD], weights))
    c_ref[...] = jnp.concatenate(heads, axis=0).T.astype(bf16)


def small_backward_kernel(kind, *refs):
    if kind == "self":
        q_ref, k_ref, v_ref, c_ref, g_ref, p_ref, dq_ref, dk_ref, dv_ref, diag_ref = refs
    else:
        q_ref, k_ref, v_ref, c_ref, g_ref, p_ref, dq_ref, dk_ref, dv_ref = refs
    grads = g_ref[...]
    keys_t = k_ref[...].T
    product_t = (grads.astype(f32) * c_ref[...].astype(f32)).T
    dq_t = []
    dk = dv = 0.0
    for hh in range(2):
        row_sum = jnp.sum(product_t[hh * HD : (hh + 1) * HD], axis=0, keepdims=True)
        weights = p_ref[hh]
        ds = score_grad(weights, dot_nt(lane_half(v_ref[...], hh), grads), row_sum)
        dv = dv + dot_nn(weights, lane_half(grads, hh))
        dk = dk + dot_nn(ds, lane_half(q_ref[...], hh))
        if kind == "self":
            diag_ref[hh] = diagonals(ds, 256)
        dq_t.append(dot_nn(keys_t[hh * HD : (hh + 1) * HD], ds))
    dq_ref[...] = jnp.concatenate(dq_t, axis=0).T.astype(bf16)
    dk_ref[...] = dk.astype(bf16)
    dv_ref[...] = dv.astype(bf16)


def small_attend(kind, q, k, v, bias=None):
    count = k.shape[0]
    specs = [pair_spec(DEC), pair_spec(count), pair_spec(count)]
    args = (q, k, v)
    if kind == "self":
        specs, args = specs + [head_spec(1, 256)], args + (bias,)
    return call(
        functools.partial(small_forward_kernel, kind),
        (shape((DEC, D)), shape((HEADS, count, DEC))),
        specs,
        (pair_spec(DEC), head_spec(count, DEC)),
        2_000_000_000,
        *args,
    )


def small_attend_back(kind, q, k, v, c, g, weights):
    count = k.shape[0]
    outs = (shape((DEC, D)), shape((count, D)), shape((count, D)))
    out_specs = (pair_spec(DEC), pair_spec(count), pair_spec(count))
    if kind == "self":
        outs, out_specs = outs + (shape((HEADS, 1, 256), f32),), out_specs + (head_spec(1, 256),)
    return call(
        functools.partial(small_backward_kernel, kind),
        outs,
        [pair_spec(DEC), pair_spec(count), pair_spec(count), pair_spec(DEC), pair_spec(DEC), head_spec(count, DEC)],
        out_specs,
        3_000_000_000,
        q, k, v, c, g, weights,
    )


def norm_scale(rows):
    return lax.rsqrt(jnp.mean(rows * rows, axis=-1, keepdims=True) + epsilon)


def norm_rows(rows, gain):
    return (rows * norm_scale(rows) * gain).astype(bf16)


def norm_back(rows, gain, grad):
    scale = norm_scale(rows)
    unit = rows * scale
    weighted = grad * gain
    grad_rows = scale * (weighted - unit * jnp.mean(weighted * unit, axis=-1, keepdims=True))
    return grad_rows, jnp.sum(grad * unit, axis=0)


def gelu_both(u):
    root = np.float32(np.sqrt(2.0 / np.pi))
    cubic = np.float32(0.044715)
    bend = jnp.tanh(root * (u + cubic * u * u * u))
    value = 0.5 * u * (1.0 + bend)
    slope = 0.5 * (1.0 + bend) + 0.5 * u * (1.0 - bend * bend) * root * (1.0 + 3.0 * cubic * u * u)
    return value.astype(bf16), slope.astype(bf16)


def swap_section(value, bit):
    count = lax.axis_size("section")
    return lax.ppermute(value, "section", [(i, i ^ bit) for i in range(count)])


def swap_dp(value, bit):
    count = lax.axis_size("dp")
    return lax.ppermute(value, "dp", [(i, i ^ bit) for i in range(count)])


def add_low(a, b):
    return (a.astype(f32) + b.astype(f32)).astype(bf16)


def halves(value, bit):
    half = value.shape[0] // 2
    mine = (lax.axis_index("dp") // bit) % 2
    keep = lax.dynamic_slice_in_dim(value, mine * half, half, 0)
    send = lax.dynamic_slice_in_dim(value, (1 - mine) * half, half, 0)
    return keep, send


def rejoin(keep, other, bit):
    mine = (lax.axis_index("dp") // bit) % 2
    return jnp.where(mine == 0, jnp.concatenate([keep, other]), jnp.concatenate([other, keep]))


def sum_dp(value, order):
    count = lax.axis_size("dp")
    if count != 8:
        return lax.psum(value, "dp")
    for bit in order[:-1]:
        keep, send = halves(value, bit)
        value = add_low(keep, swap_dp(send, bit))
    value = add_low(value, swap_dp(value, order[-1]))
    for bit in order[:-1][::-1]:
        value = rejoin(value, swap_dp(value, bit), bit)
    return value


def core_sum(own, other):
    return add_low(own, swap_section(other.astype(bf16), 1))


def gather_mats(own, section_id):
    across = swap_section(own, 2)
    near = swap_section(own, 1)
    far = swap_section(across, 1)
    full = jnp.zeros((own.shape[0], 4 * own.shape[1], D), bf16)
    for piece, bit in ((own, 0), (near, 1), (across, 2), (far, 3)):
        full = lax.dynamic_update_slice_in_dim(full, piece, (section_id ^ bit) * own.shape[1], 1)
    return full


def shards(
    encoder_in, decoder_in, lengths, query_map, attn_query, attn_keyval, attn_output,
    feed_in, feed_out, norm_gains, position_bias, cotangent,
):
    section_id = lax.axis_index("section")
    across = section_id // 2
    core = section_id % 2
    quarter = attn_query.shape[1]
    half = 2 * quarter

    enc_w = gather_mats(jnp.concatenate([attn_query[0:1], attn_keyval[0:2], attn_output[0:1]]), section_id)
    self_w = gather_mats(jnp.concatenate([attn_query[1:2], attn_keyval[2:4], attn_output[1:2]]), section_id)
    cross_w = gather_mats(jnp.concatenate([attn_query[2:3], attn_keyval[4:6], attn_output[2:3]]), section_id)
    feed_in_o, feed_out_o = swap_section(feed_in, 1), swap_section(feed_out, 1)
    w_in = [jnp.concatenate([feed_in[i], feed_in_o[i]]) for i in range(2)]
    w_out = [jnp.concatenate([feed_out[i], feed_out_o[i]]) for i in range(2)]

    big = jnp.argmax(lengths[core]).astype(jnp.int32)
    start = big * SMALL
    owners = lax.dynamic_slice_in_dim(jnp.concatenate([query_map[core]] * 2), big, QPB, 0)

    def to_front(rows):
        return lax.dynamic_slice_in_dim(jnp.concatenate([rows, rows]), start, BUF, 0)

    def from_front(rows):
        return lax.dynamic_slice_in_dim(jnp.concatenate([rows, rows]), BUF - start, BUF, 0)

    def by_owner(rows):
        return jnp.concatenate(
            [lax.dynamic_slice_in_dim(rows, owners[i] * TGT, TGT, 0) for i in range(QPB)]
        )

    def from_owner(rows):
        whole = jnp.zeros((DEC, D), rows.dtype)
        for i in range(QPB):
            whole = lax.dynamic_update_slice_in_dim(whole, rows[i * TGT : (i + 1) * TGT], owners[i] * TGT, 0)
        return whole

    enc_rows = to_front(encoder_in[core]).astype(f32)
    dec_rows = by_owner(decoder_in[core]).astype(f32)
    cot = by_owner(cotangent[core])

    enc_table = spread_table(position_bias[0], encoder_bucket(enc_offsets()))
    dec_table = spread_table(position_bias[1], decoder_bucket(dec_offsets())[None])

    n1 = norm_rows(enc_rows, norm_gains[0])
    q1, k1, v1 = (dot_nn(n1, enc_w[i]).astype(bf16) for i in range(3))
    c1, p1_big, p1_rest = enc_attend(q1, k1, v1, enc_table)
    h1 = (enc_rows + dot_nn(c1, enc_w[3])).astype(bf16)
    h1_rows = h1.astype(f32)
    n2 = norm_rows(h1_rows, norm_gains[1])
    a1, slope1 = gelu_both(dot_nt(n2, w_in[0]))
    part = dot_nn(a1, w_out[0]).astype(bf16)
    e = (h1_rows + part.astype(f32) + swap_section(part, 2).astype(f32)).astype(bf16)

    n3 = norm_rows(dec_rows, norm_gains[2])
    q2, k2, v2 = (dot_nn(n3, self_w[i]).astype(bf16) for i in range(3))
    c2, p2 = small_attend("self", q2, k2, v2, dec_table)
    m = dec_rows + dot_nn(c2, self_w[3])
    n4 = norm_rows(m, norm_gains[3])
    q3 = dot_nn(n4, cross_w[0]).astype(bf16)
    k3 = dot_nn(e, cross_w[1]).astype(bf16)
    v3 = dot_nn(e, cross_w[2]).astype(bf16)
    c3, p3 = small_attend("cross", q3, k3, v3)
    g = (m + dot_nn(c3, cross_w[3])).astype(bf16)
    g_rows = g.astype(f32)
    n5 = norm_rows(g_rows, norm_gains[4])
    a2, slope2 = gelu_both(dot_nt(n5, w_in[1]))

    def feed_back(grad, a, slope, n, index):
        du = (slope.astype(f32) * dot_nt(grad, w_out[index])).astype(bf16)
        dn = dot_nn(du, w_in[index]).astype(bf16)
        dn = dn.astype(f32) + swap_section(dn, 2).astype(f32)
        dw_in = dot_tn(du, n)
        dw_out = dot_tn(a, grad)
        return dn, core_sum(dw_in[:D], dw_in[D:]), core_sum(dw_out[:D], dw_out[D:])

    dn5, unit_in2, unit_out2 = feed_back(cot, a2, slope2, n5, 1)
    unit_in2 = sum_dp(unit_in2, (1, 2, 4))
    unit_out2 = sum_dp(unit_out2, (2, 4, 1))
    part = dot_nn(a2, w_out[1]).astype(bf16)
    out_rows = g_rows + part.astype(f32) + swap_section(part, 2).astype(f32)
    dg_rows, gain4 = norm_back(g_rows, norm_gains[4], dn5)
    dg = (dg_rows + cot.astype(f32)).astype(bf16)

    def chip_cols(rows):
        return lax.dynamic_slice_in_dim(rows, across * half, half, 1)

    def unit_of(pairs):
        own, other = [], []
        for rows, grad in pairs:
            full = dot_tn(chip_cols(rows), grad).astype(bf16)
            own.append(lax.dynamic_slice_in_dim(full, core * quarter, quarter, 0))
            other.append(lax.dynamic_slice_in_dim(full, (1 - core) * quarter, quarter, 0))
        return core_sum(jnp.concatenate(own), jnp.concatenate(other))

    dc3 = dot_nt(dg, cross_w[3]).astype(bf16)
    dq3, dk3, dv3 = small_attend_back("cross", q3, k3, v3, c3, dc3, p3)
    de = (dot_nt(dk3, cross_w[1]) + dot_nt(dv3, cross_w[2])).astype(bf16)
    dm_rows, gain3 = norm_back(m, norm_gains[3], dot_nt(dq3, cross_w[0]))
    dm = dm_rows + dg.astype(f32)
    dm_low = dm.astype(bf16)
    unit_cross = sum_dp(unit_of([(n4, dq3), (e, dk3), (e, dv3), (c3, dg)]), (1, 2, 4))

    dn2, unit_in1, unit_out1 = feed_back(de, a1, slope1, n2, 0)
    unit_in1 = sum_dp(unit_in1, (1, 2, 4))
    unit_out1 = sum_dp(unit_out1, (2, 4, 1))
    dh1_rows, gain1 = norm_back(h1_rows, norm_gains[1], dn2)
    dh1 = (dh1_rows + de.astype(f32)).astype(bf16)

    dc2 = dot_nt(dm_low, self_w[3]).astype(bf16)
    dq2, dk2, dv2, diag2 = small_attend_back("self", q2, k2, v2, c2, dc2, p2)
    dn3 = dot_nt(dq2, self_w[0]) + dot_nt(dk2, self_w[1]) + dot_nt(dv2, self_w[2])
    dd_rows, gain2 = norm_back(dec_rows, norm_gains[2], dn3)
    dec_grad = dd_rows + dm
    unit_self = sum_dp(unit_of([(n3, dq2), (n3, dk2), (n3, dv2), (c2, dm_low)]), (1, 2, 4))

    dc1 = dot_nt(dh1, enc_w[3]).astype(bf16)
    dq1, dk1, dv1, diag1, rdiag1 = enc_attend_back(q1, k1, v1, c1, dc1, p1_big, p1_rest)
    unit_enc = sum_dp(unit_of([(n1, dq1), (n1, dk1), (n1, dv1), (c1, dh1)]), (1, 2, 4))
    dn1 = dot_nt(dq1, enc_w[0]) + dot_nt(dk1, enc_w[1]) + dot_nt(dv1, enc_w[2])
    de_rows, gain0 = norm_back(enc_rows, norm_gains[0], dn1)
    enc_grad = de_rows + dh1.astype(f32)

    hot_enc = jnp.asarray(
        np.concatenate(
            [one_hot(encoder_bucket(128 * b + diagonal_offsets(128, WIDE))) for b in range(3)]
            + [one_hot(encoder_bucket(diagonal_offsets(REST, 2 * REST)))]
        )
    )
    hot_dec = jnp.asarray(one_hot(decoder_bucket(diagonal_offsets(DEC, 256))))
    sums_enc = jnp.concatenate([diag1.reshape(HEADS, -1), rdiag1.reshape(HEADS, -1)], axis=1)
    exact = lax.Precision.HIGHEST
    table_enc = jnp.einsum("mb,hm->bh", hot_enc, sums_enc, precision=exact)
    table_dec = jnp.einsum("mb,hm->bh", hot_dec, diag2.reshape(HEADS, -1), precision=exact)
    gains = jnp.stack([gain0, gain1, gain2, gain3, gain4])
    tables = jnp.stack([table_enc, table_dec])
    counts = (across == 0).astype(f32)
    gains, tables = lax.psum((gains * counts, tables * counts), ("dp", "section"))

    def spread_rows(rows, count):
        low = rows.astype(bf16)
        mine = lax.dynamic_slice_in_dim(low, section_id * count, count, 0)
        theirs = lax.dynamic_slice_in_dim(low, (section_id ^ 1) * count, count, 0)
        theirs = swap_section(theirs, 1)
        return jnp.where(core == 0, jnp.stack([mine, theirs]), jnp.stack([theirs, mine]))

    dec_part = DEC // lax.axis_size("section")
    enc_part = BUF // lax.axis_size("section")
    decoder_out = spread_rows(from_owner(out_rows), dec_part)
    decoder_in_grad = spread_rows(from_owner(dec_grad), dec_part)
    encoder_in_grad = spread_rows(from_front(enc_grad.astype(bf16)), enc_part)

    u_enc, u_self, u_cross = (
        u.reshape(4, quarter, D).astype(f32) for u in (unit_enc, unit_self, unit_cross)
    )
    query_grad = jnp.stack([u_enc[0], u_self[0], u_cross[0]])
    keyval_grad = jnp.concatenate([u_enc[1:3], u_self[1:3], u_cross[1:3]])
    output_grad = jnp.stack([u_enc[3], u_self[3], u_cross[3]])
    feed_in_grad = jnp.stack([unit_in1, unit_in2]).astype(f32)
    feed_out_grad = jnp.stack([unit_out1, unit_out2]).astype(f32)
    return (
        decoder_out, encoder_in_grad, decoder_in_grad, query_grad, keyval_grad, output_grad,
        feed_in_grad, feed_out_grad, gains, tables,
    )


def solution(mesh):
    rows = P("dp", None, None)
    mats = P(None, "section", None)
    outs = P("dp", "section", None)
    return jax.shard_map(
        shards,
        mesh=mesh,
        in_specs=(rows, rows, P("dp", None), P("dp", None), mats, mats, mats, mats, mats, P(), P(), rows),
        out_specs=(outs, outs, outs, mats, mats, mats, mats, mats, P(), P()),
        check_vma=False,
    )
```

```python
import functools

import jax
import jax.numpy as jnp
import numpy as np
from jax import lax
from jax.experimental import pallas as pl
from jax.experimental.pallas import tpu as pltpu
from jax.sharding import PartitionSpec as P

D = 768
HEADS = 12
HD = 64
PAIRS = HEADS // 2
NB = 32
BUF = 512
BIG = 384
SMALL = 64
REST = BUF - BIG
QPB = 3
TGT = 32
DEC = QPB * TGT
WIDE = 512
epsilon = 1e-06
masked_score = -1e30
enc_edges = (12, 16, 23, 32, 46, 64, 91)
dec_edges = (19, 21, 24, 27, 31)
bf16 = jnp.bfloat16
f32 = jnp.float32


def dot_nn(a, b):
    return lax.dot_general(a, b, (((1,), (0,)), ((), ())), preferred_element_type=f32)


def dot_nt(a, b):
    return lax.dot_general(a, b, (((1,), (1,)), ((), ())), preferred_element_type=f32)


def dot_tn(a, b):
    return lax.dot_general(a, b, (((0,), (0,)), ((), ())), preferred_element_type=f32)


def encoder_bucket(offset):
    distance = np.abs(offset)
    bucket = np.minimum(distance, 8)
    for boundary in enc_edges:
        bucket = bucket + (distance >= boundary)
    return bucket + 16 * (offset > 0)


def decoder_bucket(offset):
    distance = np.maximum(-offset, 0)
    bucket = np.minimum(distance, 16)
    for boundary in dec_edges:
        bucket = bucket + (distance >= boundary)
    return bucket


def enc_offsets():
    lane = np.arange(WIDE)
    shifted = np.where(lane < BIG, lane, lane - WIDE)
    return 128 * np.arange(3)[:, None] - shifted[None, :]


def diagonal_offsets(rows, width):
    return rows - 1 - np.arange(width)


def dec_offsets():
    lane = np.arange(256)
    return -np.where(lane < 128, lane, lane - 256)


def one_hot(bucket):
    return (bucket[..., None] == np.arange(NB)).astype(np.float32)


def spread_table(table, bucket):
    hot = jnp.asarray(one_hot(bucket))
    return jnp.sum(hot[None] * jnp.transpose(table).reshape((HEADS,) + (1,) * bucket.ndim + (NB,)), axis=-1)


def norm_scale(rows):
    return lax.rsqrt(jnp.mean(rows * rows, axis=-1, keepdims=True) + epsilon)


def norm_rows(rows, gain):
    return (rows * norm_scale(rows) * gain).astype(bf16)


def norm_back(rows, gain, grad):
    scale = norm_scale(rows)
    unit = rows * scale
    weighted = grad * gain
    grad_rows = scale * (weighted - unit * jnp.mean(weighted * unit, axis=-1, keepdims=True))
    return grad_rows, jnp.sum(grad * unit, axis=0, keepdims=True)


def gelu_both(u):
    root = np.float32(np.sqrt(2.0 / np.pi))
    cubic = np.float32(0.044715)
    square = u * u
    bend = jnp.tanh(u * (root + root * cubic * square))
    half = 0.5 * (1.0 + bend)
    slope = half + 0.5 * u * (1.0 - bend * bend) * (root + 3.0 * root * cubic * square)
    return (u * half).astype(bf16), slope.astype(bf16)


CORE, ACROSS, START, OWNER, BASE, PIECE = 0, 1, 2, 3, 6, 10


def shape(dims, dtype=bf16):
    return jax.ShapeDtypeStruct(dims, dtype)


def whole(*dims):
    return pl.BlockSpec(dims, lambda *_: (0,) * len(dims))


def call(kernel, grid, scalars, ins, outs, scratch=(), flops=10**10, aliases=None):
    return pl.pallas_call(
        kernel,
        grid_spec=pltpu.PrefetchScalarGridSpec(
            num_scalar_prefetch=1,
            grid=grid,
            in_specs=[spec for _, spec in ins],
            out_specs=tuple(spec for _, spec in outs),
            scratch_shapes=scratch,
        ),
        out_shape=tuple(kind for kind, _ in outs),
        input_output_aliases=aliases or {},
        compiler_params=pltpu.CompilerParams(vmem_limit_bytes=60 << 20),
        cost_estimate=pl.CostEstimate(flops=flops, bytes_accessed=1 << 20, transcendentals=0),
    )(scalars, *[array for array, _ in ins])


def lane_half(value, which):
    lane = lax.broadcasted_iota(jnp.int32, value.shape, 1)
    keep = (lane < HD) if which == 0 else (lane >= HD)
    return jnp.where(keep, value, jnp.zeros_like(value))


def softmax_t(scores):
    peak = jnp.max(scores, axis=0, keepdims=True)
    raised = jnp.exp(scores - peak)
    total = jnp.sum(raised, axis=0, keepdims=True)
    return (raised * (1.0 / total)).astype(bf16)


def toeplitz(row, rows):
    spread = jnp.broadcast_to(row, (rows, row.shape[-1]))
    return pltpu.roll(spread, 0, 1, stride=1, stride_axis=0)


def diagonals(value, width):
    rows = value.shape[0]
    row = lax.broadcasted_iota(jnp.int32, (rows, rows), 0)
    col = lax.broadcasted_iota(jnp.int32, (rows, rows), 1)
    flipped = dot_nn((row + col == rows - 1).astype(bf16), value)
    padded = jnp.concatenate([flipped, jnp.zeros((rows, width - value.shape[1]), f32)], axis=1)
    return jnp.sum(pltpu.roll(padded, 0, 1, stride=1, stride_axis=0), axis=0, keepdims=True)


def rest_mask():
    row = lax.broadcasted_iota(jnp.int32, (REST, REST), 0) // SMALL
    col = lax.broadcasted_iota(jnp.int32, (REST, REST), 1) // SMALL
    return row == col


def score_grad(weights, grad_weights, row_sum):
    return (weights.astype(f32) * (grad_weights - row_sum)).astype(bf16)


def transposed(value):
    return value.astype(f32).T.astype(bf16) if value.dtype == bf16 and value.shape[0] % 128 else value.T


def take_near(at, own, near, which):
    return jnp.where(which, own[0], near[0])


def attend_pair(q, k, v, bias_ref, big_ref, rest_ref):
    values_t = v.T
    allowed = rest_mask()
    heads = []
    for hh in range(2):
        queries = lane_half(q, hh)
        bias = [toeplitz(bias_ref[hh, b : b + 1, :], 128)[:, :BIG] for b in range(3)]
        scores = dot_nt(k[:BIG], queries[:BIG]) + jnp.concatenate(bias, axis=0)
        weights = softmax_t(scores)
        big_ref[hh] = weights
        head_v = values_t[hh * HD : (hh + 1) * HD]
        context = dot_nn(head_v[:, :BIG], weights)
        rest = dot_nt(k[BIG:], queries[BIG:]) + bias[0][:, :REST]
        rest = softmax_t(jnp.where(allowed, rest, masked_score))
        rest_ref[hh] = rest
        heads.append(jnp.concatenate([context, dot_nn(head_v[:, BIG:], rest)], axis=1))
    return jnp.concatenate(heads, axis=0).T.astype(bf16)


def enc_attention(scalars, rows, gains, bias, own, near, got, got_near, chunk):
    opening = chunk == 0
    quarter = got.shape[1]

    def kernel(at, rows_ref, gain_ref, bias_ref, oq, okv, nq, nkv, gw, gnw, *refs):
        if opening:
            qkv_ref, c_ref, big_ref, rest_ref, w_ref, n1_ref, xr_ref, twice = refs
            @pl.when(pl.program_id(0) == 0)
            def _():
                twice[:BUF] = rows_ref[0]
                twice[BUF:] = rows_ref[0, :REST]
                rolled = twice[pl.ds(pl.multiple_of(at[START], SMALL), BUF)]
                xr_ref[...] = rolled
                n1_ref[...] = norm_rows(rolled.astype(f32), gain_ref[0:1])
        else:
            qkv_ref, c_ref, big_ref, rest_ref, w_ref = refs
            n1_ref = rows_ref
        parts = ((oq[0], okv[0], okv[1]), (nq[0], nkv[0], nkv[1]), (gw[0], gw[1], gw[2]), (gnw[0], gnw[1], gnw[2]))
        for k, mats in enumerate(parts):
            place = pl.ds(pl.multiple_of(at[BASE + k], quarter), quarter)
            w_ref[0, place] = jnp.concatenate(mats, axis=1)
        qkv = dot_nn(n1_ref[...], w_ref[0]).astype(bf16)
        qkv_ref[0] = qkv
        c_ref[...] = attend_pair(qkv[:, :128], qkv[:, 128:256], qkv[:, 256:], bias_ref, big_ref, rest_ref)

    first = 3 * chunk
    one = pl.BlockSpec((1, quarter, 128), lambda p, at: (0, 0, first + p))
    two = pl.BlockSpec((2, quarter, 128), lambda p, at: (0, 0, first + p))
    three = pl.BlockSpec((3, quarter, 128), lambda p, at: (0, 0, p))
    rows_spec = pl.BlockSpec((1, BUF, D), lambda p, at: (at[CORE], 0, 0)) if opening else whole(BUF, D)
    outs = [
        (shape((3, BUF, 384)), pl.BlockSpec((1, BUF, 384), lambda p, at: (p, 0, 0))),
        (shape((BUF, 384)), pl.BlockSpec((BUF, 128), lambda p, at: (0, p))),
        (shape((6, BIG, BIG)), pl.BlockSpec((2, BIG, BIG), lambda p, at: (p, 0, 0))),
        (shape((6, REST, REST)), pl.BlockSpec((2, REST, REST), lambda p, at: (p, 0, 0))),
        (shape((3, D, 384)), pl.BlockSpec((1, D, 384), lambda p, at: (p, 0, 0))),
    ]
    if opening:
        outs += [(shape((BUF, D)), whole(BUF, D))] * 2
    return call(
        kernel, (3,), scalars,
        [
            (rows, rows_spec), (gains, whole(5, D)),
            (bias, pl.BlockSpec((2, 3, WIDE), lambda p, at: (first + p, 0, 0))),
            (own[0], one), (own[1], two), (near[0], one), (near[1], two), (got, three), (got_near, three),
        ],
        outs, [pltpu.VMEM((BUF + REST, D), bf16)] if opening else (), 2 * 10**10,
    )


FTILE = 384


def feed_specs(index, count):
    own = pl.BlockSpec((1, FTILE, D), lambda i, at: (index, jnp.minimum(i, count - 1), 0))
    near = pl.BlockSpec((1, FTILE, D), lambda i, at: (index, jnp.maximum(i - count, 0), 0))
    return own, near


def enc_feed(scalars, xr, c_a, c_b, own_o, near_o, got, got_near, gains, feed_in, near_in, feed_out, near_out):
    quarter = got.shape[0]
    count = feed_in.shape[1] // FTILE

    def kernel(at, xr_ref, ca, cb, oo, no, go, gno, gain_ref, fi, ni, fo, nf, h1_ref, n2_ref, a_ref, s_ref, p_ref, wo_ref, total):
        step = pl.program_id(0)

        @pl.when(step == 0)
        def _():
            for k, piece in enumerate((oo[0], no[0], go[...], gno[...])):
                wo_ref[pl.ds(pl.multiple_of(at[BASE + k], quarter), quarter)] = piece
            context = jnp.concatenate([ca[...], cb[...]], axis=1)
            h1 = (xr_ref[...].astype(f32) + dot_nn(context, wo_ref[...])).astype(bf16)
            h1_ref[...] = h1
            n2_ref[...] = norm_rows(h1.astype(f32), gain_ref[1:2])
            total[...] = jnp.zeros_like(total)

        w_in = jnp.where(step < count, fi[0], ni[0])
        w_out = jnp.where(step < count, fo[0], nf[0])
        a, slope = gelu_both(dot_nt(n2_ref[...], w_in))
        a_ref[...] = a
        s_ref[...] = slope
        total[...] += dot_nn(a, w_out)

        @pl.when(step == 2 * count - 1)
        def _():
            p_ref[...] = total[...].astype(bf16)

    own, near = feed_specs(0, count)
    rows = whole(BUF, D)
    tile = pl.BlockSpec((BUF, FTILE), lambda i, at: (0, i))
    quarter_spec = pl.BlockSpec((1, quarter, D), lambda i, at: (0, 0, 0))
    return call(
        kernel, (2 * count,), scalars,
        [
            (xr, rows), (c_a, whole(BUF, 384)), (c_b, whole(BUF, 384)), (own_o, quarter_spec), (near_o, quarter_spec),
            (got, whole(quarter, D)), (got_near, whole(quarter, D)), (gains, whole(5, D)),
            (feed_in, own), (near_in, near), (feed_out, own), (near_out, near),
        ],
        [
            (shape((BUF, D)), rows), (shape((BUF, D)), rows), (shape((BUF, 2 * count * FTILE)), tile),
            (shape((BUF, 2 * count * FTILE)), tile), (shape((BUF, D)), rows), (shape((D, D)), whole(D, D)),
        ],
        [pltpu.VMEM((BUF, D), f32)], 2 * 10**10,
    )


def small_masks(kind, count):
    row = lax.broadcasted_iota(jnp.int32, (count, DEC), 0)
    col = lax.broadcasted_iota(jnp.int32, (count, DEC), 1)
    if kind == "self":
        return (row // TGT == col // TGT) & (row <= col)
    return jnp.where(row < BIG, 0, row // SMALL - (BIG // SMALL - 1)) == col // TGT


def small_attend(kind, q, k, v, p_ref, bias_ref=None):
    allowed = small_masks(kind, k.shape[0])
    contexts = []
    for pair in range(PAIRS):
        lanes = slice(128 * pair, 128 * pair + 128)
        values_t = transposed(v[:, lanes])
        for hh in range(2):
            scores = dot_nt(k[:, lanes], lane_half(q[:, lanes], hh))
            if bias_ref is not None:
                scores = scores + toeplitz(bias_ref[2 * pair + hh], DEC)[:, :DEC]
            weights = softmax_t(jnp.where(allowed, scores, masked_score))
            p_ref[2 * pair + hh] = weights
            contexts.append(dot_nn(values_t[hh * HD : (hh + 1) * HD], weights))
    return jnp.concatenate(contexts, axis=0).T.astype(bf16)


def small_attend_back(q, k, v, c, grads, p_ref, diag_ref=None):
    product_t = (grads.astype(f32) * c.astype(f32)).T
    dq_t, dk, dv = [], [], []
    for pair in range(PAIRS):
        lanes = slice(128 * pair, 128 * pair + 128)
        keys_t = transposed(k[:, lanes])
        dk_pair = dv_pair = 0.0
        for hh in range(2):
            head = 2 * pair + hh
            row_sum = jnp.sum(product_t[head * HD : (head + 1) * HD], axis=0, keepdims=True)
            weights = p_ref[head]
            ds = score_grad(weights, dot_nt(lane_half(v[:, lanes], hh), grads[:, lanes]), row_sum)
            dv_pair = dv_pair + dot_nn(weights, lane_half(grads[:, lanes], hh))
            dk_pair = dk_pair + dot_nn(ds, lane_half(q[:, lanes], hh))
            if diag_ref is not None:
                diag_ref[head] = diagonals(ds, 256)
            dq_t.append(dot_nn(keys_t[hh * HD : (hh + 1) * HD], ds))
        dk.append(dk_pair.astype(bf16))
        dv.append(dv_pair.astype(bf16))
    return jnp.concatenate(dq_t, axis=0).T.astype(bf16), jnp.concatenate(dk, axis=1), jnp.concatenate(dv, axis=1)


def by_owner(at, ref):
    return jnp.concatenate(
        [ref[0, pl.ds(pl.multiple_of(at[OWNER + i] * TGT, TGT), TGT)] for i in range(QPB)], axis=0
    )


def core_rows():
    return pl.BlockSpec((1, DEC, D), lambda i, at: (at[CORE], 0, 0))


ANYWHERE = pl.BlockSpec(memory_space=pl.ANY)


def weight_args(parts):
    return [(array, ANYWHERE) for array in parts]


def weight_copies(at, index, refs, w, sem):
    quarter = refs[0].shape[1]
    pieces, piece = refs[6].shape[0], refs[6].shape[2]
    copies = []

    def copy(source, target):
        copies.append(pltpu.make_async_copy(source, target, sem.at[len(copies)]))

    for k in range(2):
        place = pl.ds(pl.multiple_of(at[BASE + k], quarter), quarter)
        q, kv, o = refs[3 * k : 3 * k + 3]
        copy(q.at[index], w.at[0, place])
        copy(kv.at[pl.ds(2 * index, 2)], w.at[pl.ds(1, 2), place])
        copy(o.at[index], w.at[3, place])
    for k in range(2):
        for j in range(pieces):
            row = at[BASE + 2 + k] + at[PIECE + 4 * (index - 1) + j]
            copy(refs[6 + k].at[j], w.at[:, pl.ds(pl.multiple_of(row, piece), piece)])
    for one in copies:
        one.start()
    return copies


WEIGHT_SCRATCH = [pltpu.VMEM((4, D, D), bf16), pltpu.SemaphoreType.DMA((14,))]


def dec_self(scalars, decoder_in, gains, bias, self_w):
    def kernel(at, x_ref, gain_ref, bias_ref, *refs):
        xd_ref, n3_ref, q_ref, k_ref, v_ref, c_ref, p_ref, m_ref, n4_ref, w, sem = refs[8:]
        copies = weight_copies(at, 1, refs[:8], w, sem)
        xd = by_owner(at, x_ref)
        xd_ref[...] = xd
        n3 = norm_rows(xd.astype(f32), gain_ref[2:3])
        n3_ref[...] = n3
        for one in copies:
            one.wait()
        q, k, v = (dot_nn(n3, w[i]).astype(bf16) for i in range(3))
        q_ref[...], k_ref[...], v_ref[...] = q, k, v
        c = small_attend("self", q, k, v, p_ref, bias_ref)
        c_ref[...] = c
        m = xd.astype(f32) + dot_nn(c, w[3])
        m_ref[...] = m
        n4_ref[...] = norm_rows(m, gain_ref[3:4])

    rows = whole(DEC, D)
    low = (shape((DEC, D)), rows)
    return call(
        kernel, (1,), scalars,
        [(decoder_in, core_rows()), (gains, whole(5, D)), (bias, whole(HEADS, 1, 256))] + weight_args(self_w),
        [low] * 6 + [(shape((HEADS, DEC, DEC)), whole(HEADS, DEC, DEC)), (shape((DEC, D), f32), rows), low],
        WEIGHT_SCRATCH,
    )


def dec_cross(scalars, h1, part, other, m, n4, cross_w, gains, cotangent, feed_in, near_in, feed_out, near_out):
    hidden = feed_in.shape[1]

    def kernel(
        at, h1_ref, p0, p1, m_ref, n4_ref, gain_ref, cot_ref, fi, ni, fo, nf, *refs
    ):
        e_ref, q_ref, k_ref, v_ref, c_ref, p_ref, g_ref, n5_ref, cot_out, a_ref, du_ref, dn_ref, o_ref = refs[8:21]
        w, w_sem, w_in, w_out, sem = refs[21:]
        first = weight_copies(at, 2, refs[:8], w, w_sem)
        copies = []
        for k, (own, near, to) in enumerate(((fi, ni, w_in), (fo, nf, w_out))):
            copies.append(pltpu.make_async_copy(own.at[1], to.at[pl.ds(0, hidden)], sem.at[2 * k]))
            copies.append(pltpu.make_async_copy(near.at[1], to.at[pl.ds(hidden, hidden)], sem.at[1 + 2 * k]))
        for copy in copies:
            copy.start()
        cot = by_owner(at, cot_ref)
        cot_out[...] = cot
        e = (h1_ref[...].astype(f32) + (p0[...].astype(f32) + p1[...].astype(f32))).astype(bf16)
        e_ref[...] = e
        for one in first:
            one.wait()
        k = dot_nn(e, w[1]).astype(bf16)
        v = dot_nn(e, w[2]).astype(bf16)
        q = dot_nn(n4_ref[...], w[0]).astype(bf16)
        q_ref[...], k_ref[...], v_ref[...] = q, k, v
        c = small_attend("cross", q, k, v, p_ref)
        c_ref[...] = c
        g = (m_ref[...] + dot_nn(c, w[3])).astype(bf16)
        g_ref[...] = g
        n5 = norm_rows(g.astype(f32), gain_ref[4:5])
        n5_ref[...] = n5
        copies[0].wait()
        copies[1].wait()
        a, slope = gelu_both(dot_nt(n5, w_in[...]))
        a_ref[...] = a
        copies[2].wait()
        copies[3].wait()
        du = (slope.astype(f32) * dot_nt(cot, w_out[...])).astype(bf16)
        du_ref[...] = du
        dn_ref[...] = dot_nn(du, w_in[...]).astype(bf16)
        o_ref[...] = dot_nn(a, w_out[...]).astype(bf16)

    rows, small = whole(BUF, D), whole(DEC, D)
    big_low, low = (shape((BUF, D)), rows), (shape((DEC, D)), small)
    wide = (shape((DEC, 2 * hidden)), whole(DEC, 2 * hidden))
    return call(
        kernel, (1,), scalars,
        [
            (h1, rows), (part, rows), (other, rows), (m, small), (n4, small),
            (gains, whole(5, D)), (cotangent, core_rows()),
            (feed_in, ANYWHERE), (near_in, ANYWHERE), (feed_out, ANYWHERE), (near_out, ANYWHERE),
        ]
        + weight_args(cross_w),
        [
            big_low, low, big_low, big_low, low, (shape((HEADS, BUF, DEC)), whole(HEADS, BUF, DEC)),
            low, low, low, wide, wide, low, low,
        ],
        WEIGHT_SCRATCH
        + [
            pltpu.VMEM((2 * hidden, D), bf16), pltpu.VMEM((2 * hidden, D), bf16), pltpu.SemaphoreType.DMA((4,)),
        ],
        2 * 10**10,
    )


def feed_weights(scalars, lefts, right_rows, hidden):
    count = hidden // FTILE
    pairs = len(lefts)
    rows = lefts[0].shape[0]

    def kernel(at, *refs):
        step = pl.program_id(0)
        ins, outs = refs[: 2 * pairs], refs[2 * pairs :]
        for keep, to in ((step < count, outs[:pairs]), (step >= count, outs[pairs:])):

            @pl.when(keep)
            def _(to=to):
                for k in range(pairs):
                    to[k][...] = dot_nn(transposed(ins[2 * k][...]), ins[2 * k + 1][...]).astype(bf16)

    tile = pl.BlockSpec((rows, FTILE), lambda i, at: (0, i))
    ins = []
    for left, right in zip(lefts, right_rows):
        ins += [(left, tile), (right, whole(rows, D))]
    kind = shape((hidden, D))
    own = (kind, pl.BlockSpec((FTILE, D), lambda i, at: (jnp.minimum(i, count - 1), 0)))
    other = (kind, pl.BlockSpec((FTILE, D), lambda i, at: (jnp.maximum(i - count, 0), 0)))
    return call(
        kernel, (2 * count,), scalars, ins, [own] * pairs + [other] * pairs,
        flops=10**10,
    )


def cross_back(scalars, g, gains, p0, p1, cot, cross_w, q, k, v, c, weights, m):
    def kernel(
        at, g_ref, gain_ref, p0_ref, p1_ref, cot_ref, q_ref, k_ref, v_ref, c_ref, p_ref, m_ref, *refs
    ):
        dg_ref, dq_ref, dk_ref, dv_ref, de_ref, gain_out, dm_ref, w, sem = refs[8:]
        copies = weight_copies(at, 2, refs[:8], w, sem)
        dn5 = p0_ref[...].astype(f32) + p1_ref[...].astype(f32)
        dg_rows, gain4 = norm_back(g_ref[...].astype(f32), gain_ref[4:5], dn5)
        dg = (dg_rows + cot_ref[...].astype(f32)).astype(bf16)
        dg_ref[...] = dg
        for one in copies:
            one.wait()
        dc = dot_nt(dg, w[3]).astype(bf16)
        dq, dk, dv = small_attend_back(q_ref[...], k_ref[...], v_ref[...], c_ref[...], dc, p_ref)
        dq_ref[...], dk_ref[...], dv_ref[...] = dq, dk, dv
        de_ref[...] = (dot_nt(dk, w[1]) + dot_nt(dv, w[2])).astype(bf16)
        dm_rows, gain3 = norm_back(m_ref[...], gain_ref[3:4], dot_nt(dq, w[0]))
        dm_ref[...] = dm_rows + dg.astype(f32)
        gain_out[...] = jnp.concatenate([gain3, gain4], axis=0)

    rows, small = whole(BUF, D), whole(DEC, D)
    big_low, low = (shape((BUF, D)), rows), (shape((DEC, D)), small)
    return call(
        kernel, (1,), scalars,
        [
            (g, small), (gains, whole(5, D)), (p0, small), (p1, small), (cot, small),
            (q, small), (k, rows), (v, rows), (c, small), (weights, whole(HEADS, BUF, DEC)), (m, small),
        ]
        + weight_args(cross_w),
        [low, low, big_low, big_low, big_low, (shape((2, D), f32), whole(2, D)), (shape((DEC, D), f32), small)],
        WEIGHT_SCRATCH,
        2 * 10**10,
    )


def enc_feed_back(scalars, de, slope, feed_in, near_in, feed_out, near_out):
    count = feed_in.shape[1] // FTILE

    def kernel(at, de_ref, s_ref, fi, ni, fo, nf, du_ref, p_ref, total):
        step = pl.program_id(0)
        w_in = jnp.where(step < count, fi[0], ni[0])
        w_out = jnp.where(step < count, fo[0], nf[0])
        du = (s_ref[...].astype(f32) * dot_nt(de_ref[...], w_out)).astype(bf16)
        du_ref[...] = du
        grad = dot_nn(du, w_in)

        @pl.when(step == 0)
        def _():
            total[...] = grad

        @pl.when(step > 0)
        def _():
            total[...] += grad

        @pl.when(step == 2 * count - 1)
        def _():
            p_ref[...] = total[...].astype(bf16)

    own, near = feed_specs(0, count)
    tile = pl.BlockSpec((BUF, FTILE), lambda i, at: (0, i))
    return call(
        kernel, (2 * count,), scalars,
        [(de, whole(BUF, D)), (slope, tile), (feed_in, own), (near_in, near), (feed_out, own), (near_out, near)],
        [(shape(slope.shape), tile), (shape((BUF, D)), whole(BUF, D))],
        [pltpu.VMEM((BUF, D), f32)], 2 * 10**10,
    )


def chip_cols(at, ref):
    return ref[:, pl.ds(pl.multiple_of(at[ACROSS] * BIG, 128), BIG)]


def store_rows(at, grads, own_ref, other_ref):
    first = at[CORE] == 0
    for i, grad in enumerate(grads):
        low = grad.astype(bf16)
        half = low.shape[0] // 2
        own_ref[i] = jnp.where(first, low[:half], low[half:])
        other_ref[i] = jnp.where(first, low[half:], low[:half])


def quarter_outs(mats):
    kind = (shape((mats, BIG // 2, D)), whole(mats, BIG // 2, D))
    return [kind, kind]


def cross_weights(scalars, n4, dq, e, dk, dv, c, dg):
    def kernel(at, n4_ref, dq_ref, e_ref, dk_ref, dv_ref, c_ref, dg_ref, own_ref, other_ref):
        n4_t, e_t, c_t = (transposed(chip_cols(at, ref)) for ref in (n4_ref, e_ref, c_ref))
        pairs = ((n4_t, dq_ref), (e_t, dk_ref), (e_t, dv_ref), (c_t, dg_ref))
        store_rows(at, [dot_nn(left, right[...]) for left, right in pairs], own_ref, other_ref)

    rows, small = whole(BUF, D), whole(DEC, D)
    return call(
        kernel, (1,), scalars,
        [(n4, small), (dq, small), (e, rows), (dk, rows), (dv, rows), (c, small), (dg, small)],
        quarter_outs(4),
    )


def self_back(scalars, dm, gains, self_w, q, k, v, c, weights, xd, n3):
    def kernel(at, dm_ref, gain_ref, q_ref, k_ref, v_ref, c_ref, p_ref, xd_ref, n3_ref, *refs):
        own_ref, other_ref, grad_ref, gain_out, diag_ref, w, sem = refs[8:]
        copies = weight_copies(at, 1, refs[:8], w, sem)
        dm = dm_ref[...]
        low = dm.astype(bf16)
        for one in copies:
            one.wait()
        dc = dot_nt(low, w[3]).astype(bf16)
        dq, dk, dv = small_attend_back(q_ref[...], k_ref[...], v_ref[...], c_ref[...], dc, p_ref, diag_ref)
        dn3 = dot_nt(dq, w[0]) + dot_nt(dk, w[1]) + dot_nt(dv, w[2])
        dd, gain2 = norm_back(xd_ref[...].astype(f32), gain_ref[2:3], dn3)
        gain_out[...] = gain2
        grad = (dd + dm).astype(bf16)
        for i in range(QPB):
            grad_ref[pl.ds(pl.multiple_of(at[OWNER + i] * TGT, TGT), TGT)] = grad[i * TGT : (i + 1) * TGT]
        n3_t, c_t = transposed(chip_cols(at, n3_ref)), transposed(chip_cols(at, c_ref))
        store_rows(at, [dot_nn(n3_t, dq), dot_nn(n3_t, dk), dot_nn(n3_t, dv), dot_nn(c_t, low)], own_ref, other_ref)

    small = whole(DEC, D)
    return call(
        kernel, (1,), scalars,
        [
            (dm, small), (gains, whole(5, D)),
            (q, small), (k, small), (v, small), (c, small), (weights, whole(HEADS, DEC, DEC)), (xd, small), (n3, small),
        ]
        + weight_args(self_w),
        quarter_outs(4)
        + [
            (shape((DEC, D)), small), (shape((1, D), f32), whole(1, D)),
            (shape((HEADS, 1, 256), f32), whole(HEADS, 1, 256)),
        ],
        WEIGHT_SCRATCH, 10**9,
    )


def enc_back(scalars, opening, gains, xr, chunk, chunk_c, n1=None, start=None, carried=None):
    half = BIG // 2
    first = 0 if opening else 3

    def kernel(at, gain_ref, xr_ref, wo_ref, ca_ref, cb_ref, qkv_ref, c_ref, big_ref, rest_ref, w_ref, *refs):
        if opening:
            h1_ref, p0_ref, p1_ref, de_ref, n1_ref = refs[:5]
            own_ref, other_ref, diag_ref, rdiag_ref, dh1_ref, dn1_ref, n1_t, c_t, gain_out = refs[5:]
        else:
            dh1_ref, dn1_in, n1_t, c_t = refs[:4]
            own_ref, other_ref, diag_ref, rdiag_ref, grad_ref, gain_out, dn1_ref, twice = refs[6:]
        p = pl.program_id(0)

        @pl.when(p == 0)
        def _():
            if opening:
                dn2 = p0_ref[...].astype(f32) + p1_ref[...].astype(f32)
                dh1_rows, gain1 = norm_back(h1_ref[...].astype(f32), gain_ref[1:2], dn2)
                dh1_ref[...] = (dh1_rows + de_ref[...].astype(f32)).astype(bf16)
                gain_out[...] = gain1
                n1_t[...] = chip_cols(at, n1_ref).T
                c_t[...] = jnp.where(at[ACROSS] == 0, ca_ref[...], cb_ref[...]).T
                dn1_ref[...] = jnp.zeros_like(dn1_ref)
            else:
                dn1_ref[...] = dn1_in[...]

        qkv, c, w = qkv_ref[0], c_ref[...], w_ref[0]
        q, k, v = qkv[:, :128], qkv[:, 128:256], qkv[:, 256:]
        dh1 = dh1_ref[...]
        grads = dot_nt(dh1, wo_ref[...]).astype(bf16)
        keys_t = k.T
        product_t = (grads.astype(f32) * c.astype(f32)).T
        dq_t = []
        dk_big = dv_big = dk_rest = dv_rest = 0.0
        for hh in range(2):
            row_sum = jnp.sum(product_t[hh * HD : (hh + 1) * HD], axis=0, keepdims=True)
            queries, values, grads_h = lane_half(q, hh), lane_half(v, hh), lane_half(grads, hh)
            head_k = keys_t[hh * HD : (hh + 1) * HD]
            weights = big_ref[hh]
            ds = score_grad(weights, dot_nt(values[:BIG], grads[:BIG]), row_sum[:, :BIG])
            dv_big = dv_big + dot_nn(weights, grads_h[:BIG])
            dk_big = dk_big + dot_nn(ds, queries[:BIG])
            diag_ref[hh] = jnp.concatenate(
                [diagonals(ds[128 * b : 128 * (b + 1)], WIDE) for b in range(3)], axis=0
            )
            dq_head = dot_nn(head_k[:, :BIG], ds)
            weights = rest_ref[hh]
            ds = score_grad(weights, dot_nt(values[BIG:], grads[BIG:]), row_sum[:, BIG:])
            dv_rest = dv_rest + dot_nn(weights, grads_h[BIG:])
            dk_rest = dk_rest + dot_nn(ds, queries[BIG:])
            rdiag_ref[hh] = diagonals(ds, 2 * REST)
            dq_t.append(jnp.concatenate([dq_head, dot_nn(head_k[:, BIG:], ds)], axis=1))
        dq = jnp.concatenate(dq_t, axis=0).T.astype(bf16)
        dk = jnp.concatenate([dk_big, dk_rest], axis=0).astype(bf16)
        dv = jnp.concatenate([dv_big, dv_rest], axis=0).astype(bf16)
        dqkv = jnp.concatenate([dq, dk, dv], axis=1)
        dn1_ref[...] += dot_nt(dqkv, w)
        grad = dot_nn(n1_t[...], dqkv)
        columns = pl.ds(pl.multiple_of(128 * (first + p), 128), 128)
        out_grad = dot_nn(c_t[...], dh1_ref[:, columns])
        store_rows(at, [grad[:, 128 * i : 128 * i + 128] for i in range(3)] + [out_grad], own_ref, other_ref)

        if not opening:

            @pl.when(p == 2)
            def _():
                rows, gain0 = norm_back(xr_ref[...].astype(f32), gain_ref[0:1], dn1_ref[...])
                gain_out[...] = gain0
                low = (rows + dh1.astype(f32)).astype(bf16)
                twice[:BUF] = low
                twice[BUF:] = low
                grad_ref[...] = twice[pl.ds(pl.multiple_of(BUF - at[START], SMALL), BUF)]

    rows = whole(BUF, D)
    wo = start[4] if opening else carried[-1]
    qkv, c, big, rest, w = chunk
    ins = [
        (gains, whole(5, D)), (xr, rows), (wo, pl.BlockSpec((128, D), lambda p, at: (first + p, 0))),
        (chunk_c[0], whole(BUF, BIG)), (chunk_c[1], whole(BUF, BIG)),
        (qkv, pl.BlockSpec((1, BUF, BIG), lambda p, at: (p, 0, 0))),
        (c, pl.BlockSpec((BUF, 128), lambda p, at: (0, p))),
        (big, pl.BlockSpec((2, BIG, BIG), lambda p, at: (p, 0, 0))),
        (rest, pl.BlockSpec((2, REST, REST), lambda p, at: (p, 0, 0))),
        (w, pl.BlockSpec((1, D, BIG), lambda p, at: (p, 0, 0))),
    ]
    columns = (shape((4, half, D)), pl.BlockSpec((4, half, 128), lambda p, at: (0, 0, first + p)))
    outs = [
        columns, columns,
        (shape((6, 3, WIDE), f32), pl.BlockSpec((2, 3, WIDE), lambda p, at: (p, 0, 0))),
        (shape((6, 1, 2 * REST), f32), pl.BlockSpec((2, 1, 2 * REST), lambda p, at: (p, 0, 0))),
    ]
    low, turned = (shape((BUF, D)), rows), (shape((BIG, BUF)), whole(BIG, BUF))
    one = (shape((1, D), f32), whole(1, D))
    scratch, aliases = (), {}
    if opening:
        ins += [(value, rows) for value in start[:4]] + [(n1, rows)]
        outs += [low, (shape((BUF, D), f32), rows), turned, turned, one]
    else:
        own, other, dh1, dn1, n1_t, c_t, _ = carried
        ins += [(dh1, rows), (dn1, rows), (n1_t, whole(BIG, BUF)), (c_t, whole(BIG, BUF)), (own, ANYWHERE), (other, ANYWHERE)]
        aliases = {len(ins) - 1: 0, len(ins): 1}
        outs += [low, one]
        scratch = [pltpu.VMEM((BUF, D), f32), pltpu.VMEM((2 * BUF, D), bf16)]
    return call(kernel, (3,), scalars, ins, outs, scratch, 2 * 10**10, aliases)


def swap_section(value, bit):
    count = lax.axis_size("section")
    return lax.ppermute(value, "section", [(i, i ^ bit) for i in range(count)])


def swap_dp(value, bit):
    count = lax.axis_size("dp")
    return lax.ppermute(value, "dp", [(i, i ^ bit) for i in range(count)])


def add_low(a, b):
    return (a.astype(f32) + b.astype(f32)).astype(bf16)


def tie(value, *deps):
    return lax.optimization_barrier((value,) + deps)[0] if deps else value


def halves(own, got, extra=None):
    half = own.shape[0] // 2
    mine = lax.axis_index("dp") % 2

    def part(which):
        rows = [lax.dynamic_slice_in_dim(value, which * half, half, 0) for value in (own, got)]
        total = add_low(*rows)
        return total if extra is None else jnp.concatenate([total, extra])

    return part(mine), part(1 - mine)


def rejoin(keep, other):
    mine = lax.axis_index("dp") % 2
    keep = keep[: other.shape[0]]
    return jnp.where(mine == 0, jnp.concatenate([keep, other]), jnp.concatenate([other, keep]))


Y_TIME, TREE_TIME, STEP = 12.7, 12.7, 3.0
STAGES = (("y", Y_TIME), ("in", TREE_TIME), ("mid", TREE_TIME), ("out", TREE_TIME), ("y", Y_TIME))
ROUTES = {
    "y": tuple((i, i ^ 1) for i in range(8)),
    "in": ((0, 2), (1, 3), (6, 4), (7, 5)),
    "mid": ((2, 4), (3, 5), (4, 2), (5, 3)),
    "out": ((2, 0), (3, 1), (4, 6), (5, 7)),
}


class GradSum:
    def __init__(self, pieces):
        self.count = lax.axis_size("dp")
        self.value = {}
        self.extra = None
        self.stage = {i: 0 for i in pieces}
        self.links = {name: [] for name in ROUTES}
        self.sent, self.got = {}, {}

    def enter(self, i, own, got, extra=None):
        own, got = own.reshape(-1, D), got.reshape(-1, D)
        if self.count != 8:
            self.value[i] = lax.psum(add_low(own, got), "dp")
            self.extra = None if extra is None else lax.psum(extra, "dp")
        else:
            self.value[i] = (own, got, extra)

    def step(self, i, *after):
        now = self.stage[i]
        self.stage[i] = now + 1
        if self.count != 8:
            return
        link = STAGES[now][0]
        value = self.value[i]
        if now > 0:
            value = tie(value, *after)
        if now == 0:
            value, sent = halves(*(tie(value[0], *after), tie(value[1], *after), value[2]))
        elif now == 4:
            sent = value[: value.shape[0] // 128 * 128]
            if sent.shape != value.shape:
                self.extra = value[sent.shape[0] :]
        else:
            sent = value
        before = self.links[link]
        sent = tie(sent, *before[-2:-1])
        got = lax.ppermute(sent, "dp", ROUTES[link])
        before.append(got)
        z = lax.axis_index("dp") // 2
        if now < 3:
            value = add_low(value, got)
        elif now == 3:
            value = jnp.where((z == 0) | (z == 3), got, value)
        else:
            value = rejoin(value, got)
        self.value[i], self.sent[i, now], self.got[i, now] = value, sent, got

    def between(self, after, ended, begun):
        for i in begun:
            self.step(i, after)
        if self.count != 8:
            return []
        return [self.got[key] for key in ended] + [self.sent[i, self.stage[i] - 1] for i in begun]

    def finish(self, late):
        free = {name: 0.0 for name in ROUTES}
        at = {i: late.get(i, 0.0) for i in self.stage}
        while min(self.stage.values()) < len(STAGES):
            best = None
            for i, now in self.stage.items():
                if now < len(STAGES):
                    key = (max(at[i], free[STAGES[now][0]]), now - len(STAGES), i)
                    best = key if best is None else min(best, key)
            begin, _, i = best
            link, length = STAGES[self.stage[i]]
            free[link], at[i] = begin + length + 0.5, begin + length + STEP
            self.step(i)
        return self.value


def shards(
    encoder_in, decoder_in, lengths, query_map, attn_query, attn_keyval, attn_output,
    feed_in, feed_out, norm_gains, position_bias, cotangent,
):
    section_id = lax.axis_index("section")
    across = section_id // 2
    core = section_id % 2
    quarter = attn_query.shape[1]
    half = 2 * quarter

    dp_id = lax.axis_index("dp")
    own = (attn_query, attn_keyval, attn_output)
    near = tuple(swap_section(a, 1) for a in own)
    hidden = feed_in.shape[1]

    def packed(index, mats, first, last):
        parts = [attn_query[index : index + 1], attn_keyval[2 * index : 2 * index + 2], attn_output[index : index + 1]]
        return jnp.concatenate(parts[: mats - 1], axis=0)[:, :, first:last]

    bases = [(section_id ^ k) * quarter for k in range(4)]
    def piece_of(index, count, *after):
        size = quarter // count
        piece = lax.dynamic_slice_in_dim(packed(index, 4, 0, D), (dp_id % count) * size, size, 1)
        return swap_section(tie(piece, *after), 2)

    def places(count):
        at = dp_id % count
        return [(at ^ k) * (quarter // count) if k < count else 0 for k in range(4)]

    got_a = swap_section(packed(0, 3, 0, D // 2), 2)

    big = jnp.argmax(lengths[core]).astype(jnp.int32)
    owners = lax.dynamic_slice_in_dim(jnp.concatenate([query_map[core]] * 2), big, QPB, 0)
    scalars = jnp.concatenate(
        [jnp.stack([core, across, big * SMALL]), owners, jnp.stack(bases + places(4) + places(2))]
    ).astype(jnp.int32)

    enc_table = spread_table(position_bias[0], encoder_bucket(enc_offsets()))
    dec_table = spread_table(position_bias[1], decoder_bucket(dec_offsets())[None])
    sums = GradSum(range(7))

    near_a = swap_section(tie(got_a, scalars, enc_table, dec_table), 1)
    got_b = swap_section(tie(packed(0, 3, D // 2, D), got_a), 2)
    got_self = piece_of(1, 4, got_a)
    first = enc_attention(scalars, encoder_in, norm_gains, enc_table, own, near, got_a, near_a, 0)
    n1, xr = first[5:]
    got_o = swap_section(tie(attn_output[0], n1), 2)
    near_b = swap_section(tie(got_b, n1), 1)
    got_cross = piece_of(2, 2, n1)
    pair = tie(got_self, n1)
    pair = jnp.stack([pair, swap_dp(pair, 1)])
    near_in = swap_section(tie(feed_in, near_a), 1)
    near_out = swap_section(tie(feed_out, near_a), 1)
    second = enc_attention(scalars, n1, norm_gains, enc_table, own, near, got_b, near_b, 1)
    near_got_o = swap_section(tie(got_o, second[1]), 1)
    pair = tie(pair, second[1])
    quad = jnp.concatenate([pair, swap_dp(pair, 2)])
    h1, n2, a1, slope1, part, wo = enc_feed(
        scalars, xr, first[1], second[1], attn_output, near[2], got_o, near_got_o, norm_gains,
        feed_in, near_in, feed_out, near_out,
    )
    part_other = swap_section(part, 2)
    self_w = own + near + (quad, swap_section(quad, 1))
    pair = tie(got_cross, second[1])
    pair = jnp.stack([pair, swap_dp(pair, 1)])
    cross_w = own + near + (pair, swap_section(pair, 1))
    xd, n3, q2, k2, v2, c2, p2, m, n4 = dec_self(scalars, decoder_in, norm_gains, dec_table, self_w)
    e, q3, k3, v3, c3, p3, g, n5, cot, a2, du2, dn5, out_part = dec_cross(
        scalars, h1, part, part_other, m, n4, cross_w, norm_gains, cotangent, feed_in, near_in, feed_out, near_out
    )

    dn5_other = swap_section(dn5, 2)
    own_out, own_in, other_out, other_in = feed_weights(scalars, (a2, du2), (cot, n5), hidden)
    sums.enter(0, own_out, swap_section(other_out, 1))
    sums.enter(1, own_in, swap_section(other_in, 1))

    dg, dq3, dk3, dv3, de, gains34, dm = cross_back(
        scalars, g, norm_gains, dn5, dn5_other, cot, cross_w, q3, k3, v3, c3, p3, m
    )
    de = tie(de, *sums.between(dq3, (), (0, 1)))
    du1, dn2 = enc_feed_back(scalars, de, slope1, feed_in, near_in, feed_out, near_out)
    dn2_other = swap_section(dn2, 2)
    own_w, other_w = cross_weights(scalars, n4, dq3, e, dk3, dv3, c3, tie(dg, dn2))
    sums.enter(2, own_w, swap_section(other_w, 1))

    dm = tie(dm, own_w, *sums.between(own_w, ((0, 0),), (0,)))
    own_w, other_w, dec_grad, gain2, diag2 = self_back(scalars, dm, norm_gains, self_w, q2, k2, v2, c2, p2, xd, n3)
    sums.enter(5, own_w, swap_section(other_w, 1))

    n2_late = tie(n2, own_w, dn2_other, *sums.between(dec_grad, ((1, 0),), (1,)))
    own_out, own_in, other_out, other_in = feed_weights(scalars, (a1, du1), (de, n2_late), hidden)
    sums.enter(3, own_out, swap_section(other_out, 1))
    sums.enter(4, own_in, swap_section(other_in, 1))

    dn2_late = tie(dn2_other, own_in, *sums.between(own_in, ((0, 1),), (2, 5, 0)))
    contexts = (first[1], second[1])
    own_w, other_w, diag_a, rdiag_a, dh1, dn1, n1_t, c_t, gain1 = enc_back(
        scalars, True, norm_gains, xr, first[:5], contexts, n1, (h1, dn2, dn2_late, de, wo)
    )
    dn1 = tie(dn1, *sums.between(dh1, ((2, 0), (1, 1)), (3, 4, 2, 1)))
    own_enc, other_w, diag_b, rdiag_b, enc_grad, gain0 = enc_back(
        scalars, False, norm_gains, xr, second[:5], contexts, carried=(own_w, other_w, dh1, dn1, n1_t, c_t, wo)
    )
    got_w = swap_section(other_w, 1)

    hot_enc = jnp.asarray(
        np.concatenate(
            [one_hot(encoder_bucket(128 * b + diagonal_offsets(128, WIDE))) for b in range(3)]
            + [one_hot(encoder_bucket(diagonal_offsets(REST, 2 * REST)))]
        )
    )
    hot_dec = jnp.asarray(one_hot(decoder_bucket(diagonal_offsets(DEC, 256))))
    sums_enc = jnp.concatenate(
        [
            jnp.concatenate([d.reshape(HEADS // 2, -1), r.reshape(HEADS // 2, -1)], axis=1)
            for d, r in ((diag_a, rdiag_a), (diag_b, rdiag_b))
        ]
    )
    exact = lax.Precision.HIGHEST
    table_enc = jnp.einsum("mb,hm->bh", hot_enc, sums_enc, precision=exact)
    table_dec = jnp.einsum("mb,hm->bh", hot_dec, diag2.reshape(HEADS, -1), precision=exact)
    tables = jnp.stack([table_enc, table_dec]).reshape(-1, D)
    small = jnp.concatenate([gain0, gain1, gain2, gains34, tables, jnp.zeros((10, D), f32)])
    small = small + swap_section(small, 1)
    sums.enter(6, own_enc, got_w, small.astype(bf16))
    total = sums.finish({6: 6.0})
    unit_out2, unit_in2, unit_cross, unit_out1, unit_in1, unit_self, unit_enc = (total[i] for i in range(7))
    small = sums.extra.astype(f32)
    gains = small[:5]
    tables = small[5].reshape(2, NB, HEADS)

    def split_rows(rows, count):
        mine = lax.dynamic_slice_in_dim(rows, section_id * count, count, 0)
        theirs = swap_section(lax.dynamic_slice_in_dim(rows, (section_id ^ 1) * count, count, 0), 1)
        return jnp.where(core == 0, jnp.stack([mine, theirs]), jnp.stack([theirs, mine]))

    out_rows = (g.astype(f32) + (out_part.astype(f32) + swap_section(out_part, 2).astype(f32))).astype(bf16)
    restored = jnp.zeros((DEC, D), bf16)
    for i in range(QPB):
        restored = lax.dynamic_update_slice_in_dim(restored, out_rows[i * TGT : (i + 1) * TGT], owners[i] * TGT, 0)
    sections = lax.axis_size("section")
    decoder_out = split_rows(restored, DEC // sections)
    decoder_in_grad = split_rows(dec_grad, DEC // sections)
    encoder_in_grad = split_rows(enc_grad, BUF // sections)

    u_enc, u_self, u_cross = (
        u.reshape(4, quarter, D).astype(f32) for u in (unit_enc, unit_self, unit_cross)
    )
    query_grad = jnp.stack([u_enc[0], u_self[0], u_cross[0]])
    keyval_grad = jnp.concatenate([u_enc[1:3], u_self[1:3], u_cross[1:3]])
    output_grad = jnp.stack([u_enc[3], u_self[3], u_cross[3]])
    feed_in_grad = jnp.stack([unit_in1, unit_in2]).astype(f32)
    feed_out_grad = jnp.stack([unit_out1, unit_out2]).astype(f32)
    return (
        decoder_out, encoder_in_grad, decoder_in_grad, query_grad, keyval_grad, output_grad,
        feed_in_grad, feed_out_grad, gains, tables,
    )


def solution(mesh):
    rows = P("dp", None, None)
    mats = P(None, "section", None)
    outs = P("dp", "section", None)
    return jax.shard_map(
        shards,
        mesh=mesh,
        in_specs=(rows, rows, P("dp", None), P("dp", None), mats, mats, mats, mats, mats, P(), P(), rows),
        out_specs=(outs, outs, outs, mats, mats, mats, mats, mats, P(), P()),
        check_vma=False,
    )
```

```python
import functools

import jax
import jax.numpy as jnp
import numpy as np
from jax import lax
from jax.experimental import pallas as pl
from jax.experimental.pallas import tpu as pltpu
from jax.sharding import PartitionSpec as P

D = 768
HEADS = 12
HD = 64
PAIRS = HEADS // 2
NB = 32
BUF = 512
BIG = 384
SMALL = 64
REST = BUF - BIG
QPB = 3
TGT = 32
DEC = QPB * TGT
WIDE = 512
epsilon = 1e-06
masked_score = -1e30
enc_edges = (12, 16, 23, 32, 46, 64, 91)
dec_edges = (19, 21, 24, 27, 31)
bf16 = jnp.bfloat16
f32 = jnp.float32


def dot_nn(a, b):
    return lax.dot_general(a, b, (((1,), (0,)), ((), ())), preferred_element_type=f32)


def dot_nt(a, b):
    return lax.dot_general(a, b, (((1,), (1,)), ((), ())), preferred_element_type=f32)


def dot_tn(a, b):
    return lax.dot_general(a, b, (((0,), (0,)), ((), ())), preferred_element_type=f32)


def encoder_bucket(offset):
    distance = np.abs(offset)
    bucket = np.minimum(distance, 8)
    for boundary in enc_edges:
        bucket = bucket + (distance >= boundary)
    return bucket + 16 * (offset > 0)


def decoder_bucket(offset):
    distance = np.maximum(-offset, 0)
    bucket = np.minimum(distance, 16)
    for boundary in dec_edges:
        bucket = bucket + (distance >= boundary)
    return bucket


def enc_offsets():
    lane = np.arange(WIDE)
    shifted = np.where(lane < BIG, lane, lane - WIDE)
    return 128 * np.arange(3)[:, None] - shifted[None, :]


def diagonal_offsets(rows, width):
    return rows - 1 - np.arange(width)


def dec_offsets():
    return np.arange(TGT)[:, None] - np.arange(TGT)[None, :]


def one_hot(bucket):
    return (bucket[..., None] == np.arange(NB)).astype(np.float32)


def spread_table(table, bucket):
    hot = jnp.asarray(one_hot(bucket))
    return jnp.sum(hot[None] * jnp.transpose(table).reshape((HEADS,) + (1,) * bucket.ndim + (NB,)), axis=-1)


def norm_scale(rows):
    return lax.rsqrt(jnp.mean(rows * rows, axis=-1, keepdims=True) + epsilon)


def norm_rows(rows, gain):
    return (rows * norm_scale(rows) * gain).astype(bf16)


def norm_back(rows, gain, grad):
    scale = norm_scale(rows)
    unit = rows * scale
    weighted = grad * gain
    grad_rows = scale * (weighted - unit * jnp.mean(weighted * unit, axis=-1, keepdims=True))
    return grad_rows, jnp.sum(grad * unit, axis=0, keepdims=True)


def gelu_both(u):
    root = np.float32(np.sqrt(2.0 / np.pi))
    cubic = np.float32(0.044715)
    square = u * u
    bend = jnp.tanh(u * (root + root * cubic * square))
    half = 0.5 * (1.0 + bend)
    slope = half + 0.5 * u * (1.0 - bend * bend) * (root + 3.0 * root * cubic * square)
    return (u * half).astype(bf16), slope.astype(bf16)


CORE, ACROSS, START, OWNER, BASE, PIECE = 0, 1, 2, 3, 6, 10


def shape(dims, dtype=bf16):
    return jax.ShapeDtypeStruct(dims, dtype)


def whole(*dims):
    return pl.BlockSpec(dims, lambda *_: (0,) * len(dims))


def call(kernel, grid, scalars, ins, outs, scratch=(), flops=10**10, aliases=None):
    return pl.pallas_call(
        kernel,
        grid_spec=pltpu.PrefetchScalarGridSpec(
            num_scalar_prefetch=1,
            grid=grid,
            in_specs=[spec for _, spec in ins],
            out_specs=tuple(spec for _, spec in outs),
            scratch_shapes=scratch,
        ),
        out_shape=tuple(kind for kind, _ in outs),
        input_output_aliases=aliases or {},
        compiler_params=pltpu.CompilerParams(vmem_limit_bytes=25 << 20),
        cost_estimate=pl.CostEstimate(flops=flops, bytes_accessed=1 << 20, transcendentals=0),
    )(scalars, *[array for array, _ in ins])


def lane_half(value, which):
    lane = lax.broadcasted_iota(jnp.int32, value.shape, 1)
    keep = (lane < HD) if which == 0 else (lane >= HD)
    return jnp.where(keep, value, jnp.zeros_like(value))


def softmax_t(scores):
    peak = jnp.max(scores, axis=0, keepdims=True)
    raised = jnp.exp(scores - peak)
    total = jnp.sum(raised, axis=0, keepdims=True)
    return (raised * (1.0 / total)).astype(bf16)


def toeplitz(row, rows):
    spread = jnp.broadcast_to(row, (rows, row.shape[-1]))
    return pltpu.roll(spread, 0, 1, stride=1, stride_axis=0)


def diagonals(value, width):
    rows = value.shape[0]
    row = lax.broadcasted_iota(jnp.int32, (rows, rows), 0)
    col = lax.broadcasted_iota(jnp.int32, (rows, rows), 1)
    flipped = dot_nn((row + col == rows - 1).astype(bf16), value)
    padded = jnp.concatenate([flipped, jnp.zeros((rows, width - value.shape[1]), f32)], axis=1)
    return jnp.sum(pltpu.roll(padded, 0, 1, stride=1, stride_axis=0), axis=0, keepdims=True)


def rest_mask():
    row = lax.broadcasted_iota(jnp.int32, (REST, REST), 0) // SMALL
    col = lax.broadcasted_iota(jnp.int32, (REST, REST), 1) // SMALL
    return row == col


def score_grad(weights, grad_weights, row_sum):
    return (weights.astype(f32) * (grad_weights - row_sum)).astype(bf16)


def transposed(value):
    return value.astype(f32).T.astype(bf16) if value.dtype == bf16 and value.shape[0] % 128 else value.T


def take_near(at, own, near, which):
    return jnp.where(which, own[0], near[0])


def attend_pair(q, k, v, bias_ref, big_ref, rest_ref):
    values_t = v.T
    allowed = rest_mask()
    heads = []
    for hh in range(2):
        queries = lane_half(q, hh)
        bias = [toeplitz(bias_ref[hh, b : b + 1, :], 128)[:, :BIG] for b in range(3)]
        scores = dot_nt(k[:BIG], queries[:BIG]) + jnp.concatenate(bias, axis=0)
        weights = softmax_t(scores)
        big_ref[hh] = weights
        head_v = values_t[hh * HD : (hh + 1) * HD]
        context = dot_nn(head_v[:, :BIG], weights)
        rest = dot_nt(k[BIG:], queries[BIG:]) + bias[0][:, :REST]
        rest = softmax_t(jnp.where(allowed, rest, masked_score))
        rest_ref[hh] = rest
        heads.append(jnp.concatenate([context, dot_nn(head_v[:, BIG:], rest)], axis=1))
    return jnp.concatenate(heads, axis=0).T.astype(bf16)


def enc_attention(scalars, rows, gains, bias, own, near, got, got_near, chunk):
    opening = chunk == 0
    quarter = got.shape[1]

    def kernel(at, rows_ref, gain_ref, bias_ref, oq, okv, nq, nkv, gw, gnw, *refs):
        if opening:
            qkv_ref, c_ref, big_ref, rest_ref, w_ref, n1_ref, xr_ref, twice = refs
            @pl.when(pl.program_id(0) == 0)
            def _():
                twice[:BUF] = rows_ref[0]
                twice[BUF:] = rows_ref[0, :REST]
                rolled = twice[pl.ds(pl.multiple_of(at[START], SMALL), BUF)]
                xr_ref[...] = rolled
                n1_ref[...] = norm_rows(rolled.astype(f32), gain_ref[0:1])
        else:
            qkv_ref, c_ref, big_ref, rest_ref, w_ref = refs
            n1_ref = rows_ref
        parts = ((oq[0], okv[0], okv[1]), (nq[0], nkv[0], nkv[1]), (gw[0], gw[1], gw[2]), (gnw[0], gnw[1], gnw[2]))
        for k, mats in enumerate(parts):
            place = pl.ds(pl.multiple_of(at[BASE + k], quarter), quarter)
            w_ref[0, place] = jnp.concatenate(mats, axis=1)
        qkv = dot_nn(n1_ref[...], w_ref[0]).astype(bf16)
        qkv_ref[0] = qkv
        c_ref[...] = attend_pair(qkv[:, :128], qkv[:, 128:256], qkv[:, 256:], bias_ref, big_ref, rest_ref)

    first = 3 * chunk
    one = pl.BlockSpec((1, quarter, 128), lambda p, at: (0, 0, first + p))
    two = pl.BlockSpec((2, quarter, 128), lambda p, at: (0, 0, first + p))
    three = pl.BlockSpec((3, quarter, 128), lambda p, at: (0, 0, p))
    rows_spec = pl.BlockSpec((1, BUF, D), lambda p, at: (at[CORE], 0, 0)) if opening else whole(BUF, D)
    outs = [
        (shape((3, BUF, 384)), pl.BlockSpec((1, BUF, 384), lambda p, at: (p, 0, 0))),
        (shape((BUF, 384)), pl.BlockSpec((BUF, 128), lambda p, at: (0, p))),
        (shape((6, BIG, BIG)), pl.BlockSpec((2, BIG, BIG), lambda p, at: (p, 0, 0))),
        (shape((6, REST, REST)), pl.BlockSpec((2, REST, REST), lambda p, at: (p, 0, 0))),
        (shape((3, D, 384)), pl.BlockSpec((1, D, 384), lambda p, at: (p, 0, 0))),
    ]
    if opening:
        outs += [(shape((BUF, D)), whole(BUF, D))] * 2
    return call(
        kernel, (3,), scalars,
        [
            (rows, rows_spec), (gains, whole(5, D)),
            (bias, pl.BlockSpec((2, 3, WIDE), lambda p, at: (first + p, 0, 0))),
            (own[0], one), (own[1], two), (near[0], one), (near[1], two), (got, three), (got_near, three),
        ],
        outs, [pltpu.VMEM((BUF + REST, D), bf16)] if opening else (), 2 * 10**10,
    )


FTILE = 384


def feed_specs(index, count):
    own = pl.BlockSpec((1, FTILE, D), lambda i, at: (index, jnp.minimum(i, count - 1), 0))
    near = pl.BlockSpec((1, FTILE, D), lambda i, at: (index, jnp.maximum(i - count, 0), 0))
    return own, near


def enc_feed(scalars, xr, c_a, c_b, own_o, near_o, got, got_near, gains, feed_in, near_in, feed_out, near_out):
    quarter = got.shape[0]
    count = feed_in.shape[1] // FTILE

    def kernel(at, xr_ref, ca, cb, oo, no, go, gno, gain_ref, fi, ni, fo, nf, h1_ref, n2_ref, a_ref, s_ref, p_ref, wo_ref, total):
        step = pl.program_id(0)

        @pl.when(step == 0)
        def _():
            for k, piece in enumerate((oo[0], no[0], go[...], gno[...])):
                wo_ref[pl.ds(pl.multiple_of(at[BASE + k], quarter), quarter)] = piece
            context = jnp.concatenate([ca[...], cb[...]], axis=1)
            h1 = (xr_ref[...].astype(f32) + dot_nn(context, wo_ref[...])).astype(bf16)
            h1_ref[...] = h1
            n2_ref[...] = norm_rows(h1.astype(f32), gain_ref[1:2])
            total[...] = jnp.zeros_like(total)

        w_in = jnp.where(step < count, fi[0], ni[0])
        w_out = jnp.where(step < count, fo[0], nf[0])
        a, slope = gelu_both(dot_nt(n2_ref[...], w_in))
        a_ref[...] = a
        s_ref[...] = slope
        total[...] += dot_nn(a, w_out)

        @pl.when(step == 2 * count - 1)
        def _():
            p_ref[...] = total[...].astype(bf16)

    own, near = feed_specs(0, count)
    rows = whole(BUF, D)
    tile = pl.BlockSpec((BUF, FTILE), lambda i, at: (0, i))
    quarter_spec = pl.BlockSpec((1, quarter, D), lambda i, at: (0, 0, 0))
    return call(
        kernel, (2 * count,), scalars,
        [
            (xr, rows), (c_a, whole(BUF, 384)), (c_b, whole(BUF, 384)), (own_o, quarter_spec), (near_o, quarter_spec),
            (got, whole(quarter, D)), (got_near, whole(quarter, D)), (gains, whole(5, D)),
            (feed_in, own), (near_in, near), (feed_out, own), (near_out, near),
        ],
        [
            (shape((BUF, D)), rows), (shape((BUF, D)), rows), (shape((BUF, 2 * count * FTILE)), tile),
            (shape((BUF, 2 * count * FTILE)), tile), (shape((BUF, D)), rows), (shape((D, D)), whole(D, D)),
        ],
        [pltpu.VMEM((BUF, D), f32)], 2 * 10**10,
    )


GROUP = 4
GROUPS = HEADS // GROUP
CROSS_KEYS = ((0, BIG), (BIG, BIG + SMALL), (BIG + SMALL, BUF))
SELF_KEYS = tuple((i * TGT, (i + 1) * TGT) for i in range(QPB))


def own_head(value):
    row = lax.broadcasted_iota(jnp.int32, value.shape, 0) // TGT
    lane = lax.broadcasted_iota(jnp.int32, value.shape, 1) // HD
    return jnp.where(row == lane, value, jnp.zeros_like(value))


def spread_heads(rows):
    return own_head(jnp.concatenate([rows] * GROUP, axis=0))


def join_heads(value):
    value = own_head(value)
    return sum(value[h * TGT : (h + 1) * TGT] for h in range(GROUP))


def turned(value):
    return value.astype(f32).T.astype(bf16)


def small_attend(keys_of, q, k, v, p_ref, bias_ref=None):
    contexts = []
    for group in range(GROUPS):
        lanes = slice(GROUP * HD * group, GROUP * HD * (group + 1))
        rows = []
        for i, (first, last) in enumerate(keys_of):
            scores = dot_nt(k[first:last, lanes], spread_heads(q[i * TGT : (i + 1) * TGT, lanes]))
            if bias_ref is not None:
                scores = scores + bias_ref[group]
            weights = softmax_t(scores)
            p_ref[group, first:last] = weights
            rows.append(join_heads(dot_nn(turned(weights), v[first:last, lanes])))
        contexts.append(jnp.concatenate(rows, axis=0))
    return jnp.concatenate(contexts, axis=1).astype(bf16)


def small_attend_back(keys_of, q, k, v, grads, p_ref, bias_ref=None):
    dq, dk, dv = [], [], []
    for group in range(GROUPS):
        lanes = slice(GROUP * HD * group, GROUP * HD * (group + 1))
        dq_rows, dk_rows, dv_rows = [], [], []
        bias_grad = 0.0
        for i, (first, last) in enumerate(keys_of):
            own = slice(i * TGT, (i + 1) * TGT)
            queries, out_grads = spread_heads(q[own, lanes]), spread_heads(grads[own, lanes])
            weights = p_ref[group, first:last]
            grad_weights = dot_nt(v[first:last, lanes], out_grads)
            row_sum = jnp.sum(weights.astype(f32) * grad_weights, axis=0, keepdims=True)
            ds = score_grad(weights, grad_weights, row_sum)
            dv_rows.append(dot_nn(weights, out_grads))
            dk_rows.append(dot_nn(ds, queries))
            dq_rows.append(join_heads(dot_nn(turned(ds), k[first:last, lanes])))
            if bias_ref is not None:
                bias_grad = bias_grad + ds.astype(f32)
        if bias_ref is not None:
            bias_ref[group] = bias_grad
        for to, parts in ((dq, dq_rows), (dk, dk_rows), (dv, dv_rows)):
            to.append(jnp.concatenate(parts, axis=0).astype(bf16))
    return tuple(jnp.concatenate(parts, axis=1) for parts in (dq, dk, dv))


def by_owner(at, ref):
    return jnp.concatenate(
        [ref[0, pl.ds(pl.multiple_of(at[OWNER + i] * TGT, TGT), TGT)] for i in range(QPB)], axis=0
    )


def core_rows():
    return pl.BlockSpec((1, DEC, D), lambda i, at: (at[CORE], 0, 0))


ANYWHERE = pl.BlockSpec(memory_space=pl.ANY)


def weight_args(parts):
    return [(array, ANYWHERE) for array in parts]


def weight_copies(at, index, refs, w, sem):
    quarter = refs[0].shape[1]
    pieces, piece = refs[6].shape[0], refs[6].shape[2]
    copies = []

    def copy(source, target):
        copies.append(pltpu.make_async_copy(source, target, sem.at[len(copies)]))

    for k in range(2):
        place = pl.ds(pl.multiple_of(at[BASE + k], quarter), quarter)
        q, kv, o = refs[3 * k : 3 * k + 3]
        copy(q.at[index], w.at[0, place])
        copy(kv.at[pl.ds(2 * index, 2)], w.at[pl.ds(1, 2), place])
        copy(o.at[index], w.at[3, place])
    for k in range(2):
        for j in range(pieces):
            row = at[BASE + 2 + k] + at[PIECE + 4 * (index - 1) + j]
            copy(refs[6 + k].at[j], w.at[:, pl.ds(pl.multiple_of(row, piece), piece)])
    for one in copies:
        one.start()
    return copies


WEIGHT_SCRATCH = [pltpu.VMEM((4, D, D), bf16), pltpu.SemaphoreType.DMA((14,))]


def dec_self(scalars, decoder_in, gains, bias, self_w):
    def kernel(at, x_ref, gain_ref, bias_ref, *refs):
        xd_ref, n3_ref, q_ref, k_ref, v_ref, c_ref, p_ref, m_ref, n4_ref, w, sem = refs[8:]
        copies = weight_copies(at, 1, refs[:8], w, sem)
        xd = by_owner(at, x_ref)
        xd_ref[...] = xd
        n3 = norm_rows(xd.astype(f32), gain_ref[2:3])
        n3_ref[...] = n3
        for one in copies:
            one.wait()
        q, k, v = (dot_nn(n3, w[i]).astype(bf16) for i in range(3))
        q_ref[...], k_ref[...], v_ref[...] = q, k, v
        c = small_attend(SELF_KEYS, q, k, v, p_ref, bias_ref)
        c_ref[...] = c
        m = xd.astype(f32) + dot_nn(c, w[3])
        m_ref[...] = m
        n4_ref[...] = norm_rows(m, gain_ref[3:4])

    rows = whole(DEC, D)
    low = (shape((DEC, D)), rows)
    return call(
        kernel, (1,), scalars,
        [(decoder_in, core_rows()), (gains, whole(5, D)), (bias, whole(GROUPS, TGT, GROUP * TGT))] + weight_args(self_w),
        [low] * 6 + [(shape((GROUPS, DEC, 128)), whole(GROUPS, DEC, 128)), (shape((DEC, D), f32), rows), low],
        WEIGHT_SCRATCH, 10**8,
    )


def dec_cross(scalars, h1, part, other, m, n4, cross_w, gains, cotangent, feed_in, near_in, feed_out, near_out):
    hidden = feed_in.shape[1]

    def kernel(
        at, h1_ref, p0, p1, m_ref, n4_ref, gain_ref, cot_ref, fi, ni, fo, nf, *refs
    ):
        e_ref, q_ref, k_ref, v_ref, c_ref, p_ref, g_ref, n5_ref, cot_out, a_ref, du_ref, dn_ref, o_ref = refs[8:21]
        w, w_sem, w_in, w_out, sem = refs[21:]
        first = weight_copies(at, 2, refs[:8], w, w_sem)
        copies = []
        for k, (own, near, to) in enumerate(((fi, ni, w_in), (fo, nf, w_out))):
            copies.append(pltpu.make_async_copy(own.at[1], to.at[pl.ds(0, hidden)], sem.at[2 * k]))
            copies.append(pltpu.make_async_copy(near.at[1], to.at[pl.ds(hidden, hidden)], sem.at[1 + 2 * k]))
        for copy in copies:
            copy.start()
        cot = by_owner(at, cot_ref)
        cot_out[...] = cot
        e = (h1_ref[...].astype(f32) + (p0[...].astype(f32) + p1[...].astype(f32))).astype(bf16)
        e_ref[...] = e
        for one in first:
            one.wait()
        k = dot_nn(e, w[1]).astype(bf16)
        v = dot_nn(e, w[2]).astype(bf16)
        q = dot_nn(n4_ref[...], w[0]).astype(bf16)
        q_ref[...], k_ref[...], v_ref[...] = q, k, v
        c = small_attend(CROSS_KEYS, q, k, v, p_ref)
        c_ref[...] = c
        g = (m_ref[...] + dot_nn(c, w[3])).astype(bf16)
        g_ref[...] = g
        n5 = norm_rows(g.astype(f32), gain_ref[4:5])
        n5_ref[...] = n5
        copies[0].wait()
        copies[1].wait()
        a, slope = gelu_both(dot_nt(n5, w_in[...]))
        a_ref[...] = a
        copies[2].wait()
        copies[3].wait()
        du = (slope.astype(f32) * dot_nt(cot, w_out[...])).astype(bf16)
        du_ref[...] = du
        dn_ref[...] = dot_nn(du, w_in[...]).astype(bf16)
        o_ref[...] = dot_nn(a, w_out[...]).astype(bf16)

    rows, small = whole(BUF, D), whole(DEC, D)
    big_low, low = (shape((BUF, D)), rows), (shape((DEC, D)), small)
    wide = (shape((DEC, 2 * hidden)), whole(DEC, 2 * hidden))
    return call(
        kernel, (1,), scalars,
        [
            (h1, rows), (part, rows), (other, rows), (m, small), (n4, small),
            (gains, whole(5, D)), (cotangent, core_rows()),
            (feed_in, ANYWHERE), (near_in, ANYWHERE), (feed_out, ANYWHERE), (near_out, ANYWHERE),
        ]
        + weight_args(cross_w),
        [
            big_low, low, big_low, big_low, low, (shape((GROUPS, BUF, 128)), whole(GROUPS, BUF, 128)),
            low, low, low, wide, wide, low, low,
        ],
        WEIGHT_SCRATCH
        + [
            pltpu.VMEM((2 * hidden, D), bf16), pltpu.VMEM((2 * hidden, D), bf16), pltpu.SemaphoreType.DMA((4,)),
        ],
        2 * 10**10,
    )


def feed_weights(scalars, lefts, right_rows, hidden):
    count = hidden // FTILE
    pairs = len(lefts)
    rows = lefts[0].shape[0]

    def kernel(at, *refs):
        step = pl.program_id(0)
        ins, outs = refs[: 2 * pairs], refs[2 * pairs :]
        for keep, to in ((step < count, outs[:pairs]), (step >= count, outs[pairs:])):

            @pl.when(keep)
            def _(to=to):
                for k in range(pairs):
                    to[k][...] = dot_nn(transposed(ins[2 * k][...]), ins[2 * k + 1][...]).astype(bf16)

    tile = pl.BlockSpec((rows, FTILE), lambda i, at: (0, i))
    ins = []
    for left, right in zip(lefts, right_rows):
        ins += [(left, tile), (right, whole(rows, D))]
    kind = shape((hidden, D))
    own = (kind, pl.BlockSpec((FTILE, D), lambda i, at: (jnp.minimum(i, count - 1), 0)))
    other = (kind, pl.BlockSpec((FTILE, D), lambda i, at: (jnp.maximum(i - count, 0), 0)))
    return call(
        kernel, (2 * count,), scalars, ins, [own] * pairs + [other] * pairs,
        flops=10**10,
    )


def cross_back(scalars, g, gains, p0, p1, cot, cross_w, q, k, v, weights, m):
    def kernel(
        at, g_ref, gain_ref, p0_ref, p1_ref, cot_ref, q_ref, k_ref, v_ref, p_ref, m_ref, *refs
    ):
        dg_ref, dq_ref, dk_ref, dv_ref, de_ref, gain_out, dm_ref, w, sem = refs[8:]
        copies = weight_copies(at, 2, refs[:8], w, sem)
        dn5 = p0_ref[...].astype(f32) + p1_ref[...].astype(f32)
        dg_rows, gain4 = norm_back(g_ref[...].astype(f32), gain_ref[4:5], dn5)
        dg = (dg_rows + cot_ref[...].astype(f32)).astype(bf16)
        dg_ref[...] = dg
        for one in copies:
            one.wait()
        dc = dot_nt(dg, w[3]).astype(bf16)
        dq, dk, dv = small_attend_back(CROSS_KEYS, q_ref[...], k_ref[...], v_ref[...], dc, p_ref)
        dq_ref[...], dk_ref[...], dv_ref[...] = dq, dk, dv
        de_ref[...] = (dot_nt(dk, w[1]) + dot_nt(dv, w[2])).astype(bf16)
        dm_rows, gain3 = norm_back(m_ref[...], gain_ref[3:4], dot_nt(dq, w[0]))
        dm_ref[...] = dm_rows + dg.astype(f32)
        gain_out[...] = jnp.concatenate([gain3, gain4], axis=0)

    rows, small = whole(BUF, D), whole(DEC, D)
    big_low, low = (shape((BUF, D)), rows), (shape((DEC, D)), small)
    return call(
        kernel, (1,), scalars,
        [
            (g, small), (gains, whole(5, D)), (p0, small), (p1, small), (cot, small),
            (q, small), (k, rows), (v, rows), (weights, whole(GROUPS, BUF, 128)), (m, small),
        ]
        + weight_args(cross_w),
        [low, low, big_low, big_low, big_low, (shape((2, D), f32), whole(2, D)), (shape((DEC, D), f32), small)],
        WEIGHT_SCRATCH,
        2 * 10**10,
    )


def enc_feed_back(scalars, de, slope, feed_in, near_in, feed_out, near_out):
    count = feed_in.shape[1] // FTILE

    def kernel(at, de_ref, s_ref, fi, ni, fo, nf, du_ref, p_ref, total):
        step = pl.program_id(0)
        w_in = jnp.where(step < count, fi[0], ni[0])
        w_out = jnp.where(step < count, fo[0], nf[0])
        du = (s_ref[...].astype(f32) * dot_nt(de_ref[...], w_out)).astype(bf16)
        du_ref[...] = du
        grad = dot_nn(du, w_in)

        @pl.when(step == 0)
        def _():
            total[...] = grad

        @pl.when(step > 0)
        def _():
            total[...] += grad

        @pl.when(step == 2 * count - 1)
        def _():
            p_ref[...] = total[...].astype(bf16)

    own, near = feed_specs(0, count)
    tile = pl.BlockSpec((BUF, FTILE), lambda i, at: (0, i))
    return call(
        kernel, (2 * count,), scalars,
        [(de, whole(BUF, D)), (slope, tile), (feed_in, own), (near_in, near), (feed_out, own), (near_out, near)],
        [(shape(slope.shape), tile), (shape((BUF, D)), whole(BUF, D))],
        [pltpu.VMEM((BUF, D), f32)], 2 * 10**10,
    )


def chip_cols(at, ref):
    return ref[:, pl.ds(pl.multiple_of(at[ACROSS] * BIG, 128), BIG)]


def store_rows(at, grads, own_ref, other_ref):
    first = at[CORE] == 0
    for i, grad in enumerate(grads):
        low = grad.astype(bf16)
        half = low.shape[0] // 2
        own_ref[i] = jnp.where(first, low[:half], low[half:])
        other_ref[i] = jnp.where(first, low[half:], low[:half])


def quarter_outs(mats):
    kind = (shape((mats, BIG // 2, D)), whole(mats, BIG // 2, D))
    return [kind, kind]


def cross_weights(scalars, n4, dq, e, dk, dv, c, dg):
    def kernel(at, n4_ref, dq_ref, e_ref, dk_ref, dv_ref, c_ref, dg_ref, own_ref, other_ref):
        n4_t, e_t, c_t = (transposed(chip_cols(at, ref)) for ref in (n4_ref, e_ref, c_ref))
        pairs = ((n4_t, dq_ref), (e_t, dk_ref), (e_t, dv_ref), (c_t, dg_ref))
        store_rows(at, [dot_nn(left, right[...]) for left, right in pairs], own_ref, other_ref)

    rows, small = whole(BUF, D), whole(DEC, D)
    return call(
        kernel, (1,), scalars,
        [(n4, small), (dq, small), (e, rows), (dk, rows), (dv, rows), (c, small), (dg, small)],
        quarter_outs(4),
    )


def self_back(scalars, dm, gains, self_w, q, k, v, c, weights, xd, n3):
    def kernel(at, dm_ref, gain_ref, q_ref, k_ref, v_ref, c_ref, p_ref, xd_ref, n3_ref, *refs):
        own_ref, other_ref, grad_ref, gain_out, diag_ref, w, sem = refs[8:]
        copies = weight_copies(at, 1, refs[:8], w, sem)
        dm = dm_ref[...]
        low = dm.astype(bf16)
        for one in copies:
            one.wait()
        dc = dot_nt(low, w[3]).astype(bf16)
        dq, dk, dv = small_attend_back(SELF_KEYS, q_ref[...], k_ref[...], v_ref[...], dc, p_ref, diag_ref)
        dn3 = dot_nt(dq, w[0]) + dot_nt(dk, w[1]) + dot_nt(dv, w[2])
        dd, gain2 = norm_back(xd_ref[...].astype(f32), gain_ref[2:3], dn3)
        gain_out[...] = gain2
        grad = (dd + dm).astype(bf16)
        for i in range(QPB):
            grad_ref[pl.ds(pl.multiple_of(at[OWNER + i] * TGT, TGT), TGT)] = grad[i * TGT : (i + 1) * TGT]
        n3_t, c_t = transposed(chip_cols(at, n3_ref)), transposed(chip_cols(at, c_ref))
        store_rows(at, [dot_nn(n3_t, dq), dot_nn(n3_t, dk), dot_nn(n3_t, dv), dot_nn(c_t, low)], own_ref, other_ref)

    small = whole(DEC, D)
    return call(
        kernel, (1,), scalars,
        [
            (dm, small), (gains, whole(5, D)),
            (q, small), (k, small), (v, small), (c, small), (weights, whole(GROUPS, DEC, 128)), (xd, small), (n3, small),
        ]
        + weight_args(self_w),
        quarter_outs(4)
        + [
            (shape((DEC, D)), small), (shape((1, D), f32), whole(1, D)),
            (shape((GROUPS, TGT, 128), f32), whole(GROUPS, TGT, 128)),
        ],
        WEIGHT_SCRATCH, 10**9,
    )


def enc_back(scalars, opening, gains, xr, chunk, chunk_c, n1=None, start=None, carried=None):
    half = BIG // 2
    first = 0 if opening else 3

    def kernel(at, gain_ref, xr_ref, wo_ref, ca_ref, cb_ref, qkv_ref, c_ref, big_ref, rest_ref, w_ref, *refs):
        if opening:
            h1_ref, p0_ref, p1_ref, de_ref, n1_ref = refs[:5]
            own_ref, other_ref, diag_ref, rdiag_ref, dh1_ref, dn1_ref, n1_t, c_t, gain_out = refs[5:]
        else:
            dh1_ref, dn1_in, n1_t, c_t = refs[:4]
            own_ref, other_ref, diag_ref, rdiag_ref, grad_ref, gain_out, dn1_ref, twice = refs[6:]
        p = pl.program_id(0)

        @pl.when(p == 0)
        def _():
            if opening:
                dn2 = p0_ref[...].astype(f32) + p1_ref[...].astype(f32)
                dh1_rows, gain1 = norm_back(h1_ref[...].astype(f32), gain_ref[1:2], dn2)
                dh1_ref[...] = (dh1_rows + de_ref[...].astype(f32)).astype(bf16)
                gain_out[...] = gain1
                n1_t[...] = chip_cols(at, n1_ref).T
                c_t[...] = jnp.where(at[ACROSS] == 0, ca_ref[...], cb_ref[...]).T
                dn1_ref[...] = jnp.zeros_like(dn1_ref)
            else:
                dn1_ref[...] = dn1_in[...]

        qkv, c, w = qkv_ref[0], c_ref[...], w_ref[0]
        q, k, v = qkv[:, :128], qkv[:, 128:256], qkv[:, 256:]
        dh1 = dh1_ref[...]
        grads = dot_nt(dh1, wo_ref[...]).astype(bf16)
        keys_t = k.T
        product_t = (grads.astype(f32) * c.astype(f32)).T
        dq_t = []
        dk_big = dv_big = dk_rest = dv_rest = 0.0
        for hh in range(2):
            row_sum = jnp.sum(product_t[hh * HD : (hh + 1) * HD], axis=0, keepdims=True)
            queries, values, grads_h = lane_half(q, hh), lane_half(v, hh), lane_half(grads, hh)
            head_k = keys_t[hh * HD : (hh + 1) * HD]
            weights = big_ref[hh]
            ds = score_grad(weights, dot_nt(values[:BIG], grads[:BIG]), row_sum[:, :BIG])
            dv_big = dv_big + dot_nn(weights, grads_h[:BIG])
            dk_big = dk_big + dot_nn(ds, queries[:BIG])
            diag_ref[hh] = jnp.concatenate(
                [diagonals(ds[128 * b : 128 * (b + 1)], WIDE) for b in range(3)], axis=0
            )
            dq_head = dot_nn(head_k[:, :BIG], ds)
            weights = rest_ref[hh]
            ds = score_grad(weights, dot_nt(values[BIG:], grads[BIG:]), row_sum[:, BIG:])
            dv_rest = dv_rest + dot_nn(weights, grads_h[BIG:])
            dk_rest = dk_rest + dot_nn(ds, queries[BIG:])
            rdiag_ref[hh] = diagonals(ds, 2 * REST)
            dq_t.append(jnp.concatenate([dq_head, dot_nn(head_k[:, BIG:], ds)], axis=1))
        dq = jnp.concatenate(dq_t, axis=0).T.astype(bf16)
        dk = jnp.concatenate([dk_big, dk_rest], axis=0).astype(bf16)
        dv = jnp.concatenate([dv_big, dv_rest], axis=0).astype(bf16)
        dqkv = jnp.concatenate([dq, dk, dv], axis=1)
        dn1_ref[...] += dot_nt(dqkv, w)
        grad = dot_nn(n1_t[...], dqkv)
        columns = pl.ds(pl.multiple_of(128 * (first + p), 128), 128)
        out_grad = dot_nn(c_t[...], dh1_ref[:, columns])
        store_rows(at, [grad[:, 128 * i : 128 * i + 128] for i in range(3)] + [out_grad], own_ref, other_ref)

        if not opening:

            @pl.when(p == 2)
            def _():
                rows, gain0 = norm_back(xr_ref[...].astype(f32), gain_ref[0:1], dn1_ref[...])
                gain_out[...] = gain0
                low = (rows + dh1.astype(f32)).astype(bf16)
                twice[:BUF] = low
                twice[BUF:] = low
                grad_ref[...] = twice[pl.ds(pl.multiple_of(BUF - at[START], SMALL), BUF)]

    rows = whole(BUF, D)
    wo = start[4] if opening else carried[-1]
    qkv, c, big, rest, w = chunk
    ins = [
        (gains, whole(5, D)), (xr, rows), (wo, pl.BlockSpec((128, D), lambda p, at: (first + p, 0))),
        (chunk_c[0], whole(BUF, BIG)), (chunk_c[1], whole(BUF, BIG)),
        (qkv, pl.BlockSpec((1, BUF, BIG), lambda p, at: (p, 0, 0))),
        (c, pl.BlockSpec((BUF, 128), lambda p, at: (0, p))),
        (big, pl.BlockSpec((2, BIG, BIG), lambda p, at: (p, 0, 0))),
        (rest, pl.BlockSpec((2, REST, REST), lambda p, at: (p, 0, 0))),
        (w, pl.BlockSpec((1, D, BIG), lambda p, at: (p, 0, 0))),
    ]
    columns = (shape((4, half, D)), pl.BlockSpec((4, half, 128), lambda p, at: (0, 0, first + p)))
    outs = [
        columns, columns,
        (shape((6, 3, WIDE), f32), pl.BlockSpec((2, 3, WIDE), lambda p, at: (p, 0, 0))),
        (shape((6, 1, 2 * REST), f32), pl.BlockSpec((2, 1, 2 * REST), lambda p, at: (p, 0, 0))),
    ]
    low, turned = (shape((BUF, D)), rows), (shape((BIG, BUF)), whole(BIG, BUF))
    one = (shape((1, D), f32), whole(1, D))
    scratch, aliases = (), {}
    if opening:
        ins += [(value, rows) for value in start[:4]] + [(n1, rows)]
        outs += [low, (shape((BUF, D), f32), rows), turned, turned, one]
    else:
        own, other, dh1, dn1, n1_t, c_t, _ = carried
        ins += [(dh1, rows), (dn1, rows), (n1_t, whole(BIG, BUF)), (c_t, whole(BIG, BUF)), (own, ANYWHERE), (other, ANYWHERE)]
        aliases = {len(ins) - 1: 0, len(ins): 1}
        outs += [low, one]
        scratch = [pltpu.VMEM((BUF, D), f32), pltpu.VMEM((2 * BUF, D), bf16)]
    return call(kernel, (3,), scalars, ins, outs, scratch, 2 * 10**10, aliases)


def swap_section(value, bit):
    count = lax.axis_size("section")
    return lax.ppermute(value, "section", [(i, i ^ bit) for i in range(count)])


def swap_dp(value, bit):
    count = lax.axis_size("dp")
    return lax.ppermute(value, "dp", [(i, i ^ bit) for i in range(count)])


def add_low(a, b):
    return (a.astype(f32) + b.astype(f32)).astype(bf16)


def tie(value, *deps):
    return lax.optimization_barrier((value,) + deps)[0] if deps else value


def halves(own, got, extra=None):
    half = own.shape[0] // 2
    mine = lax.axis_index("dp") % 2

    def part(which):
        rows = [lax.dynamic_slice_in_dim(value, which * half, half, 0) for value in (own, got)]
        total = add_low(*rows)
        return total if extra is None else jnp.concatenate([total, extra])

    return part(mine), part(1 - mine)


def rejoin(keep, other):
    mine = lax.axis_index("dp") % 2
    keep = keep[: other.shape[0]]
    return jnp.where(mine == 0, jnp.concatenate([keep, other]), jnp.concatenate([other, keep]))


Y_TIME, TREE_TIME, STEP = 12.7, 12.7, 3.0
STAGES = (("y", Y_TIME), ("in", TREE_TIME), ("mid", TREE_TIME), ("out", TREE_TIME), ("y", Y_TIME))
ROUTES = {
    "y": tuple((i, i ^ 1) for i in range(8)),
    "in": ((0, 2), (1, 3), (6, 4), (7, 5)),
    "mid": ((2, 4), (3, 5), (4, 2), (5, 3)),
    "out": ((2, 0), (3, 1), (4, 6), (5, 7)),
}


class GradSum:
    def __init__(self, pieces):
        self.count = lax.axis_size("dp")
        self.value = {}
        self.extra = None
        self.stage = {i: 0 for i in pieces}
        self.links = {name: [] for name in ROUTES}
        self.sent, self.got = {}, {}

    def enter(self, i, own, got, extra=None):
        own, got = own.reshape(-1, D), got.reshape(-1, D)
        if self.count != 8:
            self.value[i] = lax.psum(add_low(own, got), "dp")
            self.extra = None if extra is None else lax.psum(extra, "dp")
        else:
            self.value[i] = (own, got, extra)

    def step(self, i, *after):
        now = self.stage[i]
        self.stage[i] = now + 1
        if self.count != 8:
            return
        link = STAGES[now][0]
        value = self.value[i]
        if now > 0:
            value = tie(value, *after)
        if now == 0:
            value, sent = halves(*(tie(value[0], *after), tie(value[1], *after), value[2]))
        elif now == 4:
            sent = value[: value.shape[0] // 128 * 128]
            if sent.shape != value.shape:
                self.extra = value[sent.shape[0] :]
        else:
            sent = value
        before = self.links[link]
        sent = tie(sent, *before[-2:-1])
        got = lax.ppermute(sent, "dp", ROUTES[link])
        before.append(got)
        z = lax.axis_index("dp") // 2
        if now < 3:
            value = add_low(value, got)
        elif now == 3:
            value = jnp.where((z == 0) | (z == 3), got, value)
        else:
            value = rejoin(value, got)
        self.value[i], self.sent[i, now], self.got[i, now] = value, sent, got

    def between(self, after, ended, begun):
        for i in begun:
            self.step(i, after)
        if self.count != 8:
            return []
        return [self.got[key] for key in ended] + [self.sent[i, self.stage[i] - 1] for i in begun]

    def finish(self, late):
        free = {name: 0.0 for name in ROUTES}
        at = {i: late.get(i, 0.0) for i in self.stage}
        while min(self.stage.values()) < len(STAGES):
            best = None
            for i, now in self.stage.items():
                if now < len(STAGES):
                    key = (max(at[i], free[STAGES[now][0]]), now - len(STAGES), i)
                    best = key if best is None else min(best, key)
            begin, _, i = best
            link, length = STAGES[self.stage[i]]
            free[link], at[i] = begin + length + 0.5, begin + length + STEP
            self.step(i)
        return self.value


def shards(
    encoder_in, decoder_in, lengths, query_map, attn_query, attn_keyval, attn_output,
    feed_in, feed_out, norm_gains, position_bias, cotangent,
):
    section_id = lax.axis_index("section")
    across = section_id // 2
    core = section_id % 2
    quarter = attn_query.shape[1]
    half = 2 * quarter

    dp_id = lax.axis_index("dp")
    own = (attn_query, attn_keyval, attn_output)
    near = tuple(swap_section(a, 1) for a in own)
    hidden = feed_in.shape[1]

    def packed(index, mats, first, last, *after):
        parts = [tie(attn_query[index : index + 1], *after), attn_keyval[2 * index : 2 * index + 2], attn_output[index : index + 1]]
        return jnp.concatenate(parts[: mats - 1], axis=0)[:, :, first:last]

    bases = [(section_id ^ k) * quarter for k in range(4)]
    def piece_of(index, count, *after):
        size = quarter // count
        piece = lax.dynamic_slice_in_dim(packed(index, 4, 0, D), (dp_id % count) * size, size, 1)
        return swap_section(tie(piece, *after), 2)

    def places(count):
        at = dp_id % count
        return [(at ^ k) * (quarter // count) if k < count else 0 for k in range(4)]

    pack_a = packed(0, 3, 0, D // 2)
    got_a = swap_section(pack_a, 2)

    big = jnp.argmax(lengths[core]).astype(jnp.int32)
    owners = lax.dynamic_slice_in_dim(jnp.concatenate([query_map[core]] * 2), big, QPB, 0)
    scalars = jnp.concatenate(
        [jnp.stack([core, across, big * SMALL]), owners, jnp.stack(bases + places(4) + places(2))]
    ).astype(jnp.int32)

    enc_table = spread_table(position_bias[0], encoder_bucket(enc_offsets()))
    causal = jnp.asarray(dec_offsets() <= 0)
    dec_table = jnp.where(causal, spread_table(position_bias[1], decoder_bucket(dec_offsets())), masked_score)
    dec_table = jnp.transpose(dec_table.reshape(GROUPS, GROUP, TGT, TGT), (0, 2, 1, 3)).reshape(GROUPS, TGT, GROUP * TGT)
    sums = GradSum(range(7))

    near_a = swap_section(tie(got_a, scalars, enc_table, dec_table), 1)
    got_b = swap_section(packed(0, 3, D // 2, D, pack_a), 2)
    got_self = piece_of(1, 4, near_a)
    first = enc_attention(scalars, encoder_in, norm_gains, enc_table, own, near, got_a, near_a, 0)
    n1, xr = first[5:]
    got_o = swap_section(tie(attn_output[0], near_a), 2)
    near_b = swap_section(tie(got_b, n1), 1)
    got_cross = piece_of(2, 2, n1)
    piece = tie(got_self, n1)
    second_piece, third_piece = swap_dp(piece, 1), swap_dp(piece, 2)
    near_in = swap_section(tie(feed_in, near_a), 1)
    near_out = swap_section(tie(feed_out, near_a), 1)
    second = enc_attention(scalars, n1, norm_gains, enc_table, own, near, got_b, near_b, 1)
    near_got_o = swap_section(tie(got_o, second[1]), 1)
    fourth_piece = swap_dp(tie(second_piece, second[1]), 2)
    quad = jnp.stack([piece, second_piece, third_piece, fourth_piece])
    h1, n2, a1, slope1, part, wo = enc_feed(
        scalars, xr, first[1], second[1], attn_output, near[2], got_o, near_got_o, norm_gains,
        feed_in, near_in, feed_out, near_out,
    )
    part_other = swap_section(part, 2)
    quad = tie(quad, part)
    self_w = own + near + (quad, swap_section(quad, 1))
    pair = tie(got_cross, second[1])
    pair = tie(jnp.stack([pair, swap_dp(pair, 1)]), part)
    cross_w = own + near + (pair, swap_section(pair, 1))
    xd, n3, q2, k2, v2, c2, p2, m, n4 = dec_self(scalars, decoder_in, norm_gains, dec_table, self_w)
    e, q3, k3, v3, c3, p3, g, n5, cot, a2, du2, dn5, out_part = dec_cross(
        scalars, h1, part, part_other, m, n4, cross_w, norm_gains, cotangent, feed_in, near_in, feed_out, near_out
    )

    dn5_other = swap_section(dn5, 2)
    own_out, own_in, other_out, other_in = feed_weights(scalars, (a2, du2), (cot, n5), hidden)
    sums.enter(0, own_out, swap_section(other_out, 1))
    sums.enter(1, own_in, swap_section(other_in, 1))

    dn5_other = tie(dn5_other, *sums.between(own_in, (), (0,)))
    dg, dq3, dk3, dv3, de, gains34, dm = cross_back(
        scalars, g, norm_gains, dn5, dn5_other, cot, cross_w, q3, k3, v3, p3, m
    )
    de = tie(de, *sums.between(dq3, (), (1,)))
    du1, dn2 = enc_feed_back(scalars, de, slope1, feed_in, near_in, feed_out, near_out)
    dn2_other = swap_section(dn2, 2)
    own_w, other_w = cross_weights(scalars, n4, dq3, e, dk3, dv3, c3, tie(dg, dn2))
    sums.enter(2, own_w, swap_section(other_w, 1))

    dm = tie(dm, own_w, *sums.between(own_w, (), (0,)))
    own_w, other_w, dec_grad, gain2, diag2 = self_back(scalars, dm, norm_gains, self_w, q2, k2, v2, c2, p2, xd, n3)
    sums.enter(5, own_w, swap_section(other_w, 1))

    n2_late = tie(n2, own_w, dn2_other, *sums.between(dec_grad, (), (1, 2)))
    own_out, own_in, other_out, other_in = feed_weights(scalars, (a1, du1), (de, n2_late), hidden)
    sums.enter(3, own_out, swap_section(other_out, 1))
    sums.enter(4, own_in, swap_section(other_in, 1))

    dn2_late = tie(dn2_other, own_in, *sums.between(own_in, (), (5, 0)))
    contexts = (first[1], second[1])
    own_w, other_w, diag_a, rdiag_a, dh1, dn1, n1_t, c_t, gain1 = enc_back(
        scalars, True, norm_gains, xr, first[:5], contexts, n1, (h1, dn2, dn2_late, de, wo)
    )
    dn1 = tie(dn1, *sums.between(dh1, (), (3, 1)))
    own_enc, other_w, diag_b, rdiag_b, enc_grad, gain0 = enc_back(
        scalars, False, norm_gains, xr, second[:5], contexts, carried=(own_w, other_w, dh1, dn1, n1_t, c_t, wo)
    )
    got_w = swap_section(other_w, 1)

    hot_enc = jnp.asarray(
        np.concatenate(
            [one_hot(encoder_bucket(128 * b + diagonal_offsets(128, WIDE))) for b in range(3)]
            + [one_hot(encoder_bucket(diagonal_offsets(REST, 2 * REST)))]
        )
    )
    hot_dec = jnp.asarray(one_hot(decoder_bucket(dec_offsets())))
    sums_enc = jnp.concatenate(
        [
            jnp.concatenate([d.reshape(HEADS // 2, -1), r.reshape(HEADS // 2, -1)], axis=1)
            for d, r in ((diag_a, rdiag_a), (diag_b, rdiag_b))
        ]
    )
    exact = lax.Precision.HIGHEST
    table_enc = jnp.einsum("mb,hm->bh", hot_enc, sums_enc, precision=exact)
    diag2 = diag2.reshape(GROUPS, TGT, GROUP, TGT)
    table_dec = jnp.einsum("kqb,gkhq->bgh", hot_dec, diag2, precision=exact).reshape(NB, HEADS)
    tables = jnp.stack([table_enc, table_dec]).reshape(-1, D)
    small = jnp.concatenate([gain0, gain1, gain2, gains34, tables, jnp.zeros((10, D), f32)])
    small = small + swap_section(small, 1)
    sums.enter(6, own_enc, got_w, small.astype(bf16))
    total = sums.finish({6: 6.0})
    unit_out2, unit_in2, unit_cross, unit_out1, unit_in1, unit_self, unit_enc = (total[i] for i in range(7))
    small = sums.extra.astype(f32)
    gains = small[:5]
    tables = small[5].reshape(2, NB, HEADS)

    def split_rows(rows, count):
        mine = lax.dynamic_slice_in_dim(rows, section_id * count, count, 0)
        theirs = swap_section(lax.dynamic_slice_in_dim(rows, (section_id ^ 1) * count, count, 0), 1)
        return jnp.where(core == 0, jnp.stack([mine, theirs]), jnp.stack([theirs, mine]))

    out_rows = (g.astype(f32) + (out_part.astype(f32) + swap_section(out_part, 2).astype(f32))).astype(bf16)
    restored = jnp.zeros((DEC, D), bf16)
    for i in range(QPB):
        restored = lax.dynamic_update_slice_in_dim(restored, out_rows[i * TGT : (i + 1) * TGT], owners[i] * TGT, 0)
    sections = lax.axis_size("section")
    decoder_out = split_rows(restored, DEC // sections)
    decoder_in_grad = split_rows(dec_grad, DEC // sections)
    encoder_in_grad = split_rows(enc_grad, BUF // sections)

    u_enc, u_self, u_cross = (
        u.reshape(4, quarter, D).astype(f32) for u in (unit_enc, unit_self, unit_cross)
    )
    query_grad = jnp.stack([u_enc[0], u_self[0], u_cross[0]])
    keyval_grad = jnp.concatenate([u_enc[1:3], u_self[1:3], u_cross[1:3]])
    output_grad = jnp.stack([u_enc[3], u_self[3], u_cross[3]])
    feed_in_grad = jnp.stack([unit_in1, unit_in2]).astype(f32)
    feed_out_grad = jnp.stack([unit_out1, unit_out2]).astype(f32)
    return (
        decoder_out, encoder_in_grad, decoder_in_grad, query_grad, keyval_grad, output_grad,
        feed_in_grad, feed_out_grad, gains, tables,
    )


def solution(mesh):
    rows = P("dp", None, None)
    mats = P(None, "section", None)
    outs = P("dp", "section", None)
    return jax.shard_map(
        shards,
        mesh=mesh,
        in_specs=(rows, rows, P("dp", None), P("dp", None), mats, mats, mats, mats, mats, P(), P(), rows),
        out_specs=(outs, outs, outs, mats, mats, mats, mats, mats, P(), P()),
        check_vma=False,
    )
```

```python
import functools

import jax
import jax.numpy as jnp
import numpy as np
from jax import lax
from jax.experimental import pallas as pl
from jax.experimental.pallas import tpu as pltpu
from jax.sharding import PartitionSpec as P

D = 768
HEADS = 12
HD = 64
PAIRS = HEADS // 2
NB = 32
BUF = 512
BIG = 384
SMALL = 64
REST = BUF - BIG
QPB = 3
TGT = 32
DEC = QPB * TGT
WIDE = 512
epsilon = 1e-06
masked_score = -1e30
enc_edges = (12, 16, 23, 32, 46, 64, 91)
dec_edges = (19, 21, 24, 27, 31)
bf16 = jnp.bfloat16
f32 = jnp.float32


def dot_nn(a, b):
    return lax.dot_general(a, b, (((1,), (0,)), ((), ())), preferred_element_type=f32)


def dot_nt(a, b):
    return lax.dot_general(a, b, (((1,), (1,)), ((), ())), preferred_element_type=f32)


def dot_tn(a, b):
    return lax.dot_general(a, b, (((0,), (0,)), ((), ())), preferred_element_type=f32)


def encoder_bucket(offset):
    distance = np.abs(offset)
    bucket = np.minimum(distance, 8)
    for boundary in enc_edges:
        bucket = bucket + (distance >= boundary)
    return bucket + 16 * (offset > 0)


def decoder_bucket(offset):
    distance = np.maximum(-offset, 0)
    bucket = np.minimum(distance, 16)
    for boundary in dec_edges:
        bucket = bucket + (distance >= boundary)
    return bucket


def enc_offsets():
    lane = np.arange(WIDE)
    shifted = np.where(lane < BIG, lane, lane - WIDE)
    return 128 * np.arange(3)[:, None] - shifted[None, :]


def diagonal_offsets(rows, width):
    return rows - 1 - np.arange(width)


def dec_offsets():
    return np.arange(TGT)[:, None] - np.arange(TGT)[None, :]


def one_hot(bucket):
    return (bucket[..., None] == np.arange(NB)).astype(np.float32)


def spread_table(table, bucket):
    hot = jnp.asarray(one_hot(bucket))
    return jnp.sum(hot[None] * jnp.transpose(table).reshape((HEADS,) + (1,) * bucket.ndim + (NB,)), axis=-1)


def norm_scale(rows):
    return lax.rsqrt(jnp.mean(rows * rows, axis=-1, keepdims=True) + epsilon)


def norm_rows(rows, gain):
    return (rows * norm_scale(rows) * gain).astype(bf16)


def norm_back(rows, gain, grad):
    scale = norm_scale(rows)
    unit = rows * scale
    weighted = grad * gain
    grad_rows = scale * (weighted - unit * jnp.mean(weighted * unit, axis=-1, keepdims=True))
    return grad_rows, jnp.sum(grad * unit, axis=0, keepdims=True)


def gelu_both(u):
    root = np.float32(np.sqrt(2.0 / np.pi))
    cubic = np.float32(0.044715)
    square = u * u
    bend = jnp.tanh(u * (root + root * cubic * square))
    half = 0.5 * (1.0 + bend)
    slope = half + 0.5 * u * (1.0 - bend * bend) * (root + 3.0 * root * cubic * square)
    return (u * half).astype(bf16), slope.astype(bf16)


CORE, ACROSS, START, OWNER, BASE, PIECE = 0, 1, 2, 3, 6, 10


def shape(dims, dtype=bf16):
    return jax.ShapeDtypeStruct(dims, dtype)


def whole(*dims):
    return pl.BlockSpec(dims, lambda *_: (0,) * len(dims))


def call(kernel, grid, scalars, ins, outs, scratch=(), flops=10**10, aliases=None):
    return pl.pallas_call(
        kernel,
        grid_spec=pltpu.PrefetchScalarGridSpec(
            num_scalar_prefetch=1,
            grid=grid,
            in_specs=[spec for _, spec in ins],
            out_specs=tuple(spec for _, spec in outs),
            scratch_shapes=scratch,
        ),
        out_shape=tuple(kind for kind, _ in outs),
        input_output_aliases=aliases or {},
        compiler_params=pltpu.CompilerParams(vmem_limit_bytes=25 << 20),
        cost_estimate=pl.CostEstimate(flops=flops, bytes_accessed=1 << 20, transcendentals=0),
    )(scalars, *[array for array, _ in ins])


def lane_half(value, which):
    lane = lax.broadcasted_iota(jnp.int32, value.shape, 1)
    keep = (lane < HD) if which == 0 else (lane >= HD)
    return jnp.where(keep, value, jnp.zeros_like(value))


def softmax_t(scores):
    peak = jnp.max(scores, axis=0, keepdims=True)
    raised = jnp.exp(scores - peak)
    total = jnp.sum(raised, axis=0, keepdims=True)
    return (raised * (1.0 / total)).astype(bf16)


def toeplitz(row, rows):
    spread = jnp.broadcast_to(row, (rows, row.shape[-1]))
    return pltpu.roll(spread, 0, 1, stride=1, stride_axis=0)


def diagonals(value, width):
    rows = value.shape[0]
    row = lax.broadcasted_iota(jnp.int32, (rows, rows), 0)
    col = lax.broadcasted_iota(jnp.int32, (rows, rows), 1)
    flipped = dot_nn((row + col == rows - 1).astype(bf16), value)
    padded = jnp.concatenate([flipped, jnp.zeros((rows, width - value.shape[1]), f32)], axis=1)
    return jnp.sum(pltpu.roll(padded, 0, 1, stride=1, stride_axis=0), axis=0, keepdims=True)


def rest_mask():
    row = lax.broadcasted_iota(jnp.int32, (REST, REST), 0) // SMALL
    col = lax.broadcasted_iota(jnp.int32, (REST, REST), 1) // SMALL
    return row == col


def score_grad(weights, grad_weights, row_sum):
    return (weights.astype(f32) * (grad_weights - row_sum)).astype(bf16)


def transposed(value):
    return value.astype(f32).T.astype(bf16) if value.dtype == bf16 and value.shape[0] % 128 else value.T


def take_near(at, own, near, which):
    return jnp.where(which, own[0], near[0])


def attend_pair(q, k, v, bias_ref, big_ref, rest_ref):
    values_t = v.T
    allowed = rest_mask()
    heads = []
    for hh in range(2):
        queries = lane_half(q, hh)
        bias = [toeplitz(bias_ref[hh, b : b + 1, :], 128)[:, :BIG] for b in range(3)]
        scores = dot_nt(k[:BIG], queries[:BIG]) + jnp.concatenate(bias, axis=0)
        weights = softmax_t(scores)
        big_ref[hh] = weights
        head_v = values_t[hh * HD : (hh + 1) * HD]
        context = dot_nn(head_v[:, :BIG], weights)
        rest = dot_nt(k[BIG:], queries[BIG:]) + bias[0][:, :REST]
        rest = softmax_t(jnp.where(allowed, rest, masked_score))
        rest_ref[hh] = rest
        heads.append(jnp.concatenate([context, dot_nn(head_v[:, BIG:], rest)], axis=1))
    return jnp.concatenate(heads, axis=0).T.astype(bf16)


def enc_attention(scalars, rows, gains, bias, own, near, got, got_near, chunk):
    opening = chunk == 0
    quarter = got.shape[1]

    def kernel(at, rows_ref, gain_ref, bias_ref, oq, okv, nq, nkv, gw, gnw, *refs):
        if opening:
            qkv_ref, c_ref, big_ref, rest_ref, w_ref, n1_ref, xr_ref, twice = refs
            @pl.when(pl.program_id(0) == 0)
            def _():
                twice[:BUF] = rows_ref[0]
                twice[BUF:] = rows_ref[0, :REST]
                rolled = twice[pl.ds(pl.multiple_of(at[START], SMALL), BUF)]
                xr_ref[...] = rolled
                n1_ref[...] = norm_rows(rolled.astype(f32), gain_ref[0:1])
        else:
            qkv_ref, c_ref, big_ref, rest_ref, w_ref = refs
            n1_ref = rows_ref
        parts = ((oq[0], okv[0], okv[1]), (nq[0], nkv[0], nkv[1]), (gw[0], gw[1], gw[2]), (gnw[0], gnw[1], gnw[2]))
        for k, mats in enumerate(parts):
            place = pl.ds(pl.multiple_of(at[BASE + k], quarter), quarter)
            w_ref[0, place] = jnp.concatenate(mats, axis=1)
        qkv = dot_nn(n1_ref[...], w_ref[0]).astype(bf16)
        qkv_ref[0] = qkv
        c_ref[...] = attend_pair(qkv[:, :128], qkv[:, 128:256], qkv[:, 256:], bias_ref, big_ref, rest_ref)

    first = 3 * chunk
    one = pl.BlockSpec((1, quarter, 128), lambda p, at: (0, 0, first + p))
    two = pl.BlockSpec((2, quarter, 128), lambda p, at: (0, 0, first + p))
    three = pl.BlockSpec((3, quarter, 128), lambda p, at: (0, 0, p))
    rows_spec = pl.BlockSpec((1, BUF, D), lambda p, at: (at[CORE], 0, 0)) if opening else whole(BUF, D)
    outs = [
        (shape((3, BUF, 384)), pl.BlockSpec((1, BUF, 384), lambda p, at: (p, 0, 0))),
        (shape((BUF, 384)), pl.BlockSpec((BUF, 128), lambda p, at: (0, p))),
        (shape((6, BIG, BIG)), pl.BlockSpec((2, BIG, BIG), lambda p, at: (p, 0, 0))),
        (shape((6, REST, REST)), pl.BlockSpec((2, REST, REST), lambda p, at: (p, 0, 0))),
        (shape((3, D, 384)), pl.BlockSpec((1, D, 384), lambda p, at: (p, 0, 0))),
    ]
    if opening:
        outs += [(shape((BUF, D)), whole(BUF, D))] * 2
    return call(
        kernel, (3,), scalars,
        [
            (rows, rows_spec), (gains, whole(5, D)),
            (bias, pl.BlockSpec((2, 3, WIDE), lambda p, at: (first + p, 0, 0))),
            (own[0], one), (own[1], two), (near[0], one), (near[1], two), (got, three), (got_near, three),
        ],
        outs, [pltpu.VMEM((BUF + REST, D), bf16)] if opening else (), 2 * 10**10,
    )


FTILE = 384


def feed_specs(index, count):
    own = pl.BlockSpec((1, FTILE, D), lambda i, at: (index, jnp.minimum(i, count - 1), 0))
    near = pl.BlockSpec((1, FTILE, D), lambda i, at: (index, jnp.maximum(i - count, 0), 0))
    return own, near


def enc_feed(scalars, xr, c_a, c_b, own_o, near_o, got, got_near, gains, feed_in, near_in, feed_out, near_out):
    quarter = got.shape[0]
    count = feed_in.shape[1] // FTILE

    def kernel(at, xr_ref, ca, cb, oo, no, go, gno, gain_ref, fi, ni, fo, nf, h1_ref, n2_ref, a_ref, s_ref, p_ref, wo_ref, total):
        step = pl.program_id(0)

        @pl.when(step == 0)
        def _():
            for k, piece in enumerate((oo[0], no[0], go[...], gno[...])):
                wo_ref[pl.ds(pl.multiple_of(at[BASE + k], quarter), quarter)] = piece
            context = jnp.concatenate([ca[...], cb[...]], axis=1)
            h1 = (xr_ref[...].astype(f32) + dot_nn(context, wo_ref[...])).astype(bf16)
            h1_ref[...] = h1
            n2_ref[...] = norm_rows(h1.astype(f32), gain_ref[1:2])
            total[...] = jnp.zeros_like(total)

        w_in = jnp.where(step < count, fi[0], ni[0])
        w_out = jnp.where(step < count, fo[0], nf[0])
        a, slope = gelu_both(dot_nt(n2_ref[...], w_in))
        a_ref[...] = a
        s_ref[...] = slope
        total[...] += dot_nn(a, w_out)

        @pl.when(step == 2 * count - 1)
        def _():
            p_ref[...] = total[...].astype(bf16)

    own, near = feed_specs(0, count)
    rows = whole(BUF, D)
    tile = pl.BlockSpec((BUF, FTILE), lambda i, at: (0, i))
    quarter_spec = pl.BlockSpec((1, quarter, D), lambda i, at: (0, 0, 0))
    return call(
        kernel, (2 * count,), scalars,
        [
            (xr, rows), (c_a, whole(BUF, 384)), (c_b, whole(BUF, 384)), (own_o, quarter_spec), (near_o, quarter_spec),
            (got, whole(quarter, D)), (got_near, whole(quarter, D)), (gains, whole(5, D)),
            (feed_in, own), (near_in, near), (feed_out, own), (near_out, near),
        ],
        [
            (shape((BUF, D)), rows), (shape((BUF, D)), rows), (shape((BUF, 2 * count * FTILE)), tile),
            (shape((BUF, 2 * count * FTILE)), tile), (shape((BUF, D)), rows), (shape((D, D)), whole(D, D)),
        ],
        [pltpu.VMEM((BUF, D), f32)], 2 * 10**10,
    )


GROUP = 4
GROUPS = HEADS // GROUP
CROSS_KEYS = ((0, BIG), (BIG, BIG + SMALL), (BIG + SMALL, BUF))
SELF_KEYS = tuple((i * TGT, (i + 1) * TGT) for i in range(QPB))


def own_head(value):
    row = lax.broadcasted_iota(jnp.int32, value.shape, 0) // TGT
    lane = lax.broadcasted_iota(jnp.int32, value.shape, 1) // HD
    return jnp.where(row == lane, value, jnp.zeros_like(value))


def spread_heads(rows):
    return own_head(jnp.concatenate([rows] * GROUP, axis=0))


def join_heads(value):
    value = own_head(value)
    return sum(value[h * TGT : (h + 1) * TGT] for h in range(GROUP))


def turned(value):
    return value.astype(f32).T.astype(bf16)


def small_attend(keys_of, q, k, v, p_ref, bias_ref=None):
    contexts = []
    for group in range(GROUPS):
        lanes = slice(GROUP * HD * group, GROUP * HD * (group + 1))
        rows = []
        for i, (first, last) in enumerate(keys_of):
            scores = dot_nt(k[first:last, lanes], spread_heads(q[i * TGT : (i + 1) * TGT, lanes]))
            if bias_ref is not None:
                scores = scores + bias_ref[group]
            weights = softmax_t(scores)
            p_ref[group, first:last] = weights
            rows.append(join_heads(dot_nn(turned(weights), v[first:last, lanes])))
        contexts.append(jnp.concatenate(rows, axis=0))
    return jnp.concatenate(contexts, axis=1).astype(bf16)


def small_attend_back(keys_of, q, k, v, grads, p_ref, bias_ref=None):
    dq, dk, dv = [], [], []
    for group in range(GROUPS):
        lanes = slice(GROUP * HD * group, GROUP * HD * (group + 1))
        dq_rows, dk_rows, dv_rows = [], [], []
        bias_grad = 0.0
        for i, (first, last) in enumerate(keys_of):
            own = slice(i * TGT, (i + 1) * TGT)
            queries, out_grads = spread_heads(q[own, lanes]), spread_heads(grads[own, lanes])
            weights = p_ref[group, first:last]
            grad_weights = dot_nt(v[first:last, lanes], out_grads)
            row_sum = jnp.sum(weights.astype(f32) * grad_weights, axis=0, keepdims=True)
            ds = score_grad(weights, grad_weights, row_sum)
            dv_rows.append(dot_nn(weights, out_grads))
            dk_rows.append(dot_nn(ds, queries))
            dq_rows.append(join_heads(dot_nn(turned(ds), k[first:last, lanes])))
            if bias_ref is not None:
                bias_grad = bias_grad + ds.astype(f32)
        if bias_ref is not None:
            bias_ref[group] = bias_grad
        for to, parts in ((dq, dq_rows), (dk, dk_rows), (dv, dv_rows)):
            to.append(jnp.concatenate(parts, axis=0).astype(bf16))
    return tuple(jnp.concatenate(parts, axis=1) for parts in (dq, dk, dv))


def by_owner(at, ref):
    return jnp.concatenate(
        [ref[0, pl.ds(pl.multiple_of(at[OWNER + i] * TGT, TGT), TGT)] for i in range(QPB)], axis=0
    )


def core_rows():
    return pl.BlockSpec((1, DEC, D), lambda i, at: (at[CORE], 0, 0))


ANYWHERE = pl.BlockSpec(memory_space=pl.ANY)


def weight_args(parts):
    return [(array, ANYWHERE) for array in parts]


def weight_copies(at, index, refs, w, sem):
    quarter = refs[0].shape[1]
    pieces, piece = refs[6].shape[0], refs[6].shape[2]
    copies = []

    def copy(source, target):
        copies.append(pltpu.make_async_copy(source, target, sem.at[len(copies)]))

    for k in range(2):
        place = pl.ds(pl.multiple_of(at[BASE + k], quarter), quarter)
        q, kv, o = refs[3 * k : 3 * k + 3]
        copy(q.at[index], w.at[0, place])
        copy(kv.at[pl.ds(2 * index, 2)], w.at[pl.ds(1, 2), place])
        copy(o.at[index], w.at[3, place])
    for k in range(2):
        for j in range(pieces):
            row = at[BASE + 2 + k] + at[PIECE + 4 * (index - 1) + j]
            copy(refs[6 + k].at[j], w.at[:, pl.ds(pl.multiple_of(row, piece), piece)])
    for one in copies:
        one.start()
    return copies


WEIGHT_SCRATCH = [pltpu.VMEM((4, D, D), bf16), pltpu.SemaphoreType.DMA((14,))]


def dec_self(scalars, decoder_in, gains, bias, self_w):
    def kernel(at, x_ref, gain_ref, bias_ref, *refs):
        xd_ref, n3_ref, q_ref, k_ref, v_ref, c_ref, p_ref, m_ref, n4_ref, w, sem = refs[8:]
        copies = weight_copies(at, 1, refs[:8], w, sem)
        xd = by_owner(at, x_ref)
        xd_ref[...] = xd
        n3 = norm_rows(xd.astype(f32), gain_ref[2:3])
        n3_ref[...] = n3
        for one in copies:
            one.wait()
        q, k, v = (dot_nn(n3, w[i]).astype(bf16) for i in range(3))
        q_ref[...], k_ref[...], v_ref[...] = q, k, v
        c = small_attend(SELF_KEYS, q, k, v, p_ref, bias_ref)
        c_ref[...] = c
        m = xd.astype(f32) + dot_nn(c, w[3])
        m_ref[...] = m
        n4_ref[...] = norm_rows(m, gain_ref[3:4])

    rows = whole(DEC, D)
    low = (shape((DEC, D)), rows)
    return call(
        kernel, (1,), scalars,
        [(decoder_in, core_rows()), (gains, whole(5, D)), (bias, whole(GROUPS, TGT, GROUP * TGT))] + weight_args(self_w),
        [low] * 6 + [(shape((GROUPS, DEC, 128)), whole(GROUPS, DEC, 128)), (shape((DEC, D), f32), rows), low],
        WEIGHT_SCRATCH, 10**8,
    )


def dec_cross(scalars, h1, part, other, m, n4, cross_w, gains, cotangent, feed_in, near_in, feed_out, near_out):
    hidden = feed_in.shape[1]

    def kernel(
        at, h1_ref, p0, p1, m_ref, n4_ref, gain_ref, cot_ref, fi, ni, fo, nf, *refs
    ):
        e_ref, q_ref, k_ref, v_ref, c_ref, p_ref, g_ref, n5_ref, cot_out, a_ref, du_ref, dn_ref, o_ref = refs[8:21]
        w, w_sem, w_in, w_out, sem = refs[21:]
        first = weight_copies(at, 2, refs[:8], w, w_sem)
        copies = []
        for k, (own, near, to) in enumerate(((fi, ni, w_in), (fo, nf, w_out))):
            copies.append(pltpu.make_async_copy(own.at[1], to.at[pl.ds(0, hidden)], sem.at[2 * k]))
            copies.append(pltpu.make_async_copy(near.at[1], to.at[pl.ds(hidden, hidden)], sem.at[1 + 2 * k]))
        for copy in copies:
            copy.start()
        cot = by_owner(at, cot_ref)
        cot_out[...] = cot
        e = (h1_ref[...].astype(f32) + (p0[...].astype(f32) + p1[...].astype(f32))).astype(bf16)
        e_ref[...] = e
        for one in first:
            one.wait()
        k = dot_nn(e, w[1]).astype(bf16)
        v = dot_nn(e, w[2]).astype(bf16)
        q = dot_nn(n4_ref[...], w[0]).astype(bf16)
        q_ref[...], k_ref[...], v_ref[...] = q, k, v
        c = small_attend(CROSS_KEYS, q, k, v, p_ref)
        c_ref[...] = c
        g = (m_ref[...] + dot_nn(c, w[3])).astype(bf16)
        g_ref[...] = g
        n5 = norm_rows(g.astype(f32), gain_ref[4:5])
        n5_ref[...] = n5
        copies[0].wait()
        copies[1].wait()
        a, slope = gelu_both(dot_nt(n5, w_in[...]))
        a_ref[...] = a
        copies[2].wait()
        copies[3].wait()
        du = (slope.astype(f32) * dot_nt(cot, w_out[...])).astype(bf16)
        du_ref[...] = du
        dn_ref[...] = dot_nn(du, w_in[...]).astype(bf16)
        o_ref[...] = dot_nn(a, w_out[...]).astype(bf16)

    rows, small = whole(BUF, D), whole(DEC, D)
    big_low, low = (shape((BUF, D)), rows), (shape((DEC, D)), small)
    wide = (shape((DEC, 2 * hidden)), whole(DEC, 2 * hidden))
    return call(
        kernel, (1,), scalars,
        [
            (h1, rows), (part, rows), (other, rows), (m, small), (n4, small),
            (gains, whole(5, D)), (cotangent, core_rows()),
            (feed_in, ANYWHERE), (near_in, ANYWHERE), (feed_out, ANYWHERE), (near_out, ANYWHERE),
        ]
        + weight_args(cross_w),
        [
            big_low, low, big_low, big_low, low, (shape((GROUPS, BUF, 128)), whole(GROUPS, BUF, 128)),
            low, low, low, wide, wide, low, low,
        ],
        WEIGHT_SCRATCH
        + [
            pltpu.VMEM((2 * hidden, D), bf16), pltpu.VMEM((2 * hidden, D), bf16), pltpu.SemaphoreType.DMA((4,)),
        ],
        2 * 10**10,
    )


def feed_weights(scalars, lefts, right_rows, hidden):
    count = hidden // FTILE
    pairs = len(lefts)
    rows = lefts[0].shape[0]

    def kernel(at, *refs):
        step = pl.program_id(0)
        ins, outs = refs[: 2 * pairs], refs[2 * pairs :]
        for keep, to in ((step < count, outs[:pairs]), (step >= count, outs[pairs:])):

            @pl.when(keep)
            def _(to=to):
                for k in range(pairs):
                    to[k][...] = dot_nn(transposed(ins[2 * k][...]), ins[2 * k + 1][...]).astype(bf16)

    tile = pl.BlockSpec((rows, FTILE), lambda i, at: (0, i))
    ins = []
    for left, right in zip(lefts, right_rows):
        ins += [(left, tile), (right, whole(rows, D))]
    kind = shape((hidden, D))
    own = (kind, pl.BlockSpec((FTILE, D), lambda i, at: (jnp.minimum(i, count - 1), 0)))
    other = (kind, pl.BlockSpec((FTILE, D), lambda i, at: (jnp.maximum(i - count, 0), 0)))
    return call(
        kernel, (2 * count,), scalars, ins, [own] * pairs + [other] * pairs,
        flops=10**10,
    )


def cross_back(scalars, g, gains, p0, p1, cot, cross_w, q, k, v, weights, m):
    def kernel(
        at, g_ref, gain_ref, p0_ref, p1_ref, cot_ref, q_ref, k_ref, v_ref, p_ref, m_ref, *refs
    ):
        dg_ref, dq_ref, dk_ref, dv_ref, de_ref, gain_out, dm_ref, w, sem = refs[8:]
        copies = weight_copies(at, 2, refs[:8], w, sem)
        dn5 = p0_ref[...].astype(f32) + p1_ref[...].astype(f32)
        dg_rows, gain4 = norm_back(g_ref[...].astype(f32), gain_ref[4:5], dn5)
        dg = (dg_rows + cot_ref[...].astype(f32)).astype(bf16)
        dg_ref[...] = dg
        for one in copies:
            one.wait()
        dc = dot_nt(dg, w[3]).astype(bf16)
        dq, dk, dv = small_attend_back(CROSS_KEYS, q_ref[...], k_ref[...], v_ref[...], dc, p_ref)
        dq_ref[...], dk_ref[...], dv_ref[...] = dq, dk, dv
        de_ref[...] = (dot_nt(dk, w[1]) + dot_nt(dv, w[2])).astype(bf16)
        dm_rows, gain3 = norm_back(m_ref[...], gain_ref[3:4], dot_nt(dq, w[0]))
        dm_ref[...] = dm_rows + dg.astype(f32)
        gain_out[...] = jnp.concatenate([gain3, gain4], axis=0)

    rows, small = whole(BUF, D), whole(DEC, D)
    big_low, low = (shape((BUF, D)), rows), (shape((DEC, D)), small)
    return call(
        kernel, (1,), scalars,
        [
            (g, small), (gains, whole(5, D)), (p0, small), (p1, small), (cot, small),
            (q, small), (k, rows), (v, rows), (weights, whole(GROUPS, BUF, 128)), (m, small),
        ]
        + weight_args(cross_w),
        [low, low, big_low, big_low, big_low, (shape((2, D), f32), whole(2, D)), (shape((DEC, D), f32), small)],
        WEIGHT_SCRATCH,
        2 * 10**10,
    )


def enc_feed_back(scalars, de, slope, feed_in, near_in, feed_out, near_out):
    count = feed_in.shape[1] // FTILE

    def kernel(at, de_ref, s_ref, fi, ni, fo, nf, du_ref, p_ref, total):
        step = pl.program_id(0)
        w_in = jnp.where(step < count, fi[0], ni[0])
        w_out = jnp.where(step < count, fo[0], nf[0])
        du = (s_ref[...].astype(f32) * dot_nt(de_ref[...], w_out)).astype(bf16)
        du_ref[...] = du
        grad = dot_nn(du, w_in)

        @pl.when(step == 0)
        def _():
            total[...] = grad

        @pl.when(step > 0)
        def _():
            total[...] += grad

        @pl.when(step == 2 * count - 1)
        def _():
            p_ref[...] = total[...].astype(bf16)

    own, near = feed_specs(0, count)
    tile = pl.BlockSpec((BUF, FTILE), lambda i, at: (0, i))
    return call(
        kernel, (2 * count,), scalars,
        [(de, whole(BUF, D)), (slope, tile), (feed_in, own), (near_in, near), (feed_out, own), (near_out, near)],
        [(shape(slope.shape), tile), (shape((BUF, D)), whole(BUF, D))],
        [pltpu.VMEM((BUF, D), f32)], 2 * 10**10,
    )


def chip_cols(at, ref):
    return ref[:, pl.ds(pl.multiple_of(at[ACROSS] * BIG, 128), BIG)]


def store_rows(at, grads, own_ref, other_ref):
    first = at[CORE] == 0
    for i, grad in enumerate(grads):
        low = grad.astype(bf16)
        half = low.shape[0] // 2
        own_ref[i] = jnp.where(first, low[:half], low[half:])
        other_ref[i] = jnp.where(first, low[half:], low[:half])


def quarter_outs(mats):
    kind = (shape((mats, BIG // 2, D)), whole(mats, BIG // 2, D))
    return [kind, kind]


def cross_weights(scalars, n4, dq, e, dk, dv, c, dg):
    def kernel(at, n4_ref, dq_ref, e_ref, dk_ref, dv_ref, c_ref, dg_ref, own_ref, other_ref):
        n4_t, e_t, c_t = (transposed(chip_cols(at, ref)) for ref in (n4_ref, e_ref, c_ref))
        pairs = ((n4_t, dq_ref), (e_t, dk_ref), (e_t, dv_ref), (c_t, dg_ref))
        store_rows(at, [dot_nn(left, right[...]) for left, right in pairs], own_ref, other_ref)

    rows, small = whole(BUF, D), whole(DEC, D)
    return call(
        kernel, (1,), scalars,
        [(n4, small), (dq, small), (e, rows), (dk, rows), (dv, rows), (c, small), (dg, small)],
        quarter_outs(4),
    )


def self_back(scalars, dm, gains, self_w, q, k, v, c, weights, xd, n3):
    def kernel(at, dm_ref, gain_ref, q_ref, k_ref, v_ref, c_ref, p_ref, xd_ref, n3_ref, *refs):
        own_ref, other_ref, grad_ref, gain_out, diag_ref, w, sem = refs[8:]
        copies = weight_copies(at, 1, refs[:8], w, sem)
        dm = dm_ref[...]
        low = dm.astype(bf16)
        for one in copies:
            one.wait()
        dc = dot_nt(low, w[3]).astype(bf16)
        dq, dk, dv = small_attend_back(SELF_KEYS, q_ref[...], k_ref[...], v_ref[...], dc, p_ref, diag_ref)
        dn3 = dot_nt(dq, w[0]) + dot_nt(dk, w[1]) + dot_nt(dv, w[2])
        dd, gain2 = norm_back(xd_ref[...].astype(f32), gain_ref[2:3], dn3)
        gain_out[...] = gain2
        grad = (dd + dm).astype(bf16)
        for i in range(QPB):
            grad_ref[pl.ds(pl.multiple_of(at[OWNER + i] * TGT, TGT), TGT)] = grad[i * TGT : (i + 1) * TGT]
        n3_t, c_t = transposed(chip_cols(at, n3_ref)), transposed(chip_cols(at, c_ref))
        store_rows(at, [dot_nn(n3_t, dq), dot_nn(n3_t, dk), dot_nn(n3_t, dv), dot_nn(c_t, low)], own_ref, other_ref)

    small = whole(DEC, D)
    return call(
        kernel, (1,), scalars,
        [
            (dm, small), (gains, whole(5, D)),
            (q, small), (k, small), (v, small), (c, small), (weights, whole(GROUPS, DEC, 128)), (xd, small), (n3, small),
        ]
        + weight_args(self_w),
        quarter_outs(4)
        + [
            (shape((DEC, D)), small), (shape((1, D), f32), whole(1, D)),
            (shape((GROUPS, TGT, 128), f32), whole(GROUPS, TGT, 128)),
        ],
        WEIGHT_SCRATCH, 10**9,
    )


def enc_back(scalars, opening, gains, xr, chunk, chunk_c, n1=None, start=None, carried=None):
    half = BIG // 2
    first = 0 if opening else 3

    def kernel(at, gain_ref, xr_ref, wo_ref, ca_ref, cb_ref, qkv_ref, c_ref, big_ref, rest_ref, w_ref, *refs):
        if opening:
            h1_ref, p0_ref, p1_ref, de_ref, n1_ref = refs[:5]
            own_ref, other_ref, diag_ref, rdiag_ref, dh1_ref, dn1_ref, n1_t, c_t, gain_out = refs[5:]
        else:
            dh1_ref, dn1_in, n1_t, c_t = refs[:4]
            own_ref, other_ref, diag_ref, rdiag_ref, grad_ref, gain_out, dn1_ref, twice = refs[6:]
        p = pl.program_id(0)

        @pl.when(p == 0)
        def _():
            if opening:
                dn2 = p0_ref[...].astype(f32) + p1_ref[...].astype(f32)
                dh1_rows, gain1 = norm_back(h1_ref[...].astype(f32), gain_ref[1:2], dn2)
                dh1_ref[...] = (dh1_rows + de_ref[...].astype(f32)).astype(bf16)
                gain_out[...] = gain1
                n1_t[...] = chip_cols(at, n1_ref).T
                c_t[...] = jnp.where(at[ACROSS] == 0, ca_ref[...], cb_ref[...]).T
                dn1_ref[...] = jnp.zeros_like(dn1_ref)
            else:
                dn1_ref[...] = dn1_in[...]

        qkv, c, w = qkv_ref[0], c_ref[...], w_ref[0]
        q, k, v = qkv[:, :128], qkv[:, 128:256], qkv[:, 256:]
        dh1 = dh1_ref[...]
        grads = dot_nt(dh1, wo_ref[...]).astype(bf16)
        keys_t = k.T
        product_t = (grads.astype(f32) * c.astype(f32)).T
        dq_t = []
        dk_big = dv_big = dk_rest = dv_rest = 0.0
        for hh in range(2):
            row_sum = jnp.sum(product_t[hh * HD : (hh + 1) * HD], axis=0, keepdims=True)
            queries, values, grads_h = lane_half(q, hh), lane_half(v, hh), lane_half(grads, hh)
            head_k = keys_t[hh * HD : (hh + 1) * HD]
            weights = big_ref[hh]
            ds = score_grad(weights, dot_nt(values[:BIG], grads[:BIG]), row_sum[:, :BIG])
            dv_big = dv_big + dot_nn(weights, grads_h[:BIG])
            dk_big = dk_big + dot_nn(ds, queries[:BIG])
            diag_ref[hh] = jnp.concatenate(
                [diagonals(ds[128 * b : 128 * (b + 1)], WIDE) for b in range(3)], axis=0
            )
            dq_head = dot_nn(head_k[:, :BIG], ds)
            weights = rest_ref[hh]
            ds = score_grad(weights, dot_nt(values[BIG:], grads[BIG:]), row_sum[:, BIG:])
            dv_rest = dv_rest + dot_nn(weights, grads_h[BIG:])
            dk_rest = dk_rest + dot_nn(ds, queries[BIG:])
            rdiag_ref[hh] = diagonals(ds, 2 * REST)
            dq_t.append(jnp.concatenate([dq_head, dot_nn(head_k[:, BIG:], ds)], axis=1))
        dq = jnp.concatenate(dq_t, axis=0).T.astype(bf16)
        dk = jnp.concatenate([dk_big, dk_rest], axis=0).astype(bf16)
        dv = jnp.concatenate([dv_big, dv_rest], axis=0).astype(bf16)
        dqkv = jnp.concatenate([dq, dk, dv], axis=1)
        dn1_ref[...] += dot_nt(dqkv, w)
        grad = dot_nn(n1_t[...], dqkv)
        columns = pl.ds(pl.multiple_of(128 * (first + p), 128), 128)
        out_grad = dot_nn(c_t[...], dh1_ref[:, columns])
        store_rows(at, [grad[:, 128 * i : 128 * i + 128] for i in range(3)] + [out_grad], own_ref, other_ref)

        if not opening:

            @pl.when(p == 2)
            def _():
                rows, gain0 = norm_back(xr_ref[...].astype(f32), gain_ref[0:1], dn1_ref[...])
                gain_out[...] = gain0
                low = (rows + dh1.astype(f32)).astype(bf16)
                twice[:BUF] = low
                twice[BUF:] = low
                grad_ref[...] = twice[pl.ds(pl.multiple_of(BUF - at[START], SMALL), BUF)]

    rows = whole(BUF, D)
    wo = start[4] if opening else carried[-1]
    qkv, c, big, rest, w = chunk
    ins = [
        (gains, whole(5, D)), (xr, rows), (wo, pl.BlockSpec((128, D), lambda p, at: (first + p, 0))),
        (chunk_c[0], whole(BUF, BIG)), (chunk_c[1], whole(BUF, BIG)),
        (qkv, pl.BlockSpec((1, BUF, BIG), lambda p, at: (p, 0, 0))),
        (c, pl.BlockSpec((BUF, 128), lambda p, at: (0, p))),
        (big, pl.BlockSpec((2, BIG, BIG), lambda p, at: (p, 0, 0))),
        (rest, pl.BlockSpec((2, REST, REST), lambda p, at: (p, 0, 0))),
        (w, pl.BlockSpec((1, D, BIG), lambda p, at: (p, 0, 0))),
    ]
    columns = (shape((4, half, D)), pl.BlockSpec((4, half, 128), lambda p, at: (0, 0, first + p)))
    outs = [
        columns, columns,
        (shape((6, 3, WIDE), f32), pl.BlockSpec((2, 3, WIDE), lambda p, at: (p, 0, 0))),
        (shape((6, 1, 2 * REST), f32), pl.BlockSpec((2, 1, 2 * REST), lambda p, at: (p, 0, 0))),
    ]
    low, turned = (shape((BUF, D)), rows), (shape((BIG, BUF)), whole(BIG, BUF))
    one = (shape((1, D), f32), whole(1, D))
    scratch, aliases = (), {}
    if opening:
        ins += [(value, rows) for value in start[:4]] + [(n1, rows)]
        outs += [low, (shape((BUF, D), f32), rows), turned, turned, one]
    else:
        own, other, dh1, dn1, n1_t, c_t, _ = carried
        ins += [(dh1, rows), (dn1, rows), (n1_t, whole(BIG, BUF)), (c_t, whole(BIG, BUF)), (own, ANYWHERE), (other, ANYWHERE)]
        aliases = {len(ins) - 1: 0, len(ins): 1}
        outs += [low, one]
        scratch = [pltpu.VMEM((BUF, D), f32), pltpu.VMEM((2 * BUF, D), bf16)]
    return call(kernel, (3,), scalars, ins, outs, scratch, 2 * 10**10, aliases)


def swap_section(value, bit):
    count = lax.axis_size("section")
    return lax.ppermute(value, "section", [(i, i ^ bit) for i in range(count)])


def swap_dp(value, bit):
    count = lax.axis_size("dp")
    return lax.ppermute(value, "dp", [(i, i ^ bit) for i in range(count)])


def add_low(a, b):
    return (a.astype(f32) + b.astype(f32)).astype(bf16)


def tie(value, *deps):
    return lax.optimization_barrier((value,) + deps)[0] if deps else value


def halves(own, got, extra=None):
    half = own.shape[0] // 2
    mine = lax.axis_index("dp") % 2

    def part(which):
        rows = [lax.dynamic_slice_in_dim(value, which * half, half, 0) for value in (own, got)]
        total = add_low(*rows)
        return total if extra is None else jnp.concatenate([total, extra])

    return part(mine), part(1 - mine)


def rejoin(keep, other):
    mine = lax.axis_index("dp") % 2
    keep = keep[: other.shape[0]]
    return jnp.where(mine == 0, jnp.concatenate([keep, other]), jnp.concatenate([other, keep]))


Y_TIME, TREE_TIME, STEP = 12.7, 12.7, 3.0
STAGES = (("y", Y_TIME), ("in", TREE_TIME), ("mid", TREE_TIME), ("out", TREE_TIME), ("y", Y_TIME))
ROUTES = {
    "y": tuple((i, i ^ 1) for i in range(8)),
    "in": ((0, 2), (1, 3), (6, 4), (7, 5)),
    "mid": ((2, 4), (3, 5), (4, 2), (5, 3)),
    "out": ((2, 0), (3, 1), (4, 6), (5, 7)),
}


class GradSum:
    def __init__(self, pieces):
        self.count = lax.axis_size("dp")
        self.value = {}
        self.extra = None
        self.stage = {i: 0 for i in pieces}
        self.links = {name: [] for name in ROUTES}
        self.sent, self.got = {}, {}

    def enter(self, i, own, got, extra=None):
        own, got = own.reshape(-1, D), got.reshape(-1, D)
        if self.count != 8:
            self.value[i] = lax.psum(add_low(own, got), "dp")
            self.extra = None if extra is None else lax.psum(extra, "dp")
        else:
            self.value[i] = (own, got, extra)

    def step(self, i, *after):
        now = self.stage[i]
        self.stage[i] = now + 1
        if self.count != 8:
            return
        link = STAGES[now][0]
        value = self.value[i]
        if now > 0:
            value = tie(value, *after)
        if now == 0:
            value, sent = halves(*(tie(value[0], *after), tie(value[1], *after), value[2]))
        elif now == 4:
            sent = value[: value.shape[0] // 128 * 128]
            if sent.shape != value.shape:
                self.extra = value[sent.shape[0] :]
        else:
            sent = value
        before = self.links[link]
        sent = tie(sent, *before[-2:-1])
        got = lax.ppermute(sent, "dp", ROUTES[link])
        before.append(got)
        z = lax.axis_index("dp") // 2
        if now < 3:
            value = add_low(value, got)
        elif now == 3:
            value = jnp.where((z == 0) | (z == 3), got, value)
        else:
            value = rejoin(value, got)
        self.value[i], self.sent[i, now], self.got[i, now] = value, sent, got

    def between(self, after, ended, begun):
        for i in begun:
            self.step(i, after)
        if self.count != 8:
            return []
        return [self.got[key] for key in ended] + [self.sent[i, self.stage[i] - 1] for i in begun]

    def finish(self, late):
        free = {name: 0.0 for name in ROUTES}
        at = {i: late.get(i, 0.0) for i in self.stage}
        while min(self.stage.values()) < len(STAGES):
            choices = [(max(at[i], free[STAGES[now][0]]), now, i) for i, now in self.stage.items() if now < len(STAGES)]
            soon = min(choices)[0] + 6.0
            begin, _, i = min((c for c in choices if c[0] <= soon), key=lambda c: (c[1], c[0]))
            link, length = STAGES[self.stage[i]]
            free[link], at[i] = begin + length + 0.5, begin + length + STEP
            self.step(i)
        return self.value


def shards(
    encoder_in, decoder_in, lengths, query_map, attn_query, attn_keyval, attn_output,
    feed_in, feed_out, norm_gains, position_bias, cotangent,
):
    section_id = lax.axis_index("section")
    across = section_id // 2
    core = section_id % 2
    quarter = attn_query.shape[1]
    half = 2 * quarter

    dp_id = lax.axis_index("dp")
    own = (attn_query, attn_keyval, attn_output)
    near = tuple(swap_section(a, 1) for a in own)
    hidden = feed_in.shape[1]

    def packed(index, mats, first, last, *after):
        parts = [tie(attn_query[index : index + 1], *after), attn_keyval[2 * index : 2 * index + 2], attn_output[index : index + 1]]
        return jnp.concatenate(parts[: mats - 1], axis=0)[:, :, first:last]

    bases = [(section_id ^ k) * quarter for k in range(4)]
    def piece_of(index, count, *after):
        size = quarter // count
        piece = lax.dynamic_slice_in_dim(packed(index, 4, 0, D), (dp_id % count) * size, size, 1)
        return swap_section(tie(piece, *after), 2)

    def places(count):
        at = dp_id % count
        return [(at ^ k) * (quarter // count) if k < count else 0 for k in range(4)]

    pack_a = packed(0, 3, 0, D // 2)
    got_a = swap_section(pack_a, 2)

    big = jnp.argmax(lengths[core]).astype(jnp.int32)
    owners = lax.dynamic_slice_in_dim(jnp.concatenate([query_map[core]] * 2), big, QPB, 0)
    scalars = jnp.concatenate(
        [jnp.stack([core, across, big * SMALL]), owners, jnp.stack(bases + places(4) + places(2))]
    ).astype(jnp.int32)

    enc_table = spread_table(position_bias[0], encoder_bucket(enc_offsets()))
    causal = jnp.asarray(dec_offsets() <= 0)
    dec_table = jnp.where(causal, spread_table(position_bias[1], decoder_bucket(dec_offsets())), masked_score)
    dec_table = jnp.transpose(dec_table.reshape(GROUPS, GROUP, TGT, TGT), (0, 2, 1, 3)).reshape(GROUPS, TGT, GROUP * TGT)
    sums = GradSum(range(7))

    near_a = swap_section(tie(got_a, scalars, enc_table, dec_table), 1)
    got_b = swap_section(packed(0, 3, D // 2, D, pack_a), 2)
    got_self = piece_of(1, 4, near_a)
    first = enc_attention(scalars, encoder_in, norm_gains, enc_table, own, near, got_a, near_a, 0)
    n1, xr = first[5:]
    got_o = swap_section(tie(attn_output[0], near_a), 2)
    near_b = swap_section(tie(got_b, n1), 1)
    got_cross = piece_of(2, 2, n1)
    piece = tie(got_self, n1)
    second_piece, third_piece = swap_dp(piece, 1), swap_dp(piece, 2)
    near_in = swap_section(tie(feed_in, near_a), 1)
    near_out = swap_section(tie(feed_out, near_a), 1)
    second = enc_attention(scalars, n1, norm_gains, enc_table, own, near, got_b, near_b, 1)
    near_got_o = swap_section(tie(got_o, second[1]), 1)
    fourth_piece = swap_dp(tie(second_piece, second[1]), 2)
    quad = jnp.stack([piece, second_piece, third_piece, fourth_piece])
    h1, n2, a1, slope1, part, wo = enc_feed(
        scalars, xr, first[1], second[1], attn_output, near[2], got_o, near_got_o, norm_gains,
        feed_in, near_in, feed_out, near_out,
    )
    part_other = swap_section(part, 2)
    quad = tie(quad, part)
    self_w = own + near + (quad, swap_section(quad, 1))
    pair = tie(got_cross, second[1])
    pair = tie(jnp.stack([pair, swap_dp(pair, 1)]), part)
    cross_w = own + near + (pair, swap_section(pair, 1))
    xd, n3, q2, k2, v2, c2, p2, m, n4 = dec_self(scalars, decoder_in, norm_gains, dec_table, self_w)
    e, q3, k3, v3, c3, p3, g, n5, cot, a2, du2, dn5, out_part = dec_cross(
        scalars, h1, part, part_other, m, n4, cross_w, norm_gains, cotangent, feed_in, near_in, feed_out, near_out
    )

    dn5_other = swap_section(dn5, 2)
    own_out, own_in, other_out, other_in = feed_weights(scalars, (a2, du2), (cot, n5), hidden)
    sums.enter(0, own_out, swap_section(other_out, 1))
    sums.enter(1, own_in, swap_section(other_in, 1))

    dn5_other = tie(dn5_other, *sums.between(own_in, (), (0,)))
    dg, dq3, dk3, dv3, de, gains34, dm = cross_back(
        scalars, g, norm_gains, dn5, dn5_other, cot, cross_w, q3, k3, v3, p3, m
    )
    de = tie(de, *sums.between(dq3, (), (1,)))
    du1, dn2 = enc_feed_back(scalars, de, slope1, feed_in, near_in, feed_out, near_out)
    dn2_other = swap_section(dn2, 2)
    own_w, other_w = cross_weights(scalars, n4, dq3, e, dk3, dv3, c3, tie(dg, dn2))
    sums.enter(2, own_w, swap_section(other_w, 1))

    dm = tie(dm, own_w, *sums.between(own_w, (), (0,)))
    own_w, other_w, dec_grad, gain2, diag2 = self_back(scalars, dm, norm_gains, self_w, q2, k2, v2, c2, p2, xd, n3)
    sums.enter(5, own_w, swap_section(other_w, 1))

    n2_late = tie(n2, own_w, dn2_other, *sums.between(dec_grad, (), (1, 2)))
    own_out, own_in, other_out, other_in = feed_weights(scalars, (a1, du1), (de, n2_late), hidden)
    sums.enter(3, own_out, swap_section(other_out, 1))
    sums.enter(4, own_in, swap_section(other_in, 1))

    dn2_late = tie(dn2_other, own_in, *sums.between(own_in, (), (5, 0)))
    contexts = (first[1], second[1])
    own_w, other_w, diag_a, rdiag_a, dh1, dn1, n1_t, c_t, gain1 = enc_back(
        scalars, True, norm_gains, xr, first[:5], contexts, n1, (h1, dn2, dn2_late, de, wo)
    )
    dn1 = tie(dn1, *sums.between(dh1, (), (3, 1)))
    own_enc, other_w, diag_b, rdiag_b, enc_grad, gain0 = enc_back(
        scalars, False, norm_gains, xr, second[:5], contexts, carried=(own_w, other_w, dh1, dn1, n1_t, c_t, wo)
    )
    got_w = swap_section(other_w, 1)

    hot_enc = jnp.asarray(
        np.concatenate(
            [one_hot(encoder_bucket(128 * b + diagonal_offsets(128, WIDE))) for b in range(3)]
            + [one_hot(encoder_bucket(diagonal_offsets(REST, 2 * REST)))]
        )
    )
    hot_dec = jnp.asarray(one_hot(decoder_bucket(dec_offsets())))
    sums_enc = jnp.concatenate(
        [
            jnp.concatenate([d.reshape(HEADS // 2, -1), r.reshape(HEADS // 2, -1)], axis=1)
            for d, r in ((diag_a, rdiag_a), (diag_b, rdiag_b))
        ]
    )
    exact = lax.Precision.HIGHEST
    table_enc = jnp.einsum("mb,hm->bh", hot_enc, sums_enc, precision=exact)
    diag2 = diag2.reshape(GROUPS, TGT, GROUP, TGT)
    table_dec = jnp.einsum("kqb,gkhq->bgh", hot_dec, diag2, precision=exact).reshape(NB, HEADS)
    tables = jnp.stack([table_enc, table_dec]).reshape(-1, D)
    small = jnp.concatenate([gain0, gain1, gain2, gains34, tables, jnp.zeros((10, D), f32)])
    small = small + swap_section(small, 1)
    sums.enter(6, own_enc, got_w, small.astype(bf16))
    total = sums.finish({0: 0.0, 2: 0.0, 5: 4.0, 3: 14.0, 4: 4.0, 6: 10.0})
    unit_out2, unit_in2, unit_cross, unit_out1, unit_in1, unit_self, unit_enc = (total[i] for i in range(7))
    small = sums.extra.astype(f32)
    gains = small[:5]
    tables = small[5].reshape(2, NB, HEADS)

    def split_rows(rows, count):
        mine = lax.dynamic_slice_in_dim(rows, section_id * count, count, 0)
        theirs = swap_section(lax.dynamic_slice_in_dim(rows, (section_id ^ 1) * count, count, 0), 1)
        return jnp.where(core == 0, jnp.stack([mine, theirs]), jnp.stack([theirs, mine]))

    out_rows = (g.astype(f32) + (out_part.astype(f32) + swap_section(out_part, 2).astype(f32))).astype(bf16)
    restored = jnp.zeros((DEC, D), bf16)
    for i in range(QPB):
        restored = lax.dynamic_update_slice_in_dim(restored, out_rows[i * TGT : (i + 1) * TGT], owners[i] * TGT, 0)
    sections = lax.axis_size("section")
    decoder_out = split_rows(restored, DEC // sections)
    decoder_in_grad = split_rows(dec_grad, DEC // sections)
    encoder_in_grad = split_rows(enc_grad, BUF // sections)

    u_enc, u_self, u_cross = (
        u.reshape(4, quarter, D).astype(f32) for u in (unit_enc, unit_self, unit_cross)
    )
    def placed(count, parts):
        whole_grad = jnp.zeros((count, quarter, D), f32)
        for at, part in parts:
            whole_grad = lax.dynamic_update_slice_in_dim(whole_grad, part, at, 0)
        return whole_grad

    query_grad = placed(3, ((2, u_cross[0:1]), (1, u_self[0:1]), (0, u_enc[0:1])))
    keyval_grad = placed(6, ((4, u_cross[1:3]), (2, u_self[1:3]), (0, u_enc[1:3])))
    output_grad = placed(3, ((2, u_cross[3:4]), (1, u_self[3:4]), (0, u_enc[3:4])))
    feed_in_grad = jnp.stack([unit_in1, unit_in2]).astype(f32)
    feed_out_grad = jnp.stack([unit_out1, unit_out2]).astype(f32)
    return (
        decoder_out, encoder_in_grad, decoder_in_grad, query_grad, keyval_grad, output_grad,
        feed_in_grad, feed_out_grad, gains, tables,
    )


def solution(mesh):
    rows = P("dp", None, None)
    mats = P(None, "section", None)
    outs = P("dp", "section", None)
    return jax.shard_map(
        shards,
        mesh=mesh,
        in_specs=(rows, rows, P("dp", None), P("dp", None), mats, mats, mats, mats, mats, P(), P(), rows),
        out_specs=(outs, outs, outs, mats, mats, mats, mats, mats, P(), P()),
        check_vma=False,
    )
```

```python
import functools

import jax
import jax.numpy as jnp
import numpy as np
from jax import lax
from jax.experimental import pallas as pl
from jax.experimental.pallas import tpu as pltpu
from jax.sharding import PartitionSpec as P

D = 768
HEADS = 12
HD = 64
PAIRS = HEADS // 2
NB = 32
BUF = 512
BIG = 384
SMALL = 64
REST = BUF - BIG
QPB = 3
TGT = 32
DEC = QPB * TGT
WIDE = 512
epsilon = 1e-06
masked_score = -1e30
enc_edges = (12, 16, 23, 32, 46, 64, 91)
dec_edges = (19, 21, 24, 27, 31)
bf16 = jnp.bfloat16
f32 = jnp.float32


def dot_nn(a, b):
    return lax.dot_general(a, b, (((1,), (0,)), ((), ())), preferred_element_type=f32)


def dot_nt(a, b):
    return lax.dot_general(a, b, (((1,), (1,)), ((), ())), preferred_element_type=f32)


def dot_tn(a, b):
    return lax.dot_general(a, b, (((0,), (0,)), ((), ())), preferred_element_type=f32)


def encoder_bucket(offset):
    distance = np.abs(offset)
    bucket = np.minimum(distance, 8)
    for boundary in enc_edges:
        bucket = bucket + (distance >= boundary)
    return bucket + 16 * (offset > 0)


def decoder_bucket(offset):
    distance = np.maximum(-offset, 0)
    bucket = np.minimum(distance, 16)
    for boundary in dec_edges:
        bucket = bucket + (distance >= boundary)
    return bucket


def enc_offsets():
    lane = np.arange(WIDE)
    shifted = np.where(lane < BIG, lane, lane - WIDE)
    return 128 * np.arange(3)[:, None] - shifted[None, :]


def diagonal_offsets(rows, width):
    return rows - 1 - np.arange(width)


def dec_offsets():
    return np.arange(TGT)[:, None] - np.arange(TGT)[None, :]


def one_hot(bucket):
    return (bucket[..., None] == np.arange(NB)).astype(np.float32)


def spread_table(table, bucket):
    hot = jnp.asarray(one_hot(bucket))
    return jnp.sum(hot[None] * jnp.transpose(table).reshape((HEADS,) + (1,) * bucket.ndim + (NB,)), axis=-1)


def norm_scale(rows):
    return lax.rsqrt(jnp.mean(rows * rows, axis=-1, keepdims=True) + epsilon)


def norm_rows(rows, gain):
    return (rows * norm_scale(rows) * gain).astype(bf16)


def norm_back(rows, gain, grad):
    scale = norm_scale(rows)
    unit = rows * scale
    weighted = grad * gain
    grad_rows = scale * (weighted - unit * jnp.mean(weighted * unit, axis=-1, keepdims=True))
    return grad_rows, jnp.sum(grad * unit, axis=0, keepdims=True)


def gelu_both(u):
    root = np.float32(np.sqrt(2.0 / np.pi))
    cubic = np.float32(0.044715)
    square = u * u
    bend = jnp.tanh(u * (root + root * cubic * square))
    half = 0.5 * (1.0 + bend)
    slope = half + 0.5 * u * (1.0 - bend * bend) * (root + 3.0 * root * cubic * square)
    return (u * half).astype(bf16), slope.astype(bf16)


CORE, ACROSS, START, OWNER, BASE, PIECE = 0, 1, 2, 3, 6, 10


def shape(dims, dtype=bf16):
    return jax.ShapeDtypeStruct(dims, dtype)


def whole(*dims):
    return pl.BlockSpec(dims, lambda *_: (0,) * len(dims))


def call(kernel, grid, scalars, ins, outs, scratch=(), flops=10**10, aliases=None):
    return pl.pallas_call(
        kernel,
        grid_spec=pltpu.PrefetchScalarGridSpec(
            num_scalar_prefetch=1,
            grid=grid,
            in_specs=[spec for _, spec in ins],
            out_specs=tuple(spec for _, spec in outs),
            scratch_shapes=scratch,
        ),
        out_shape=tuple(kind for kind, _ in outs),
        input_output_aliases=aliases or {},
        compiler_params=pltpu.CompilerParams(vmem_limit_bytes=20 << 20),
        cost_estimate=pl.CostEstimate(flops=flops, bytes_accessed=1 << 20, transcendentals=0),
    )(scalars, *[array for array, _ in ins])


def lane_half(value, which):
    lane = lax.broadcasted_iota(jnp.int32, value.shape, 1)
    keep = (lane < HD) if which == 0 else (lane >= HD)
    return jnp.where(keep, value, jnp.zeros_like(value))


def softmax_t(scores):
    peak = jnp.max(scores, axis=0, keepdims=True)
    raised = jnp.exp(scores - peak)
    total = jnp.sum(raised, axis=0, keepdims=True)
    return (raised * (1.0 / total)).astype(bf16)


def toeplitz(row, rows):
    spread = jnp.broadcast_to(row, (rows, row.shape[-1]))
    return pltpu.roll(spread, 0, 1, stride=1, stride_axis=0)


def diagonals(value, width):
    rows = value.shape[0]
    row = lax.broadcasted_iota(jnp.int32, (rows, rows), 0)
    col = lax.broadcasted_iota(jnp.int32, (rows, rows), 1)
    flipped = dot_nn((row + col == rows - 1).astype(bf16), value)
    padded = jnp.concatenate([flipped, jnp.zeros((rows, width - value.shape[1]), f32)], axis=1)
    return jnp.sum(pltpu.roll(padded, 0, 1, stride=1, stride_axis=0), axis=0, keepdims=True)


def rest_mask():
    row = lax.broadcasted_iota(jnp.int32, (REST, REST), 0) // SMALL
    col = lax.broadcasted_iota(jnp.int32, (REST, REST), 1) // SMALL
    return row == col


def score_grad(weights, grad_weights, row_sum):
    return (weights.astype(f32) * (grad_weights - row_sum)).astype(bf16)


def transposed(value):
    return value.astype(f32).T.astype(bf16) if value.dtype == bf16 and value.shape[0] % 128 else value.T


def take_near(at, own, near, which):
    return jnp.where(which, own[0], near[0])


def attend_pair(q, k, v, bias_ref, big_ref, rest_ref):
    values_t = v.T
    allowed = rest_mask()
    heads = []
    for hh in range(2):
        queries = lane_half(q, hh)
        bias = [toeplitz(bias_ref[hh, b : b + 1, :], 128)[:, :BIG] for b in range(3)]
        scores = dot_nt(k[:BIG], queries[:BIG]) + jnp.concatenate(bias, axis=0)
        weights = softmax_t(scores)
        big_ref[hh] = weights
        head_v = values_t[hh * HD : (hh + 1) * HD]
        context = dot_nn(head_v[:, :BIG], weights)
        rest = dot_nt(k[BIG:], queries[BIG:]) + bias[0][:, :REST]
        rest = softmax_t(jnp.where(allowed, rest, masked_score))
        rest_ref[hh] = rest
        heads.append(jnp.concatenate([context, dot_nn(head_v[:, BIG:], rest)], axis=1))
    return jnp.concatenate(heads, axis=0).T.astype(bf16)


def enc_attention(scalars, rows, gains, bias, own, near, got, got_near, chunk):
    opening = chunk == 0
    quarter = got.shape[1]

    def kernel(at, rows_ref, gain_ref, bias_ref, oq, okv, nq, nkv, gw, gnw, *refs):
        if opening:
            qkv_ref, c_ref, big_ref, rest_ref, w_ref, n1_ref, xr_ref, twice = refs
            @pl.when(pl.program_id(0) == 0)
            def _():
                twice[:BUF] = rows_ref[0]
                twice[BUF:] = rows_ref[0, :REST]
                rolled = twice[pl.ds(pl.multiple_of(at[START], SMALL), BUF)]
                xr_ref[...] = rolled
                n1_ref[...] = norm_rows(rolled.astype(f32), gain_ref[0:1])
        else:
            qkv_ref, c_ref, big_ref, rest_ref, w_ref = refs
            n1_ref = rows_ref
        parts = ((oq[0], okv[0], okv[1]), (nq[0], nkv[0], nkv[1]), (gw[0], gw[1], gw[2]), (gnw[0], gnw[1], gnw[2]))
        for k, mats in enumerate(parts):
            place = pl.ds(pl.multiple_of(at[BASE + k], quarter), quarter)
            w_ref[0, place] = jnp.concatenate(mats, axis=1)
        qkv = dot_nn(n1_ref[...], w_ref[0]).astype(bf16)
        qkv_ref[0] = qkv
        c_ref[...] = attend_pair(qkv[:, :128], qkv[:, 128:256], qkv[:, 256:], bias_ref, big_ref, rest_ref)

    first = 3 * chunk
    one = pl.BlockSpec((1, quarter, 128), lambda p, at: (0, 0, first + p))
    two = pl.BlockSpec((2, quarter, 128), lambda p, at: (0, 0, first + p))
    three = pl.BlockSpec((3, quarter, 128), lambda p, at: (0, 0, p))
    rows_spec = pl.BlockSpec((1, BUF, D), lambda p, at: (at[CORE], 0, 0)) if opening else whole(BUF, D)
    outs = [
        (shape((3, BUF, 384)), pl.BlockSpec((1, BUF, 384), lambda p, at: (p, 0, 0))),
        (shape((BUF, 384)), pl.BlockSpec((BUF, 128), lambda p, at: (0, p))),
        (shape((6, BIG, BIG)), pl.BlockSpec((2, BIG, BIG), lambda p, at: (p, 0, 0))),
        (shape((6, REST, REST)), pl.BlockSpec((2, REST, REST), lambda p, at: (p, 0, 0))),
        (shape((3, D, 384)), pl.BlockSpec((1, D, 384), lambda p, at: (p, 0, 0))),
    ]
    if opening:
        outs += [(shape((BUF, D)), whole(BUF, D))] * 2
    return call(
        kernel, (3,), scalars,
        [
            (rows, rows_spec), (gains, whole(5, D)),
            (bias, pl.BlockSpec((2, 3, WIDE), lambda p, at: (first + p, 0, 0))),
            (own[0], one), (own[1], two), (near[0], one), (near[1], two), (got, three), (got_near, three),
        ],
        outs, [pltpu.VMEM((BUF + REST, D), bf16)] if opening else (), 2 * 10**10,
    )


FTILE = 384


def feed_specs(index, count):
    own = pl.BlockSpec((1, FTILE, D), lambda i, at: (index, jnp.minimum(i, count - 1), 0))
    near = pl.BlockSpec((1, FTILE, D), lambda i, at: (index, jnp.maximum(i - count, 0), 0))
    return own, near


def enc_feed(scalars, xr, c_a, c_b, own_o, near_o, got, got_near, gains, feed_in, near_in, feed_out, near_out):
    quarter = got.shape[0]
    count = feed_in.shape[1] // FTILE

    def kernel(at, xr_ref, ca, cb, oo, no, go, gno, gain_ref, fi, ni, fo, nf, h1_ref, n2_ref, a_ref, s_ref, p_ref, wo_ref, total):
        step = pl.program_id(0)

        @pl.when(step == 0)
        def _():
            for k, piece in enumerate((oo[0], no[0], go[...], gno[...])):
                wo_ref[pl.ds(pl.multiple_of(at[BASE + k], quarter), quarter)] = piece
            context = jnp.concatenate([ca[...], cb[...]], axis=1)
            h1 = (xr_ref[...].astype(f32) + dot_nn(context, wo_ref[...])).astype(bf16)
            h1_ref[...] = h1
            n2_ref[...] = norm_rows(h1.astype(f32), gain_ref[1:2])
            total[...] = jnp.zeros_like(total)

        w_in = jnp.where(step < count, fi[0], ni[0])
        w_out = jnp.where(step < count, fo[0], nf[0])
        a, slope = gelu_both(dot_nt(n2_ref[...], w_in))
        a_ref[...] = a
        s_ref[...] = slope
        total[...] += dot_nn(a, w_out)

        @pl.when(step == 2 * count - 1)
        def _():
            p_ref[...] = total[...].astype(bf16)

    own, near = feed_specs(0, count)
    rows = whole(BUF, D)
    tile = pl.BlockSpec((BUF, FTILE), lambda i, at: (0, i))
    quarter_spec = pl.BlockSpec((1, quarter, D), lambda i, at: (0, 0, 0))
    return call(
        kernel, (2 * count,), scalars,
        [
            (xr, rows), (c_a, whole(BUF, 384)), (c_b, whole(BUF, 384)), (own_o, quarter_spec), (near_o, quarter_spec),
            (got, whole(quarter, D)), (got_near, whole(quarter, D)), (gains, whole(5, D)),
            (feed_in, own), (near_in, near), (feed_out, own), (near_out, near),
        ],
        [
            (shape((BUF, D)), rows), (shape((BUF, D)), rows), (shape((BUF, 2 * count * FTILE)), tile),
            (shape((BUF, 2 * count * FTILE)), tile), (shape((BUF, D)), rows), (shape((D, D)), whole(D, D)),
        ],
        [pltpu.VMEM((BUF, D), f32)], 2 * 10**10,
    )


GROUP = 4
GROUPS = HEADS // GROUP
CROSS_KEYS = ((0, BIG), (BIG, BIG + SMALL), (BIG + SMALL, BUF))
SELF_KEYS = tuple((i * TGT, (i + 1) * TGT) for i in range(QPB))


def own_head(value):
    row = lax.broadcasted_iota(jnp.int32, value.shape, 0) // TGT
    lane = lax.broadcasted_iota(jnp.int32, value.shape, 1) // HD
    return jnp.where(row == lane, value, jnp.zeros_like(value))


def spread_heads(rows):
    return own_head(jnp.concatenate([rows] * GROUP, axis=0))


def join_heads(value):
    value = own_head(value)
    return sum(value[h * TGT : (h + 1) * TGT] for h in range(GROUP))


def turned(value):
    return value.astype(f32).T.astype(bf16)


def small_attend(keys_of, q, k, v, p_ref, bias_ref=None):
    contexts = []
    for group in range(GROUPS):
        lanes = slice(GROUP * HD * group, GROUP * HD * (group + 1))
        rows = []
        for i, (first, last) in enumerate(keys_of):
            scores = dot_nt(k[first:last, lanes], spread_heads(q[i * TGT : (i + 1) * TGT, lanes]))
            if bias_ref is not None:
                scores = scores + bias_ref[group]
            weights = softmax_t(scores)
            p_ref[group, first:last] = weights
            rows.append(join_heads(dot_nn(turned(weights), v[first:last, lanes])))
        contexts.append(jnp.concatenate(rows, axis=0))
    return jnp.concatenate(contexts, axis=1).astype(bf16)


def small_attend_back(keys_of, q, k, v, grads, p_ref, bias_ref=None):
    dq, dk, dv = [], [], []
    for group in range(GROUPS):
        lanes = slice(GROUP * HD * group, GROUP * HD * (group + 1))
        dq_rows, dk_rows, dv_rows = [], [], []
        bias_grad = 0.0
        for i, (first, last) in enumerate(keys_of):
            own = slice(i * TGT, (i + 1) * TGT)
            queries, out_grads = spread_heads(q[own, lanes]), spread_heads(grads[own, lanes])
            weights = p_ref[group, first:last]
            grad_weights = dot_nt(v[first:last, lanes], out_grads)
            row_sum = jnp.sum(weights.astype(f32) * grad_weights, axis=0, keepdims=True)
            ds = score_grad(weights, grad_weights, row_sum)
            dv_rows.append(dot_nn(weights, out_grads))
            dk_rows.append(dot_nn(ds, queries))
            dq_rows.append(join_heads(dot_nn(turned(ds), k[first:last, lanes])))
            if bias_ref is not None:
                bias_grad = bias_grad + ds.astype(f32)
        if bias_ref is not None:
            bias_ref[group] = bias_grad
        for to, parts in ((dq, dq_rows), (dk, dk_rows), (dv, dv_rows)):
            to.append(jnp.concatenate(parts, axis=0).astype(bf16))
    return tuple(jnp.concatenate(parts, axis=1) for parts in (dq, dk, dv))


def by_owner(at, ref):
    return jnp.concatenate(
        [ref[0, pl.ds(pl.multiple_of(at[OWNER + i] * TGT, TGT), TGT)] for i in range(QPB)], axis=0
    )


def core_rows():
    return pl.BlockSpec((1, DEC, D), lambda i, at: (at[CORE], 0, 0))


ANYWHERE = pl.BlockSpec(memory_space=pl.ANY)


def weight_args(parts):
    return [(array, ANYWHERE) for array in parts]


def weight_copies(at, index, refs, w, sem):
    quarter = refs[0].shape[1]
    pieces, piece = refs[6].shape[0], refs[6].shape[2]
    copies = []

    def copy(source, target):
        copies.append(pltpu.make_async_copy(source, target, sem.at[len(copies)]))

    for k in range(2):
        place = pl.ds(pl.multiple_of(at[BASE + k], quarter), quarter)
        q, kv, o = refs[3 * k : 3 * k + 3]
        copy(q.at[index], w.at[0, place])
        copy(kv.at[pl.ds(2 * index, 2)], w.at[pl.ds(1, 2), place])
        copy(o.at[index], w.at[3, place])
    for k in range(2):
        for j in range(pieces):
            row = at[BASE + 2 + k] + at[PIECE + 4 * (index - 1) + j]
            copy(refs[6 + k].at[j], w.at[:, pl.ds(pl.multiple_of(row, piece), piece)])
    for one in copies:
        one.start()
    return copies


WEIGHT_SCRATCH = [pltpu.VMEM((4, D, D), bf16), pltpu.SemaphoreType.DMA((14,))]


def dec_self(scalars, decoder_in, gains, bias, self_w):
    def kernel(at, x_ref, gain_ref, bias_ref, *refs):
        xd_ref, n3_ref, q_ref, k_ref, v_ref, c_ref, p_ref, m_ref, n4_ref, w, sem = refs[8:]
        copies = weight_copies(at, 1, refs[:8], w, sem)
        xd = by_owner(at, x_ref)
        xd_ref[...] = xd
        n3 = norm_rows(xd.astype(f32), gain_ref[2:3])
        n3_ref[...] = n3
        for one in copies:
            one.wait()
        q, k, v = (dot_nn(n3, w[i]).astype(bf16) for i in range(3))
        q_ref[...], k_ref[...], v_ref[...] = q, k, v
        c = small_attend(SELF_KEYS, q, k, v, p_ref, bias_ref)
        c_ref[...] = c
        m = xd.astype(f32) + dot_nn(c, w[3])
        m_ref[...] = m
        n4_ref[...] = norm_rows(m, gain_ref[3:4])

    rows = whole(DEC, D)
    low = (shape((DEC, D)), rows)
    return call(
        kernel, (1,), scalars,
        [(decoder_in, core_rows()), (gains, whole(5, D)), (bias, whole(GROUPS, TGT, GROUP * TGT))] + weight_args(self_w),
        [low] * 6 + [(shape((GROUPS, DEC, 128)), whole(GROUPS, DEC, 128)), (shape((DEC, D), f32), rows), low],
        WEIGHT_SCRATCH, 10**8,
    )


def dec_cross(scalars, h1, part, other, m, n4, cross_w, gains, cotangent, feed_in, near_in, feed_out, near_out):
    hidden = feed_in.shape[1]

    def kernel(
        at, h1_ref, p0, p1, m_ref, n4_ref, gain_ref, cot_ref, fi, ni, fo, nf, *refs
    ):
        e_ref, q_ref, k_ref, v_ref, c_ref, p_ref, g_ref, n5_ref, cot_out, a_ref, du_ref, dn_ref, o_ref = refs[8:21]
        w, w_sem, w_in, w_out, sem = refs[21:]
        first = weight_copies(at, 2, refs[:8], w, w_sem)
        copies = []
        for k, (own, near, to) in enumerate(((fi, ni, w_in), (fo, nf, w_out))):
            copies.append(pltpu.make_async_copy(own.at[1], to.at[pl.ds(0, hidden)], sem.at[2 * k]))
            copies.append(pltpu.make_async_copy(near.at[1], to.at[pl.ds(hidden, hidden)], sem.at[1 + 2 * k]))
        for copy in copies:
            copy.start()
        cot = by_owner(at, cot_ref)
        cot_out[...] = cot
        e = (h1_ref[...].astype(f32) + (p0[...].astype(f32) + p1[...].astype(f32))).astype(bf16)
        e_ref[...] = e
        for one in first:
            one.wait()
        k = dot_nn(e, w[1]).astype(bf16)
        v = dot_nn(e, w[2]).astype(bf16)
        q = dot_nn(n4_ref[...], w[0]).astype(bf16)
        q_ref[...], k_ref[...], v_ref[...] = q, k, v
        c = small_attend(CROSS_KEYS, q, k, v, p_ref)
        c_ref[...] = c
        g = (m_ref[...] + dot_nn(c, w[3])).astype(bf16)
        g_ref[...] = g
        n5 = norm_rows(g.astype(f32), gain_ref[4:5])
        n5_ref[...] = n5
        copies[0].wait()
        copies[1].wait()
        a, slope = gelu_both(dot_nt(n5, w_in[...]))
        a_ref[...] = a
        copies[2].wait()
        copies[3].wait()
        du = (slope.astype(f32) * dot_nt(cot, w_out[...])).astype(bf16)
        du_ref[...] = du
        dn_ref[...] = dot_nn(du, w_in[...]).astype(bf16)
        o_ref[...] = dot_nn(a, w_out[...]).astype(bf16)

    rows, small = whole(BUF, D), whole(DEC, D)
    big_low, low = (shape((BUF, D)), rows), (shape((DEC, D)), small)
    wide = (shape((DEC, 2 * hidden)), whole(DEC, 2 * hidden))
    return call(
        kernel, (1,), scalars,
        [
            (h1, rows), (part, rows), (other, rows), (m, small), (n4, small),
            (gains, whole(5, D)), (cotangent, core_rows()),
            (feed_in, ANYWHERE), (near_in, ANYWHERE), (feed_out, ANYWHERE), (near_out, ANYWHERE),
        ]
        + weight_args(cross_w),
        [
            big_low, low, big_low, big_low, low, (shape((GROUPS, BUF, 128)), whole(GROUPS, BUF, 128)),
            low, low, low, wide, wide, low, low,
        ],
        WEIGHT_SCRATCH
        + [
            pltpu.VMEM((2 * hidden, D), bf16), pltpu.VMEM((2 * hidden, D), bf16), pltpu.SemaphoreType.DMA((4,)),
        ],
        2 * 10**10,
    )


def feed_weights(scalars, lefts, right_rows, hidden):
    count = hidden // FTILE
    pairs = len(lefts)
    rows = lefts[0].shape[0]

    def kernel(at, *refs):
        step = pl.program_id(0)
        ins, outs = refs[: 2 * pairs], refs[2 * pairs :]
        for keep, to in ((step < count, outs[:pairs]), (step >= count, outs[pairs:])):

            @pl.when(keep)
            def _(to=to):
                for k in range(pairs):
                    to[k][...] = dot_nn(transposed(ins[2 * k][...]), ins[2 * k + 1][...]).astype(bf16)

    tile = pl.BlockSpec((rows, FTILE), lambda i, at: (0, i))
    ins = []
    for left, right in zip(lefts, right_rows):
        ins += [(left, tile), (right, whole(rows, D))]
    kind = shape((hidden, D))
    own = (kind, pl.BlockSpec((FTILE, D), lambda i, at: (jnp.minimum(i, count - 1), 0)))
    other = (kind, pl.BlockSpec((FTILE, D), lambda i, at: (jnp.maximum(i - count, 0), 0)))
    return call(
        kernel, (2 * count,), scalars, ins, [own] * pairs + [other] * pairs,
        flops=10**10,
    )


def cross_back(scalars, g, gains, p0, p1, cot, cross_w, q, k, v, weights, m):
    def kernel(
        at, g_ref, gain_ref, p0_ref, p1_ref, cot_ref, q_ref, k_ref, v_ref, p_ref, m_ref, *refs
    ):
        dg_ref, dq_ref, dk_ref, dv_ref, de_ref, gain_out, dm_ref, w, sem = refs[8:]
        copies = weight_copies(at, 2, refs[:8], w, sem)
        dn5 = p0_ref[...].astype(f32) + p1_ref[...].astype(f32)
        dg_rows, gain4 = norm_back(g_ref[...].astype(f32), gain_ref[4:5], dn5)
        dg = (dg_rows + cot_ref[...].astype(f32)).astype(bf16)
        dg_ref[...] = dg
        for one in copies:
            one.wait()
        dc = dot_nt(dg, w[3]).astype(bf16)
        dq, dk, dv = small_attend_back(CROSS_KEYS, q_ref[...], k_ref[...], v_ref[...], dc, p_ref)
        dq_ref[...], dk_ref[...], dv_ref[...] = dq, dk, dv
        de_ref[...] = (dot_nt(dk, w[1]) + dot_nt(dv, w[2])).astype(bf16)
        dm_rows, gain3 = norm_back(m_ref[...], gain_ref[3:4], dot_nt(dq, w[0]))
        dm_ref[...] = dm_rows + dg.astype(f32)
        gain_out[...] = jnp.concatenate([gain3, gain4], axis=0)

    rows, small = whole(BUF, D), whole(DEC, D)
    big_low, low = (shape((BUF, D)), rows), (shape((DEC, D)), small)
    return call(
        kernel, (1,), scalars,
        [
            (g, small), (gains, whole(5, D)), (p0, small), (p1, small), (cot, small),
            (q, small), (k, rows), (v, rows), (weights, whole(GROUPS, BUF, 128)), (m, small),
        ]
        + weight_args(cross_w),
        [low, low, big_low, big_low, big_low, (shape((2, D), f32), whole(2, D)), (shape((DEC, D), f32), small)],
        WEIGHT_SCRATCH,
        2 * 10**10,
    )


def enc_feed_back(scalars, de, slope, feed_in, near_in, feed_out, near_out):
    count = feed_in.shape[1] // FTILE

    def kernel(at, de_ref, s_ref, fi, ni, fo, nf, du_ref, p_ref, total):
        step = pl.program_id(0)
        w_in = jnp.where(step < count, fi[0], ni[0])
        w_out = jnp.where(step < count, fo[0], nf[0])
        du = (s_ref[...].astype(f32) * dot_nt(de_ref[...], w_out)).astype(bf16)
        du_ref[...] = du
        grad = dot_nn(du, w_in)

        @pl.when(step == 0)
        def _():
            total[...] = grad

        @pl.when(step > 0)
        def _():
            total[...] += grad

        @pl.when(step == 2 * count - 1)
        def _():
            p_ref[...] = total[...].astype(bf16)

    own, near = feed_specs(0, count)
    tile = pl.BlockSpec((BUF, FTILE), lambda i, at: (0, i))
    return call(
        kernel, (2 * count,), scalars,
        [(de, whole(BUF, D)), (slope, tile), (feed_in, own), (near_in, near), (feed_out, own), (near_out, near)],
        [(shape(slope.shape), tile), (shape((BUF, D)), whole(BUF, D))],
        [pltpu.VMEM((BUF, D), f32)], 2 * 10**10,
    )


def chip_cols(at, ref):
    return ref[:, pl.ds(pl.multiple_of(at[ACROSS] * BIG, 128), BIG)]


def store_rows(at, grads, own_ref, other_ref):
    first = at[CORE] == 0
    for i, grad in enumerate(grads):
        low = grad.astype(bf16)
        half = low.shape[0] // 2
        own_ref[i] = jnp.where(first, low[:half], low[half:])
        other_ref[i] = jnp.where(first, low[half:], low[:half])


def quarter_outs(mats):
    kind = (shape((mats, BIG // 2, D)), whole(mats, BIG // 2, D))
    return [kind, kind]


def cross_weights(scalars, n4, dq, e, dk, dv, c, dg):
    def kernel(at, n4_ref, dq_ref, e_ref, dk_ref, dv_ref, c_ref, dg_ref, own_ref, other_ref):
        n4_t, e_t, c_t = (transposed(chip_cols(at, ref)) for ref in (n4_ref, e_ref, c_ref))
        pairs = ((n4_t, dq_ref), (e_t, dk_ref), (e_t, dv_ref), (c_t, dg_ref))
        store_rows(at, [dot_nn(left, right[...]) for left, right in pairs], own_ref, other_ref)

    rows, small = whole(BUF, D), whole(DEC, D)
    return call(
        kernel, (1,), scalars,
        [(n4, small), (dq, small), (e, rows), (dk, rows), (dv, rows), (c, small), (dg, small)],
        quarter_outs(4),
    )


def self_back(scalars, dm, gains, self_w, q, k, v, c, weights, xd, n3):
    def kernel(at, dm_ref, gain_ref, q_ref, k_ref, v_ref, c_ref, p_ref, xd_ref, n3_ref, *refs):
        own_ref, other_ref, grad_ref, gain_out, diag_ref, w, sem = refs[8:]
        copies = weight_copies(at, 1, refs[:8], w, sem)
        dm = dm_ref[...]
        low = dm.astype(bf16)
        for one in copies:
            one.wait()
        dc = dot_nt(low, w[3]).astype(bf16)
        dq, dk, dv = small_attend_back(SELF_KEYS, q_ref[...], k_ref[...], v_ref[...], dc, p_ref, diag_ref)
        dn3 = dot_nt(dq, w[0]) + dot_nt(dk, w[1]) + dot_nt(dv, w[2])
        dd, gain2 = norm_back(xd_ref[...].astype(f32), gain_ref[2:3], dn3)
        gain_out[...] = gain2
        grad = (dd + dm).astype(bf16)
        for i in range(QPB):
            grad_ref[pl.ds(pl.multiple_of(at[OWNER + i] * TGT, TGT), TGT)] = grad[i * TGT : (i + 1) * TGT]
        n3_t, c_t = transposed(chip_cols(at, n3_ref)), transposed(chip_cols(at, c_ref))
        store_rows(at, [dot_nn(n3_t, dq), dot_nn(n3_t, dk), dot_nn(n3_t, dv), dot_nn(c_t, low)], own_ref, other_ref)

    small = whole(DEC, D)
    return call(
        kernel, (1,), scalars,
        [
            (dm, small), (gains, whole(5, D)),
            (q, small), (k, small), (v, small), (c, small), (weights, whole(GROUPS, DEC, 128)), (xd, small), (n3, small),
        ]
        + weight_args(self_w),
        quarter_outs(4)
        + [
            (shape((DEC, D)), small), (shape((1, D), f32), whole(1, D)),
            (shape((GROUPS, TGT, 128), f32), whole(GROUPS, TGT, 128)),
        ],
        WEIGHT_SCRATCH, 10**9,
    )


def enc_back(scalars, opening, gains, xr, chunk, chunk_c, n1=None, start=None, carried=None):
    half = BIG // 2
    first = 0 if opening else 3

    def kernel(at, gain_ref, xr_ref, wo_ref, ca_ref, cb_ref, qkv_ref, c_ref, big_ref, rest_ref, w_ref, *refs):
        if opening:
            h1_ref, p0_ref, p1_ref, de_ref, n1_ref = refs[:5]
            own_ref, other_ref, diag_ref, rdiag_ref, dh1_ref, dn1_ref, n1_t, c_t, gain_out = refs[5:]
        else:
            dh1_ref, dn1_in, n1_t, c_t = refs[:4]
            own_ref, other_ref, diag_ref, rdiag_ref, grad_ref, gain_out, dn1_ref, twice = refs[6:]
        p = pl.program_id(0)

        @pl.when(p == 0)
        def _():
            if opening:
                dn2 = p0_ref[...].astype(f32) + p1_ref[...].astype(f32)
                dh1_rows, gain1 = norm_back(h1_ref[...].astype(f32), gain_ref[1:2], dn2)
                dh1_ref[...] = (dh1_rows + de_ref[...].astype(f32)).astype(bf16)
                gain_out[...] = gain1
                n1_t[...] = chip_cols(at, n1_ref).T
                c_t[...] = jnp.where(at[ACROSS] == 0, ca_ref[...], cb_ref[...]).T
                dn1_ref[...] = jnp.zeros_like(dn1_ref)
            else:
                dn1_ref[...] = dn1_in[...]

        qkv, c, w = qkv_ref[0], c_ref[...], w_ref[0]
        q, k, v = qkv[:, :128], qkv[:, 128:256], qkv[:, 256:]
        dh1 = dh1_ref[...]
        grads = dot_nt(dh1, wo_ref[...]).astype(bf16)
        keys_t = k.T
        product_t = (grads.astype(f32) * c.astype(f32)).T
        dq_t = []
        dk_big = dv_big = dk_rest = dv_rest = 0.0
        for hh in range(2):
            row_sum = jnp.sum(product_t[hh * HD : (hh + 1) * HD], axis=0, keepdims=True)
            queries, values, grads_h = lane_half(q, hh), lane_half(v, hh), lane_half(grads, hh)
            head_k = keys_t[hh * HD : (hh + 1) * HD]
            weights = big_ref[hh]
            ds = score_grad(weights, dot_nt(values[:BIG], grads[:BIG]), row_sum[:, :BIG])
            dv_big = dv_big + dot_nn(weights, grads_h[:BIG])
            dk_big = dk_big + dot_nn(ds, queries[:BIG])
            diag_ref[hh] = jnp.concatenate(
                [diagonals(ds[128 * b : 128 * (b + 1)], WIDE) for b in range(3)], axis=0
            )
            dq_head = dot_nn(head_k[:, :BIG], ds)
            weights = rest_ref[hh]
            ds = score_grad(weights, dot_nt(values[BIG:], grads[BIG:]), row_sum[:, BIG:])
            dv_rest = dv_rest + dot_nn(weights, grads_h[BIG:])
            dk_rest = dk_rest + dot_nn(ds, queries[BIG:])
            rdiag_ref[hh] = diagonals(ds, 2 * REST)
            dq_t.append(jnp.concatenate([dq_head, dot_nn(head_k[:, BIG:], ds)], axis=1))
        dq = jnp.concatenate(dq_t, axis=0).T.astype(bf16)
        dk = jnp.concatenate([dk_big, dk_rest], axis=0).astype(bf16)
        dv = jnp.concatenate([dv_big, dv_rest], axis=0).astype(bf16)
        dqkv = jnp.concatenate([dq, dk, dv], axis=1)
        dn1_ref[...] += dot_nt(dqkv, w)
        grad = dot_nn(n1_t[...], dqkv)
        columns = pl.ds(pl.multiple_of(128 * (first + p), 128), 128)
        out_grad = dot_nn(c_t[...], dh1_ref[:, columns])
        store_rows(at, [grad[:, 128 * i : 128 * i + 128] for i in range(3)] + [out_grad], own_ref, other_ref)

        if not opening:

            @pl.when(p == 2)
            def _():
                rows, gain0 = norm_back(xr_ref[...].astype(f32), gain_ref[0:1], dn1_ref[...])
                gain_out[...] = gain0
                low = (rows + dh1.astype(f32)).astype(bf16)
                twice[:BUF] = low
                twice[BUF:] = low
                grad_ref[...] = twice[pl.ds(pl.multiple_of(BUF - at[START], SMALL), BUF)]

    rows = whole(BUF, D)
    wo = start[4] if opening else carried[-1]
    qkv, c, big, rest, w = chunk
    ins = [
        (gains, whole(5, D)), (xr, rows), (wo, pl.BlockSpec((128, D), lambda p, at: (first + p, 0))),
        (chunk_c[0], whole(BUF, BIG)), (chunk_c[1], whole(BUF, BIG)),
        (qkv, pl.BlockSpec((1, BUF, BIG), lambda p, at: (p, 0, 0))),
        (c, pl.BlockSpec((BUF, 128), lambda p, at: (0, p))),
        (big, pl.BlockSpec((2, BIG, BIG), lambda p, at: (p, 0, 0))),
        (rest, pl.BlockSpec((2, REST, REST), lambda p, at: (p, 0, 0))),
        (w, pl.BlockSpec((1, D, BIG), lambda p, at: (p, 0, 0))),
    ]
    columns = (shape((4, half, D)), pl.BlockSpec((4, half, 128), lambda p, at: (0, 0, first + p)))
    outs = [
        columns, columns,
        (shape((6, 3, WIDE), f32), pl.BlockSpec((2, 3, WIDE), lambda p, at: (p, 0, 0))),
        (shape((6, 1, 2 * REST), f32), pl.BlockSpec((2, 1, 2 * REST), lambda p, at: (p, 0, 0))),
    ]
    low, turned = (shape((BUF, D)), rows), (shape((BIG, BUF)), whole(BIG, BUF))
    one = (shape((1, D), f32), whole(1, D))
    scratch, aliases = (), {}
    if opening:
        ins += [(value, rows) for value in start[:4]] + [(n1, rows)]
        outs += [low, (shape((BUF, D), f32), rows), turned, turned, one]
    else:
        own, other, dh1, dn1, n1_t, c_t, _ = carried
        ins += [(dh1, rows), (dn1, rows), (n1_t, whole(BIG, BUF)), (c_t, whole(BIG, BUF)), (own, ANYWHERE), (other, ANYWHERE)]
        aliases = {len(ins) - 1: 0, len(ins): 1}
        outs += [low, one]
        scratch = [pltpu.VMEM((BUF, D), f32), pltpu.VMEM((2 * BUF, D), bf16)]
    return call(kernel, (3,), scalars, ins, outs, scratch, 2 * 10**10, aliases)


def swap_section(value, bit):
    count = lax.axis_size("section")
    return lax.ppermute(value, "section", [(i, i ^ bit) for i in range(count)])


def swap_dp(value, bit):
    count = lax.axis_size("dp")
    return lax.ppermute(value, "dp", [(i, i ^ bit) for i in range(count)])


def add_low(a, b):
    return (a.astype(f32) + b.astype(f32)).astype(bf16)


def tie(value, *deps):
    return lax.optimization_barrier((value,) + deps)[0] if deps else value


def halves(own, got, extra=None):
    half = own.shape[0] // 2
    mine = lax.axis_index("dp") % 2

    def part(which):
        rows = [lax.dynamic_slice_in_dim(value, which * half, half, 0) for value in (own, got)]
        total = add_low(*rows)
        return total if extra is None else jnp.concatenate([total, extra])

    return part(mine), part(1 - mine)


def rejoin(keep, other):
    mine = lax.axis_index("dp") % 2
    keep = keep[: other.shape[0]]
    return jnp.where(mine == 0, jnp.concatenate([keep, other]), jnp.concatenate([other, keep]))


Y_TIME, TREE_TIME, STEP = 12.7, 12.7, 3.0
STAGES = (("y", Y_TIME), ("in", TREE_TIME), ("mid", TREE_TIME), ("out", TREE_TIME), ("y", Y_TIME))
ROUTES = {
    "y": tuple((i, i ^ 1) for i in range(8)),
    "in": ((0, 2), (1, 3), (6, 4), (7, 5)),
    "mid": ((2, 4), (3, 5), (4, 2), (5, 3)),
    "out": ((2, 0), (3, 1), (4, 6), (5, 7)),
}


class GradSum:
    def __init__(self, pieces):
        self.count = lax.axis_size("dp")
        self.value = {}
        self.extra = None
        self.stage = {i: 0 for i in pieces}
        self.links = {name: [] for name in ROUTES}
        self.sent, self.got = {}, {}

    def enter(self, i, own, got, extra=None):
        own, got = own.reshape(-1, D), got.reshape(-1, D)
        if self.count != 8:
            self.value[i] = lax.psum(add_low(own, got), "dp")
            self.extra = None if extra is None else lax.psum(extra, "dp")
        else:
            self.value[i] = (own, got, extra)

    def step(self, i, *after):
        now = self.stage[i]
        self.stage[i] = now + 1
        if self.count != 8:
            return
        link = STAGES[now][0]
        value = self.value[i]
        if now > 0:
            value = tie(value, *after)
        if now == 0:
            value, sent = halves(*(tie(value[0], *after), tie(value[1], *after), value[2]))
        elif now == 4:
            sent = value[: value.shape[0] // 128 * 128]
            if sent.shape != value.shape:
                self.extra = value[sent.shape[0] :]
        else:
            sent = value
        before = self.links[link]
        sent = tie(sent, *before[-2:-1])
        got = lax.ppermute(sent, "dp", ROUTES[link])
        before.append(got)
        z = lax.axis_index("dp") // 2
        if now < 3:
            value = add_low(value, got)
        elif now == 3:
            value = jnp.where((z == 0) | (z == 3), got, value)
        else:
            value = rejoin(value, got)
        self.value[i], self.sent[i, now], self.got[i, now] = value, sent, got

    def between(self, after, ended, begun):
        for i in begun:
            self.step(i, after)
        if self.count != 8:
            return []
        return [self.got[key] for key in ended] + [self.sent[i, self.stage[i] - 1] for i in begun]

    def finish(self, late):
        free = {name: 0.0 for name in ROUTES}
        at = {i: late.get(i, 0.0) for i in self.stage}
        while min(self.stage.values()) < len(STAGES):
            choices = [(max(at[i], free[STAGES[now][0]]), now, i) for i, now in self.stage.items() if now < len(STAGES)]
            soon = min(choices)[0] + 6.0
            begin, _, i = min((c for c in choices if c[0] <= soon), key=lambda c: (c[1], c[0]))
            link, length = STAGES[self.stage[i]]
            free[link], at[i] = begin + length + 0.5, begin + length + STEP
            self.step(i)
        return self.value


def shards(
    encoder_in, decoder_in, lengths, query_map, attn_query, attn_keyval, attn_output,
    feed_in, feed_out, norm_gains, position_bias, cotangent,
):
    section_id = lax.axis_index("section")
    across = section_id // 2
    core = section_id % 2
    quarter = attn_query.shape[1]
    half = 2 * quarter

    dp_id = lax.axis_index("dp")
    own = (attn_query, attn_keyval, attn_output)
    near = tuple(swap_section(a, 1) for a in own)
    hidden = feed_in.shape[1]

    def packed(index, mats, first, last, *after):
        parts = [tie(attn_query[index : index + 1], *after), attn_keyval[2 * index : 2 * index + 2], attn_output[index : index + 1]]
        return jnp.concatenate(parts[: mats - 1], axis=0)[:, :, first:last]

    bases = [(section_id ^ k) * quarter for k in range(4)]
    def piece_of(index, count, *after):
        size = quarter // count
        piece = lax.dynamic_slice_in_dim(packed(index, 4, 0, D), (dp_id % count) * size, size, 1)
        return swap_section(tie(piece, *after), 2)

    def places(count):
        at = dp_id % count
        return [(at ^ k) * (quarter // count) if k < count else 0 for k in range(4)]

    pack_a = packed(0, 3, 0, D // 2)
    got_a = swap_section(pack_a, 2)

    big = jnp.argmax(lengths[core]).astype(jnp.int32)
    owners = lax.dynamic_slice_in_dim(jnp.concatenate([query_map[core]] * 2), big, QPB, 0)
    scalars = jnp.concatenate(
        [jnp.stack([core, across, big * SMALL]), owners, jnp.stack(bases + places(4) + places(2))]
    ).astype(jnp.int32)

    enc_table = spread_table(position_bias[0], encoder_bucket(enc_offsets()))
    causal = jnp.asarray(dec_offsets() <= 0)
    dec_table = jnp.where(causal, spread_table(position_bias[1], decoder_bucket(dec_offsets())), masked_score)
    dec_table = jnp.transpose(dec_table.reshape(GROUPS, GROUP, TGT, TGT), (0, 2, 1, 3)).reshape(GROUPS, TGT, GROUP * TGT)
    sums = GradSum(range(7))

    near_a = swap_section(tie(got_a, scalars, enc_table, dec_table), 1)
    got_b = swap_section(packed(0, 3, D // 2, D, pack_a), 2)
    got_self = piece_of(1, 4, near_a)
    first = enc_attention(scalars, encoder_in, norm_gains, enc_table, own, near, got_a, near_a, 0)
    n1, xr = first[5:]
    got_o = swap_section(tie(attn_output[0], near_a), 2)
    near_b = swap_section(tie(got_b, n1), 1)
    got_cross = piece_of(2, 2, n1)
    piece = tie(got_self, n1)
    second_piece, third_piece = swap_dp(piece, 1), swap_dp(piece, 2)
    near_in = swap_section(tie(feed_in, near_a), 1)
    near_out = swap_section(tie(feed_out, near_a), 1)
    second = enc_attention(scalars, n1, norm_gains, enc_table, own, near, got_b, near_b, 1)
    near_got_o = swap_section(tie(got_o, second[1]), 1)
    fourth_piece = swap_dp(tie(second_piece, second[1]), 2)
    quad = jnp.stack([piece, second_piece, third_piece, fourth_piece])
    h1, n2, a1, slope1, part, wo = enc_feed(
        scalars, xr, first[1], second[1], attn_output, near[2], got_o, near_got_o, norm_gains,
        feed_in, near_in, feed_out, near_out,
    )
    part_other = swap_section(part, 2)
    quad = tie(quad, part)
    self_w = own + near + (quad, swap_section(quad, 1))
    pair = tie(got_cross, second[1])
    pair = tie(jnp.stack([pair, swap_dp(pair, 1)]), part)
    cross_w = own + near + (pair, swap_section(pair, 1))
    xd, n3, q2, k2, v2, c2, p2, m, n4 = dec_self(scalars, decoder_in, norm_gains, dec_table, self_w)
    e, q3, k3, v3, c3, p3, g, n5, cot, a2, du2, dn5, out_part = dec_cross(
        scalars, h1, part, part_other, m, n4, cross_w, norm_gains, cotangent, feed_in, near_in, feed_out, near_out
    )

    dn5_other = swap_section(dn5, 2)
    own_out, own_in, other_out, other_in = feed_weights(scalars, (a2, du2), (cot, n5), hidden)
    sums.enter(0, own_out, swap_section(other_out, 1))
    sums.enter(1, own_in, swap_section(other_in, 1))

    dn5_other = tie(dn5_other, *sums.between(own_in, (), (0,)))
    dg, dq3, dk3, dv3, de, gains34, dm = cross_back(
        scalars, g, norm_gains, dn5, dn5_other, cot, cross_w, q3, k3, v3, p3, m
    )
    de = tie(de, *sums.between(dq3, (), (1,)))
    du1, dn2 = enc_feed_back(scalars, de, slope1, feed_in, near_in, feed_out, near_out)
    dn2_other = swap_section(dn2, 2)
    own_w, other_w = cross_weights(scalars, n4, dq3, e, dk3, dv3, c3, tie(dg, dn2))
    sums.enter(2, own_w, swap_section(other_w, 1))

    dm = tie(dm, own_w, *sums.between(own_w, (), (0,)))
    own_w, other_w, dec_grad, gain2, diag2 = self_back(scalars, dm, norm_gains, self_w, q2, k2, v2, c2, p2, xd, n3)
    sums.enter(5, own_w, swap_section(other_w, 1))

    n2_late = tie(n2, own_w, dn2_other, *sums.between(dec_grad, (), (1, 2)))
    own_out, own_in, other_out, other_in = feed_weights(scalars, (a1, du1), (de, n2_late), hidden)
    sums.enter(3, own_out, swap_section(other_out, 1))
    sums.enter(4, own_in, swap_section(other_in, 1))

    dn2_late = tie(dn2_other, own_in, *sums.between(own_in, (), (5, 0)))
    contexts = (first[1], second[1])
    own_w, other_w, diag_a, rdiag_a, dh1, dn1, n1_t, c_t, gain1 = enc_back(
        scalars, True, norm_gains, xr, first[:5], contexts, n1, (h1, dn2, dn2_late, de, wo)
    )
    dn1 = tie(dn1, *sums.between(dh1, (), (3, 1)))
    own_enc, other_w, diag_b, rdiag_b, enc_grad, gain0 = enc_back(
        scalars, False, norm_gains, xr, second[:5], contexts, carried=(own_w, other_w, dh1, dn1, n1_t, c_t, wo)
    )
    got_w = swap_section(other_w, 1)

    hot_enc = jnp.asarray(
        np.concatenate(
            [one_hot(encoder_bucket(128 * b + diagonal_offsets(128, WIDE))) for b in range(3)]
            + [one_hot(encoder_bucket(diagonal_offsets(REST, 2 * REST)))]
        )
    )
    hot_dec = jnp.asarray(one_hot(decoder_bucket(dec_offsets())))
    sums_enc = jnp.concatenate(
        [
            jnp.concatenate([d.reshape(HEADS // 2, -1), r.reshape(HEADS // 2, -1)], axis=1)
            for d, r in ((diag_a, rdiag_a), (diag_b, rdiag_b))
        ]
    )
    exact = lax.Precision.HIGHEST
    table_enc = jnp.einsum("mb,hm->bh", hot_enc, sums_enc, precision=exact)
    diag2 = diag2.reshape(GROUPS, TGT, GROUP, TGT)
    table_dec = jnp.einsum("kqb,gkhq->bgh", hot_dec, diag2, precision=exact).reshape(NB, HEADS)
    tables = jnp.stack([table_enc, table_dec]).reshape(-1, D)
    small = jnp.concatenate([gain0, gain1, gain2, gains34, tables, jnp.zeros((10, D), f32)])
    small = small + swap_section(small, 1)
    sums.enter(6, own_enc, got_w, small.astype(bf16))
    total = sums.finish({0: 0.0, 2: 0.0, 5: 4.0, 3: 14.0, 4: 4.0, 6: 10.0})
    unit_out2, unit_in2, unit_cross, unit_out1, unit_in1, unit_self, unit_enc = (total[i] for i in range(7))
    small = sums.extra.astype(f32)
    gains = small[:5]
    tables = small[5].reshape(2, NB, HEADS)

    def split_rows(rows, count):
        mine = lax.dynamic_slice_in_dim(rows, section_id * count, count, 0)
        theirs = swap_section(lax.dynamic_slice_in_dim(rows, (section_id ^ 1) * count, count, 0), 1)
        return jnp.where(core == 0, jnp.stack([mine, theirs]), jnp.stack([theirs, mine]))

    out_rows = (g.astype(f32) + (out_part.astype(f32) + swap_section(out_part, 2).astype(f32))).astype(bf16)
    restored = jnp.zeros((DEC, D), bf16)
    for i in range(QPB):
        restored = lax.dynamic_update_slice_in_dim(restored, out_rows[i * TGT : (i + 1) * TGT], owners[i] * TGT, 0)
    sections = lax.axis_size("section")
    decoder_out = split_rows(restored, DEC // sections)
    decoder_in_grad = split_rows(dec_grad, DEC // sections)
    encoder_in_grad = split_rows(enc_grad, BUF // sections)

    u_enc, u_self, u_cross = (
        u.reshape(4, quarter, D).astype(f32) for u in (unit_enc, unit_self, unit_cross)
    )
    def placed(count, parts, rows=quarter):
        whole_grad = jnp.zeros((count, rows, D), f32)
        for at, part in parts:
            whole_grad = lax.dynamic_update_slice_in_dim(whole_grad, part.astype(f32), at, 0)
        return whole_grad

    query_grad = placed(3, ((2, u_cross[0:1]), (1, u_self[0:1]), (0, u_enc[0:1])))
    keyval_grad = placed(6, ((4, u_cross[1:3]), (2, u_self[1:3]), (0, u_enc[1:3])))
    output_grad = placed(3, ((2, u_cross[3:4]), (1, u_self[3:4]), (0, u_enc[3:4])))
    feed_in_grad = placed(2, ((1, unit_in2[None]), (0, unit_in1[None])), hidden)
    feed_out_grad = placed(2, ((1, unit_out2[None]), (0, unit_out1[None])), hidden)
    return (
        decoder_out, encoder_in_grad, decoder_in_grad, query_grad, keyval_grad, output_grad,
        feed_in_grad, feed_out_grad, gains, tables,
    )


def solution(mesh):
    rows = P("dp", None, None)
    mats = P(None, "section", None)
    outs = P("dp", "section", None)
    return jax.shard_map(
        shards,
        mesh=mesh,
        in_specs=(rows, rows, P("dp", None), P("dp", None), mats, mats, mats, mats, mats, P(), P(), rows),
        out_specs=(outs, outs, outs, mats, mats, mats, mats, mats, P(), P()),
        check_vma=False,
    )
```
